32 devices in a mesh: grp: 8 (over z, x), psg: 4 (over y, core).
Axes of the slice: x: 2, y: 2, z: 4, core: 2. Of those that a mesh axis runs over, the one named last changes fastest.
Arguments:
- query_ids: int32 [256, 32], P(('grp', 'psg')), may hold values from 0 to 30719
- passage_ids: int32 [32, 1024], P(('grp', 'psg')), may hold values from 0 to 30719
- passage_lengths: int32 [32, 32], P(('grp', 'psg')), may hold values from 1 to 64, 1024 in all within a row
- positives: int32 [256], P(('grp', 'psg')), may hold values from 0 to 127
- negatives: int32 [256, 8], P(('grp', 'psg')), may hold values from 0 to 127
- pair_mask: int32 [256, 8], P(('grp', 'psg')), may hold values 0 or 1
- assignments: int32 [32, 1024], P(('grp', 'psg')), may hold values from 0 to 1023
- step_count: int32 [1], replicated, may hold values from 1 to 20
- embed_table: float32 [30720, 768], P(('grp', 'psg')), may hold values from -1.75 to 1.75
- embed_table_moment: float32 [30720, 768], P(('grp', 'psg')), may hold values from -6.1035156e-05 to 6.1035156e-05
- embed_table_second: float32 [30720, 768], P(('grp', 'psg')), may hold values from 1.0625e-11 to 4.25e-11
- attention_weight: float32 [768, 3072], P(None, ('grp', 'psg')), may hold values from -0.21875 to 0.21875
- attention_weight_moment: float32 [768, 3072], P(None, ('grp', 'psg')), may hold values from -0.0017089844 to 0.0017089844
- attention_weight_second: float32 [768, 3072], P(None, ('grp', 'psg')), may hold values from 6.875e-09 to 2.75e-08
- up_weight: float32 [768, 3072], P(None, ('grp', 'psg')), may hold values from -0.21875 to 0.21875
- up_weight_moment: float32 [768, 3072], P(None, ('grp', 'psg')), may hold values from -0.0007324219 to 0.0007324219
- up_weight_second: float32 [768, 3072], P(None, ('grp', 'psg')), may hold values from 1.4375e-09 to 5.75e-09
- down_weight: float32 [3072, 768], P(('grp', 'psg')), may hold values from -0.109375 to 0.109375
- down_weight_moment: float32 [3072, 768], P(('grp', 'psg')), may hold values from -0.0017089844 to 0.0017089844
- down_weight_second: float32 [3072, 768], P(('grp', 'psg')), may hold values from 7.5e-09 to 2.875e-08
- head_weight: float32 [768, 128], P(('grp', 'psg')), may hold values from -0.21875 to 0.21875
- head_weight_moment: float32 [768, 128], P(('grp', 'psg')), may hold values from -0.0048828125 to 0.0048828125
- head_weight_second: float32 [768, 128], P(('grp', 'psg')), may hold values from 6.25e-08 to 2.5e-07
- small_params: float32 [59904], P(('grp', 'psg')), may hold values from -1.75 to 1.75
- small_params_moment: float32 [59904], P(('grp', 'psg')), may hold values from -0.0024414062 to 0.0024414062
- small_params_second: float32 [59904], P(('grp', 'psg')), may hold values from 1.5625e-08 to 6.25e-08
Outputs:
- loss: float32 [], replicated
- centroid_sums: float32 [1024, 128], P(('grp', 'psg'))
- centroid_counts: float32 [1024], P(('grp', 'psg'))
- embed_table_new: float32 [30720, 768], P(('grp', 'psg'))
- embed_table_grad: float32 [30720, 768], P(('grp', 'psg'))
- embed_table_second_new: float32 [30720, 768], P(('grp', 'psg'))
- attention_weight_new: float32 [768, 3072], P(None, ('grp', 'psg'))
- attention_weight_grad: float32 [768, 3072], P(None, ('grp', 'psg'))
- attention_weight_second_new: float32 [768, 3072], P(None, ('grp', 'psg'))
- up_weight_new: float32 [768, 3072], P(None, ('grp', 'psg'))
- up_weight_grad: float32 [768, 3072], P(None, ('grp', 'psg'))
- up_weight_second_new: float32 [768, 3072], P(None, ('grp', 'psg'))
- down_weight_new: float32 [3072, 768], P(('grp', 'psg'))
- down_weight_grad: float32 [3072, 768], P(('grp', 'psg'))
- down_weight_second_new: float32 [3072, 768], P(('grp', 'psg'))
- head_weight_new: float32 [768, 128], P(('grp', 'psg'))
- head_weight_grad: float32 [768, 128], P(('grp', 'psg'))
- head_weight_second_new: float32 [768, 128], P(('grp', 'psg'))
- small_params_new: float32 [59904], P(('grp', 'psg'))
- small_params_grad: float32 [59904], P(('grp', 'psg'))
- small_params_second_new: float32 [59904], P(('grp', 'psg'))
The draws below stay inside these ranges and needn't reach their ends.
Inputs may be any that keep to these rules, and one draw needn't show every extreme that they name: `passage_lengths`: each row's 32 lengths add up to 1024; the longest in every row is exactly 64.
All inputs are finite; a program needn't handle non-finite values. No bound on the sum of `pair_mask` on one device may be relied on, other than what follows from the above.
Results may differ from the reference program's by a relative error of at most 0.011.
Values may be sent and summed in bfloat16 or wider, within the bound.
A program may use at most 384 MiB of HBM per device.

```python
import math
import jax
import jax.numpy as jnp
import numpy as np
from jax import lax

D = 768
HEADS = 12
HD = 64
FF = 3072
V = 30720
DC = 128
SEG = 32
PMAX = 64
ROW = 1024
PPD = 32
QDEV = 8
NEG = 8
NCENT = 1024
PGRP = 128
QUERIES = 256
PROWS = 32
VEC = 59904
N_GRP = 8
N_PSG = 4
DEVICES = 32


def plant(array, own_key, least, top_value):
    longest = array.shape.index(max(array.shape))
    spots = []
    for shift in (0, 1):
        where = [jax.random.randint(jax.random.fold_in(own_key, axis), (), 0, length) for axis, length in enumerate(array.shape)]
        where[longest] = (where[longest] + shift) % array.shape[longest]
        spots.append(tuple(where))
    return array.at[spots[0]].set(least).at[spots[1]].set(top_value)


def level_of(key, dims, cuts, smallest, largest):
    gain, own = 1.0, jax.random.fold_in(key, 6)
    for dim, parts in cuts:
        steps = jnp.exp(jax.random.uniform(jax.random.fold_in(own, dim), (parts,), jnp.float32, smallest / len(cuts), largest / len(cuts)))
        gain = gain * jnp.repeat(steps, dims[dim] // parts).reshape([-1 if axis == dim else 1 for axis in range(len(dims))])
    return gain


def rank_bounds(amount, lean):
    loads = [(1 << 20) // math.isqrt(rank ** lean) + 1 for rank in range(1, amount + 1)]
    deviation = 1 + sum(loads) // (1 << 30)
    return np.cumsum(np.array([max(1, weight // deviation) for weight in loads]))


def skewed_ids(stream_key, shape, number_of, lean):
    grid = rank_bounds(number_of, lean)
    pick = jax.random.randint(jax.random.fold_in(stream_key, 1), shape, 0, int(grid[number_of - 1]))
    grade = jnp.searchsorted(jnp.asarray(grid, jnp.int32), pick, side="right")
    return jax.random.permutation(jax.random.fold_in(stream_key, 2), number_of)[grade].astype(jnp.int32)


def length_profile(amount, total, most, skew):
    weights = [(1 << 20) // math.isqrt(grade ** skew) + 1 for grade in range(2, amount + 1)]
    surplus, holding = total - most - (amount - 1), [1] * (amount - 1)
    while surplus > 0:
        free = [i for i in range(amount - 1) if holding[i] < most]
        mass, budget = sum([weights[i] for i in free]), surplus
        for i in free:
            extra = min(most - holding[i], max(1, budget * weights[i] // mass), surplus)
            holding[i] = holding[i] + extra
            surplus = surplus - extra
    return np.array([most] + holding)


def ragged(key, count, total, bound, skew):
    if count == 2:
        one = jax.random.randint(key, (), max(1, total - bound), min(bound, total - 1) + 1)
        return jnp.stack([one, total - one])
    sizes = jnp.asarray(length_profile(count, total, bound, skew), jnp.int32)
    couples = (count - 1) // 2
    source_of, sink = sizes[1:1 + 2 * couples:2], sizes[2:2 + 2 * couples:2]
    room = jnp.minimum(source_of - 1, bound - sink)
    passed = jax.random.randint(jax.random.fold_in(key, 1), (couples,), 0, 1 << 20) % (room + 1)
    sizes = sizes.at[1:1 + 2 * couples:2].set(source_of - passed).at[2:2 + 2 * couples:2].set(sink + passed)
    return sizes[jax.random.permutation(jax.random.fold_in(key, 2), count)]


def bell_draw(rng, shape, spread, most, cuts=(), held_as=jnp.bfloat16):
    values = spread * jax.random.normal(rng, shape, jnp.float32)
    if cuts:
        values = values * level_of(rng, shape, cuts, -0.22, 0.18)
    return jnp.clip(values, -most, most).astype(held_as)


def setup_inputs(seed: int = 0) -> dict:
    keys = jax.random.split(jax.random.key(seed), 27)
    query_ids = plant(skewed_ids(keys[0], (QUERIES, SEG), V, 2), jax.random.fold_in(keys[0], 3), 0, V - 1).astype(jnp.int32)
    passage_ids = plant(skewed_ids(keys[1], (PROWS, ROW), V, 2), jax.random.fold_in(keys[1], 3), 0, V - 1).astype(jnp.int32)
    passage_lengths = jax.vmap(lambda own: ragged(own, PPD, ROW, PMAX, 2))(jax.random.split(keys[2], PROWS)).reshape((PROWS, PPD)).astype(jnp.int32)
    positives = plant(jax.random.randint(keys[3], (QUERIES,), 0, PGRP), jax.random.fold_in(keys[3], 1), 0, PGRP - 1).astype(jnp.int32)
    negatives = plant(jax.random.randint(keys[4], (QUERIES, NEG), 0, PGRP), jax.random.fold_in(keys[4], 1), 0, PGRP - 1).astype(jnp.int32)
    pair_mask = plant((jax.random.randint(keys[5], (QUERIES, NEG), 0, 2) < 1).astype(jnp.int32), jax.random.fold_in(keys[5], 1), 0, 1)
    assignments = plant(jax.random.randint(keys[6], (PROWS, ROW), 0, NCENT), jax.random.fold_in(keys[6], 1), 0, NCENT - 1).astype(jnp.int32)
    step_count = jax.random.randint(keys[7], (1,), 1, 21).astype(jnp.int32)
    embed_table = bell_draw(keys[8], (V, D), 0.3, 1.75, ((0, 32),), jnp.float32)
    embed_table_moment = bell_draw(keys[9], (V, D), (0.000014 * (DEVICES * (QDEV * SEG + ROW)) ** 0.5 / (QDEV * DEVICES)), 6.103515625e-05, ((0, 32),), jnp.float32)
    embed_table_second = jnp.clip(jnp.exp(math.log(4.2500000047018816e-11) - 1.3862944 * jax.random.uniform(keys[10], (V, D), jnp.float32) ** level_of(keys[10], (V, D), ((0, 32),), -0.2, 0.2)), 1.0625000011754704e-11, 4.2500000047018816e-11)
    attention_weight = bell_draw(keys[11], (D, 4 * D), D ** -0.5, 0.21875, ((1, 32),), jnp.float32)
    attention_weight_moment = bell_draw(keys[12], (D, 4 * D), (0.00036 * (DEVICES * (QDEV * SEG + ROW)) ** 0.5 / (QDEV * DEVICES)), 0.0017089844, ((1, 32),), jnp.float32)
    attention_weight_second = jnp.clip(jnp.exp(math.log(2.7500000499003363e-08) - 1.3862944 * jax.random.uniform(keys[13], (D, 4 * D), jnp.float32) ** level_of(keys[13], (D, 4 * D), ((1, 32),), -0.2, 0.2)), 6.875000124750841e-09, 2.7500000499003363e-08)
    up_weight = bell_draw(keys[14], (D, FF), D ** -0.5, 0.21875, ((1, 32),), jnp.float32)
    up_weight_moment = bell_draw(keys[15], (D, FF), (0.000165 * (DEVICES * (QDEV * SEG + ROW)) ** 0.5 / (QDEV * DEVICES)), 0.0007324219, ((1, 32),), jnp.float32)
    up_weight_second = jnp.clip(jnp.exp(math.log(5.750000031667923e-09) - 1.3862944 * jax.random.uniform(keys[16], (D, FF), jnp.float32) ** level_of(keys[16], (D, FF), ((1, 32),), -0.2, 0.2)), 1.4375000079169808e-09, 5.750000031667923e-09)
    down_weight = bell_draw(keys[17], (FF, D), FF ** -0.5, 0.109375, ((0, 32),), jnp.float32)
    down_weight_moment = bell_draw(keys[18], (FF, D), (0.00037 * (DEVICES * (QDEV * SEG + ROW)) ** 0.5 / (QDEV * DEVICES)), 0.0017089844, ((0, 32),), jnp.float32)
    down_weight_second = jnp.clip(jnp.exp(math.log(2.8749999714250407e-08) - 1.3437348 * jax.random.uniform(keys[19], (FF, D), jnp.float32) ** level_of(keys[19], (FF, D), ((0, 32),), -0.2, 0.2)), 7.499999732374363e-09, 2.8749999714250407e-08)
    head_weight = bell_draw(keys[20], (D, DC), D ** -0.5, 0.21875, ((0, 32),), jnp.float32)
    head_weight_moment = bell_draw(keys[21], (D, DC), (0.0011 * (DEVICES * (QDEV * SEG + ROW)) ** 0.5 / (QDEV * DEVICES)), 0.0048828125, ((0, 32),), jnp.float32)
    head_weight_second = jnp.clip(jnp.exp(math.log(2.499999993688107e-07) - 1.3862944 * jax.random.uniform(keys[22], (D, DC), jnp.float32) ** level_of(keys[22], (D, DC), ((0, 32),), -0.2, 0.2)), 6.249999984220267e-08, 2.499999993688107e-07)
    small_params = bell_draw(keys[23], (VEC,), 0.3, 1.75, ((0, 32),), jnp.float32)
    small_params_moment = bell_draw(keys[24], (VEC,), (0.00055 * (DEVICES * (QDEV * SEG + ROW)) ** 0.5 / (QDEV * DEVICES)), 0.0024414062, ((0, 32),), jnp.float32)
    small_params_second = jnp.clip(jnp.exp(math.log(6.249999984220267e-08) - 1.3862944 * jax.random.uniform(keys[25], (VEC,), jnp.float32) ** level_of(keys[25], (VEC,), ((0, 32),), -0.2, 0.2)), 1.5624999960550667e-08, 6.249999984220267e-08)
    return {"query_ids": query_ids, "passage_ids": passage_ids, "passage_lengths": passage_lengths, "positives": positives, "negatives": negatives, "pair_mask": pair_mask, "assignments": assignments, "step_count": step_count, "embed_table": embed_table, "embed_table_moment": embed_table_moment, "embed_table_second": embed_table_second, "attention_weight": attention_weight, "attention_weight_moment": attention_weight_moment, "attention_weight_second": attention_weight_second, "up_weight": up_weight, "up_weight_moment": up_weight_moment, "up_weight_second": up_weight_second, "down_weight": down_weight, "down_weight_moment": down_weight_moment, "down_weight_second": down_weight_second, "head_weight": head_weight, "head_weight_moment": head_weight_moment, "head_weight_second": head_weight_second, "small_params": small_params, "small_params_moment": small_params_moment, "small_params_second": small_params_second}


HIGHEST = lax.Precision.HIGHEST
TEMPER = 0.2
MARGIN = 1.0
NORM_EPS = 1e-06
BETA_ONE = 0.9
BETA_TWO = 0.999
ADAM_EPS = 1e-08
WEIGHT_DECAY = 0.01
RATE_MATRIX = 0.01
RATE_TABLE = 0.1

@jax.custom_vjp
def low(v):
    return lax.optimization_barrier(v.astype(jnp.bfloat16)).astype(jnp.float32)

@jax.custom_vjp
def low_back(v):
    return v

def low_keep(v):
    return (low(v), None)

def low_pass(kept, grad):
    return (grad,)

def back_keep(v):
    return (v, None)

def back_low(kept, grad):
    return (low(grad),)
low.defvjp(low_keep, low_pass)
low_back.defvjp(back_keep, back_low)

def layer_norm(values, scale_gain, shift_bias):
    average = lax.optimization_barrier(jnp.mean(values, axis=-1, keepdims=True))
    centered = values - average
    inverse = lax.rsqrt(lax.optimization_barrier(jnp.mean(centered * centered, axis=-1, keepdims=True)) + NORM_EPS)
    return centered * inverse * (1.0 + scale_gain) + shift_bias

def split_vector(vector):
    positions = vector[:PMAX * D].reshape(PMAX, D)
    remainder = vector[PMAX * D:]
    return (positions, [remainder[i * D:(i + 1) * D] for i in range(10)], remainder[10 * D:])

def encode(weights, token_ids, position, segment):
    embed_table, attention_weight, up_weight, down_weight, head_weight, small_params = weights
    positions, pieces, bias_up = split_vector(small_params)
    count_rows = token_ids.shape[0]
    hidden_zero = layer_norm(embed_table[token_ids] + positions[position], pieces[0], pieces[1])
    blank = jnp.zeros((D,), jnp.float32)
    mixed = jnp.dot(low(hidden_zero), attention_weight[:, :3 * D], precision=HIGHEST) + jnp.concatenate([pieces[2], blank, pieces[3]])
    triple = low(low_back(mixed)).reshape(count_rows, 3, HEADS, HD)
    raw = jnp.einsum('rhd,chd->hrc', triple[:, 0], triple[:, 1], precision=HIGHEST) * HD ** (-0.5)
    allowed = segment[:, None] == segment[None, :]
    scores = jnp.where(allowed[None], low_back(raw), -1000000000.0)
    probs = low(jax.nn.softmax(scores, axis=-1))
    context = low(low_back(jnp.einsum('hrc,chd->rhd', probs, triple[:, 2], precision=HIGHEST).reshape(count_rows, D)))
    hidden_one = layer_norm(hidden_zero + low_back(jnp.dot(context, attention_weight[:, 3 * D:], precision=HIGHEST)) + pieces[4], pieces[5], pieces[6])
    inner = low_back(jnp.dot(low(hidden_one), up_weight, precision=HIGHEST) + bias_up)
    activated = low(jax.nn.gelu(inner, approximate=False))
    hidden_two = layer_norm(hidden_one + low_back(jnp.dot(activated, down_weight, precision=HIGHEST)) + pieces[7], pieces[8], pieces[9])
    projected = low_back(jnp.dot(low(hidden_two), head_weight, precision=HIGHEST))
    unit = projected * lax.rsqrt(lax.optimization_barrier(jnp.sum(projected * projected, axis=-1, keepdims=True)) + NORM_EPS)
    return low(unit)

def passage_layout(lengths):
    starts = (jnp.cumsum(lengths, axis=-1) - lengths).astype(jnp.int32)
    place = jnp.arange(ROW, dtype=jnp.int32)
    above = (place[None, :, None] >= starts[:, None, :]).astype(jnp.int32)
    segment = (lax.optimization_barrier(jnp.sum(above, axis=-1)) - 1).astype(jnp.int32)
    chosen = (segment[:, :, None] == jnp.arange(PPD, dtype=jnp.int32)).astype(jnp.int32)
    position = (place[None, :] - lax.optimization_barrier(jnp.sum(chosen * starts[:, None, :], axis=-1))).astype(jnp.int32)
    return (segment, position)

def group_scores(query_group, passage_group, segment_group):
    sims = low_back(jnp.einsum('qid,rtd->qirt', query_group, passage_group, precision=HIGHEST))
    weighted = jnp.exp(sims / TEMPER)
    onehot = (segment_group[:, :, None] == jnp.arange(PPD, dtype=jnp.int32)).astype(jnp.float32)
    totals = jnp.einsum('qirt,rtp->qirp', weighted, onehot, precision=HIGHEST)
    return lax.optimization_barrier(jnp.sum(TEMPER * jnp.log(totals), axis=1)).reshape(query_group.shape[0], PGRP)

def adam_update(weight, moment, second, gradient, rate, count_steps):
    moment_new = BETA_ONE * moment + (1.0 - BETA_ONE) * gradient
    second_new = BETA_TWO * second + (1.0 - BETA_TWO) * gradient * gradient
    corrected = moment_new / (1.0 - BETA_ONE ** count_steps)
    scaled = second_new / (1.0 - BETA_TWO ** count_steps)
    weight_new = weight - rate * (corrected / (jnp.sqrt(scaled) + ADAM_EPS) + WEIGHT_DECAY * weight)
    return (weight_new, second_new)

def reference(query_ids, passage_ids, passage_lengths, positives, negatives, pair_mask, assignments, step_count, embed_table, embed_table_moment, embed_table_second, attention_weight, attention_weight_moment, attention_weight_second, up_weight, up_weight_moment, up_weight_second, down_weight, down_weight_moment, down_weight_second, head_weight, head_weight_moment, head_weight_second, small_params, small_params_moment, small_params_second):
    segment, position = passage_layout(passage_lengths)
    query_position = jnp.tile(jnp.arange(SEG, dtype=jnp.int32), QDEV)
    query_segment = jnp.repeat(jnp.arange(QDEV, dtype=jnp.int32), SEG)
    query_blocks = query_ids.reshape(N_GRP * N_PSG, QDEV * SEG)
    mask_float = pair_mask.astype(jnp.float32)

    def objective(table_in, attention_in, up_in, down_in, head_in, small_in):
        rounded = (low(table_in), low(attention_in), low(up_in), low(down_in), low(head_in), low(small_in))
        encode_saved = jax.checkpoint(encode)
        query_embed = lax.map(lambda block_ids: encode_saved(rounded, block_ids, query_position, query_segment), query_blocks)
        passage_embed = lax.map(lambda trio: encode_saved(rounded, trio[0], trio[1], trio[2]), (passage_ids, position, segment))
        query_group = query_embed.reshape(N_GRP, N_PSG * QDEV, SEG, DC)
        passage_group = passage_embed.reshape(N_GRP, N_PSG, ROW, DC)
        segment_group = segment.reshape(N_GRP, N_PSG, ROW)
        scores = lax.map(jax.checkpoint(lambda trio: group_scores(trio[0], trio[1], trio[2])), (query_group, passage_group, segment_group))
        scores = scores.reshape(N_GRP * N_PSG * QDEV, PGRP)
        pos_score = jnp.take_along_axis(scores, positives[:, None], axis=1)
        neg_score = jnp.take_along_axis(scores, negatives, axis=1)
        margins = MARGIN - pos_score + neg_score
        total_pairs = jnp.maximum(jnp.sum(mask_float), 1.0)
        return (jnp.sum(mask_float * jax.nn.softplus(margins)) / total_pairs, passage_embed)
    loss, pullback, passage_embed = jax.vjp(objective, embed_table, attention_weight, up_weight, down_weight, head_weight, small_params, has_aux=True)
    grads = pullback(jnp.ones_like(loss))
    flat_embed = passage_embed.reshape(-1, DC)
    which = assignments.reshape(-1)
    centroid_sums = jax.ops.segment_sum(flat_embed, which, num_segments=NCENT)
    centroid_counts = jax.ops.segment_sum(jnp.ones(which.shape, jnp.float32), which, num_segments=NCENT)
    count_steps = step_count[0].astype(jnp.float32)
    table_new, table_second_new = adam_update(embed_table, embed_table_moment, embed_table_second, grads[0], RATE_TABLE, count_steps)
    attn_new, attn_second_new = adam_update(attention_weight, attention_weight_moment, attention_weight_second, grads[1], RATE_MATRIX, count_steps)
    up_new, up_second_new = adam_update(up_weight, up_weight_moment, up_weight_second, grads[2], RATE_MATRIX, count_steps)
    down_new, down_second_new = adam_update(down_weight, down_weight_moment, down_weight_second, grads[3], RATE_MATRIX, count_steps)
    head_new, head_second_new = adam_update(head_weight, head_weight_moment, head_weight_second, grads[4], RATE_MATRIX, count_steps)
    small_new, small_second_new = adam_update(small_params, small_params_moment, small_params_second, grads[5], RATE_TABLE, count_steps)
    return (loss, centroid_sums, centroid_counts, table_new, grads[0], table_second_new, attn_new, grads[1], attn_second_new, up_new, grads[2], up_second_new, down_new, grads[3], down_second_new, head_new, grads[4], head_second_new, small_new, grads[5], small_second_new)
```

```python
import math

import jax
import jax.numpy as jnp
from jax import lax
from jax.experimental import pallas as pl
from jax.experimental.pallas import tpu as pltpu
from jax.sharding import PartitionSpec as P

D = 768
HEADS = 12
HD = 64
SEG = 32
PMAX = 64
ROW = 1024
PPD = 32
QDEV = 8
NCENT = 1024
DC = 128
BLK = 128
WIN = 256
ALL = ("grp", "psg")
BF = jnp.bfloat16
F32 = jnp.float32
MARK = 1e30


TEMPER = 0.2
MARGIN = 1.0
NORM_EPS = 1e-06
BETA_ONE = 0.9
BETA_TWO = 0.999
ADAM_EPS = 1e-08
WEIGHT_DECAY = 0.01
RATE_MATRIX = 0.01
RATE_TABLE = 0.1


def matmul(lhs_mat, rhs_mat):
    return jnp.dot(lhs_mat, rhs_mat, preferred_element_type=jnp.float32)


def contract_rows(lhs_mat, rhs_mat):
    return lax.dot_general(
        lhs_mat, rhs_mat, (((0,), (0,)), ((), ())), preferred_element_type=jnp.float32
    )


def contract_cols(lhs_mat, rhs_mat):
    return lax.dot_general(
        lhs_mat, rhs_mat, (((1,), (1,)), ((), ())), preferred_element_type=jnp.float32
    )


def layer_norm(values, scale_gain, shift_bias):
    average = jnp.mean(values, axis=-1, keepdims=True)
    centered = values - average
    inverse = lax.rsqrt(jnp.mean(centered * centered, axis=-1, keepdims=True) + NORM_EPS)
    normed = centered * inverse
    return (normed * (1.0 + scale_gain) + shift_bias, (normed, inverse))


def norm_back(upstream, stored, scale_gain):
    normed, inverse = stored
    scaled = upstream * (1.0 + scale_gain)
    back = inverse * (
        scaled
        - jnp.mean(scaled, axis=-1, keepdims=True)
        - normed * jnp.mean(scaled * normed, axis=-1, keepdims=True)
    )
    return (back, jnp.sum(upstream * normed, axis=0), jnp.sum(upstream, axis=0))


def starts_of(lengths):
    order = jnp.arange(PPD, dtype=jnp.int32)
    before = (order[:, None] > order[None, :]).astype(jnp.int32)
    return jnp.sum(before * lengths[..., None, :], axis=-1)


def layout_of(lengths):
    starts = starts_of(lengths)
    place = jnp.arange(ROW, dtype=jnp.int32)
    above = (place[:, None] >= starts[..., None, :]).astype(jnp.int32)
    segment = jnp.sum(above, axis=-1) - 1
    begin = jnp.max(above * starts[..., None, :], axis=-1)
    return segment, place - begin


def one_hot(index, depth):
    return (index[..., None] == jnp.arange(depth, dtype=jnp.int32)).astype(BF)


def split_two(values):
    high = lax.reduce_precision(values, 8, 7)
    return high.astype(BF), (values - high).astype(BF)


def split_three(values):
    high = lax.reduce_precision(values, 8, 7)
    middle = lax.reduce_precision(values - high, 8, 7)
    return high.astype(BF), middle.astype(BF), (values - high - middle).astype(BF)


def window_start(block, count):
    return min(max(block * BLK - (WIN - BLK) // 2, 0), count - WIN)


def attn_forward_kernel(count, segc_ref, segw_ref, z_ref, o_ref, lse_ref):
    block = pl.program_id(0)
    row = pl.multiple_of(block * BLK, BLK)
    first = pl.multiple_of(jnp.clip(row - (WIN - BLK) // 2, 0, count - WIN), 64)
    allowed = segc_ref[...] == segw_ref[0]
    lane = lax.broadcasted_iota(jnp.int32, (BLK, 2 * HD), 1)
    lane_head = lax.broadcasted_iota(jnp.int32, (BLK, 128), 1)
    kept = jnp.zeros((BLK, 128), F32)
    for pair in range(HEADS // 2):
        at = pair * 2 * HD
        query = z_ref[pl.ds(row, BLK), at : at + 2 * HD] * BF(HD ** (-0.5))
        key = z_ref[pl.ds(first, WIN), D + at : D + at + 2 * HD]
        value = z_ref[pl.ds(first, WIN), 2 * D + at : 2 * D + at + 2 * HD]
        parts = []
        for half in range(2):
            mine = (lane >= half * HD) & (lane < (half + 1) * HD)
            scores = contract_cols(jnp.where(mine, query, BF(0)), key)
            scores = jnp.where(allowed, scores, -1000000000.0)
            top = jnp.max(scores, axis=-1, keepdims=True)
            weight = jnp.exp(scores - top)
            total = jnp.sum(weight, axis=-1, keepdims=True)
            probs = (weight * (1.0 / total)).astype(BF)
            parts.append(matmul(probs, value))
            kept = jnp.where(lane_head == 2 * pair + half, top + jnp.log(total), kept)
        o_ref[:, at : at + 2 * HD] = jnp.where(lane < HD, parts[0], parts[1]).astype(BF)
    lse_ref[...] = kept


def attn_backward_kernel(
    count, blocks, segc_ref, segw_ref, z_ref, do_ref, lse_ref, dz_ref, dk_ref, dv_ref
):
    block = pl.program_id(0)
    row = pl.multiple_of(block * BLK, BLK)
    first = pl.multiple_of(jnp.clip(row - (WIN - BLK) // 2, 0, count - WIN), 64)

    @pl.when(block == 0)
    def _():
        dk_ref[...] = jnp.zeros_like(dk_ref)
        dv_ref[...] = jnp.zeros_like(dv_ref)

    allowed = segc_ref[...] == segw_ref[0]
    lane = lax.broadcasted_iota(jnp.int32, (BLK, 2 * HD), 1)
    kept = lse_ref[...]
    for pair in range(HEADS // 2):
        at = pair * 2 * HD
        query = z_ref[pl.ds(row, BLK), at : at + 2 * HD] * BF(HD ** (-0.5))
        key = z_ref[pl.ds(first, WIN), D + at : D + at + 2 * HD]
        value = z_ref[pl.ds(first, WIN), 2 * D + at : 2 * D + at + 2 * HD]
        upstream = do_ref[:, at : at + 2 * HD]
        grad_query = []
        grad_key = jnp.zeros((WIN, 2 * HD), F32)
        grad_value = jnp.zeros((WIN, 2 * HD), F32)
        for half in range(2):
            mine = (lane >= half * HD) & (lane < (half + 1) * HD)
            query_own = jnp.where(mine, query, BF(0))
            up_own = jnp.where(mine, upstream, BF(0))
            scores = jnp.where(allowed, contract_cols(query_own, key), -1000000000.0)
            probs = jnp.exp(scores - kept[:, 2 * pair + half : 2 * pair + half + 1])
            grad_probs = contract_cols(up_own, value)
            grad_value = grad_value + contract_rows(probs.astype(BF), up_own)
            inner = jnp.sum(grad_probs * probs, axis=-1, keepdims=True)
            grad_scores = (probs * (grad_probs - inner)).astype(BF)
            grad_query.append(matmul(grad_scores, key))
            grad_key = grad_key + contract_rows(grad_scores, query_own)
        own = jnp.where(lane < HD, grad_query[0], grad_query[1]) * HD ** (-0.5)
        dz_ref[pl.ds(row, BLK), at : at + 2 * HD] = own.astype(BF)
        dk_ref[pl.ds(first, WIN), at : at + 2 * HD] += grad_key
        dv_ref[pl.ds(first, WIN), at : at + 2 * HD] += grad_value

    @pl.when(block == blocks - 1)
    def _():
        dz_ref[:, D : 2 * D] = dk_ref[...].astype(BF)
        dz_ref[:, 2 * D :] = dv_ref[...].astype(BF)


def attention_specs(count):
    return [
        pl.BlockSpec((BLK, 1), lambda i: (i, 0)),
        pl.BlockSpec((1, 1, WIN), lambda i: (i, 0, 0)),
        pl.BlockSpec((count, 3 * D), lambda i: (0, 0)),
    ]


def attention_forward(segment_column, segment_windows, mixed):
    count = mixed.shape[0]
    blocks = count // BLK
    return pl.pallas_call(
        lambda *refs: attn_forward_kernel(count, *refs),
        grid=(blocks,),
        in_specs=attention_specs(count),
        out_specs=[
            pl.BlockSpec((BLK, D), lambda i: (i, 0)),
            pl.BlockSpec((BLK, 128), lambda i: (i, 0)),
        ],
        out_shape=[
            jax.ShapeDtypeStruct((count, D), BF),
            jax.ShapeDtypeStruct((count, 128), F32),
        ],
        compiler_params=pltpu.CompilerParams(vmem_limit_bytes=40 * 2**20),
        cost_estimate=pl.CostEstimate(
            flops=4 * count * WIN * 128 * HEADS, bytes_accessed=12000000, transcendentals=0
        ),
    )(segment_column, segment_windows, mixed)


def attention_backward(segment_column, segment_windows, mixed, upstream, kept):
    count = mixed.shape[0]
    blocks = count // BLK
    return pl.pallas_call(
        lambda *refs: attn_backward_kernel(count, blocks, *refs),
        grid=(blocks,),
        in_specs=attention_specs(count)
        + [
            pl.BlockSpec((BLK, D), lambda i: (i, 0)),
            pl.BlockSpec((BLK, 128), lambda i: (i, 0)),
        ],
        out_specs=pl.BlockSpec((count, 3 * D), lambda i: (0, 0)),
        out_shape=jax.ShapeDtypeStruct((count, 3 * D), BF),
        scratch_shapes=[pltpu.VMEM((count, D), F32), pltpu.VMEM((count, D), F32)],
        compiler_params=pltpu.CompilerParams(vmem_limit_bytes=56 * 2**20),
        cost_estimate=pl.CostEstimate(
            flops=10 * count * WIN * 128 * HEADS, bytes_accessed=18000000, transcendentals=0
        ),
    )(segment_column, segment_windows, mixed, upstream, kept)


def swap_half(parts, axis_name, bit, axis):
    size = lax.axis_size(axis_name)
    mine = (lax.axis_index(axis_name) >> bit) & 1
    pairs = [(i, i ^ (1 << bit)) for i in range(size)]
    sent = lax.dynamic_index_in_dim(parts, 1 - mine, axis, keepdims=False).astype(BF)
    held = lax.dynamic_index_in_dim(parts, mine, axis, keepdims=False)
    return held + lax.ppermute(sent, axis_name, pairs).astype(F32)


def reduce_rows(gradient, group_first):
    group_bits = lax.axis_size("grp").bit_length() - 1
    member_bits = lax.axis_size("psg").bit_length() - 1
    rows = gradient.shape[0] // (1 << (group_bits + member_bits))
    shape = (2,) * (group_bits + member_bits) + (rows, gradient.shape[1])
    parts = gradient.reshape(shape)
    names = [("grp", b) for b in reversed(range(group_bits))] + [
        ("psg", b) for b in reversed(range(member_bits))
    ]
    order = [("psg", 0)]
    if group_first:
        order += [("grp", 0)] + [("psg", b) for b in range(1, member_bits)]
        order += [("grp", b) for b in range(1, group_bits)]
    else:
        order += [("psg", b) for b in range(1, member_bits)]
        order += [("grp", b) for b in range(group_bits)]
    for step in order:
        at = names.index(step)
        parts = swap_half(parts, step[0], step[1], at)
        names.pop(at)
    return parts


def adam_update(weight, moment, second, gradient, rate, count_steps):
    moment_new = BETA_ONE * moment + (1.0 - BETA_ONE) * gradient
    second_new = BETA_TWO * second + (1.0 - BETA_TWO) * gradient * gradient
    corrected = moment_new / (1.0 - BETA_ONE**count_steps)
    scaled = second_new / (1.0 - BETA_TWO**count_steps)
    weight_new = weight - rate * (corrected / (jnp.sqrt(scaled) + ADAM_EPS) + WEIGHT_DECAY * weight)
    return (weight_new, second_new)


def on_device(
    query_ids,
    passage_ids,
    passage_lengths,
    positives,
    negatives,
    pair_mask,
    assignments,
    step_count,
    embed_table,
    embed_table_moment,
    embed_table_second,
    attention_weight,
    attention_weight_moment,
    attention_weight_second,
    up_weight,
    up_weight_moment,
    up_weight_second,
    down_weight,
    down_weight_moment,
    down_weight_second,
    head_weight,
    head_weight_moment,
    head_weight_second,
    small_params,
    small_params_moment,
    small_params_second,
):
    devices = lax.axis_size("grp") * lax.axis_size("psg")
    members = lax.axis_size("psg")
    member = lax.axis_index("psg")
    group = lax.axis_index("grp")
    shard_rows = embed_table.shape[0]
    queries = query_ids.shape[0]
    negative_count = negatives.shape[1]
    query_rows = queries * SEG
    count = ROW + query_rows
    capacity = 16 * ((count // devices + 8 + 15) // 16)
    small_size = small_params.shape[0]
    head_rows = head_weight.shape[0]
    mask_float = pair_mask.astype(F32)

    tokens = jnp.concatenate([passage_ids.reshape(-1), query_ids.reshape(-1)])
    passage_segment, passage_position = layout_of(passage_lengths[0])
    query_place = jnp.arange(query_rows, dtype=jnp.int32)
    segment = jnp.concatenate([passage_segment, PPD + query_place // SEG])
    position = jnp.concatenate([passage_position, query_place % SEG])
    segment_column = segment[:, None]
    segment_windows = jnp.stack(
        [
            segment[window_start(i, count) : window_start(i, count) + WIN][None]
            for i in range(count // BLK)
        ]
    )

    attn_rows = lax.all_gather(attention_weight.T.astype(BF), ALL, axis=0, tiled=True)
    up_rows = lax.all_gather(up_weight.T.astype(BF), ALL, axis=0, tiled=True)
    down_rows = lax.all_gather(down_weight.astype(BF), ALL, axis=0, tiled=True)

    owner = tokens // shard_rows
    local_row = tokens - owner * shard_rows
    owner_hot = one_hot(owner, devices)
    row_hot = one_hot(local_row, shard_rows)
    needed = jnp.minimum(contract_rows(owner_hot, row_hot), 1.0).astype(BF)
    spread = lambda v: jnp.broadcast_to(v.reshape(1, -1).astype(BF), (devices, v.size))
    payload = jnp.concatenate(
        [
            needed,
            spread(small_params),
            spread(head_weight),
            spread(passage_lengths),
            spread(jnp.sum(mask_float)),
        ],
        axis=1,
    )
    width = payload.shape[1]
    payload = jnp.pad(payload, ((0, 0), (0, -width % 128)))
    arrived = lax.all_to_all(payload, ALL, split_axis=0, concat_axis=0, tiled=True)
    cut = [0, shard_rows, small_size, head_rows * DC, PPD, 1]
    for i in range(1, len(cut)):
        cut[i] += cut[i - 1]
    asked, small_all, head_all, lengths_all, pairs_all = (
        arrived[:, cut[i] : cut[i + 1]] for i in range(5)
    )
    small_all = small_all.reshape(-1)
    head_full = head_all.reshape(D, DC)
    pair_floor = jnp.maximum(jnp.sum(pairs_all.astype(F32)), 1.0)
    place_row = jnp.arange(shard_rows, dtype=jnp.int32)
    earlier = (place_row[:, None] < place_row[None, :]).astype(BF)
    asked_rank = matmul(asked, earlier)
    slots = jnp.arange(capacity, dtype=jnp.int32).astype(F32)
    picked = (
        ((asked_rank[:, None, :] == slots[None, :, None]) & (asked[:, None, :] > 0))
        .astype(BF)
        .reshape(devices * capacity, shard_rows)
    )
    packed = matmul(picked, embed_table.astype(BF)).astype(BF).reshape(devices, capacity, D)
    too_many = jnp.max(jnp.sum(asked.astype(F32), axis=1)) > capacity
    last_slot = (jnp.arange(capacity) == capacity - 1)[None, :, None]
    packed = jnp.where(too_many & last_slot, BF(MARK), packed)
    packed = lax.all_to_all(packed, ALL, split_axis=0, concat_axis=0, tiled=True)
    overflow = jnp.max(packed[:, capacity - 1, :].astype(F32)) > 0.5 * MARK
    packed = packed.reshape(devices * capacity, D)
    needed_rank = jnp.minimum(matmul(needed, earlier), 255.0)
    token_rank = jnp.sum(matmul(owner_hot, needed_rank.astype(BF)) * row_hot.astype(F32), axis=1)
    slot = owner * capacity + jnp.minimum(token_rank.astype(jnp.int32), capacity - 1)
    slot_hot = one_hot(slot, devices * capacity)
    looked_up = lax.cond(
        overflow,
        lambda: lax.all_gather(embed_table.astype(BF), ALL, axis=0, tiled=True)[tokens].astype(F32),
        lambda: matmul(slot_hot, packed),
    )

    positions = small_all[: PMAX * D].reshape(PMAX, D)
    remainder = small_all[PMAX * D :].astype(F32)
    pieces = [remainder[i * D : (i + 1) * D] for i in range(10)]
    bias_up = remainder[10 * D :]
    position_hot = one_hot(position, PMAX)
    embedded = looked_up + matmul(position_hot, positions)
    hidden_zero, norm_zero = layer_norm(embedded, pieces[0], pieces[1])
    input_zero = hidden_zero.astype(BF)
    bias_mixed = jnp.concatenate([pieces[2], jnp.zeros((D,), F32), pieces[3]])
    mixed = (contract_cols(input_zero, attn_rows[: 3 * D]) + bias_mixed).astype(BF)
    context, kept = attention_forward(segment_column, segment_windows, mixed)
    hidden_one, norm_one = layer_norm(
        hidden_zero + contract_cols(context, attn_rows[3 * D :]) + pieces[4], pieces[5], pieces[6]
    )
    input_one = hidden_one.astype(BF)
    inner = contract_cols(input_one, up_rows) + bias_up
    activated = jax.nn.gelu(inner, approximate=False).astype(BF)
    hidden_two, norm_two = layer_norm(
        hidden_one + matmul(activated, down_rows) + pieces[7], pieces[8], pieces[9]
    )
    input_two = hidden_two.astype(BF)
    projected = matmul(input_two, head_full)
    scale_inverse = lax.rsqrt(jnp.sum(projected * projected, axis=-1, keepdims=True) + NORM_EPS)
    unit = projected * scale_inverse
    unit_low = unit.astype(BF)

    units = lax.all_gather(unit_low, "psg", axis=0)
    group_passage = units[:, :ROW]
    group_query = units[:, ROW:].reshape(members * query_rows, DC)
    own_query = unit_low[ROW:]
    own_passage = unit_low[:ROW]
    group_lengths = lax.dynamic_slice_in_dim(lengths_all, group * members, members, 0)
    group_segment, _ = layout_of(group_lengths.astype(jnp.int32))
    group_hot = one_hot(group_segment, PPD)
    passage_hot = one_hot(passage_segment, PPD)

    weighted_own = jnp.exp(
        jnp.einsum("qd,mtd->mqt", own_query, group_passage, preferred_element_type=F32) / TEMPER
    )
    sum_own = lambda part: jnp.einsum(
        "mqt,mtp->mqp", part, group_hot, preferred_element_type=F32
    )
    high, low = split_two(weighted_own)
    totals_own = sum_own(high) + sum_own(low)
    weighted = jnp.exp(contract_cols(group_query, own_passage) / TEMPER)
    high, low = split_two(weighted)
    totals = matmul(high, passage_hot) + matmul(low, passage_hot)
    own_scores = jnp.sum(
        (TEMPER * jnp.log(totals_own)).reshape(members, queries, SEG, PPD), axis=2
    )
    own_scores = own_scores.transpose(1, 0, 2).reshape(queries, members * PPD)
    columns = jnp.arange(members * PPD, dtype=jnp.int32)
    pick_positive = (positives[:, None] == columns[None, :]).astype(F32)
    pick_negative = (negatives[:, :, None] == columns[None, None, :]).astype(F32)
    pos_score = jnp.sum(own_scores * pick_positive, axis=1)
    neg_score = jnp.sum(pick_negative * own_scores[:, None, :], axis=2)
    margins = MARGIN - pos_score[:, None] + neg_score
    numerator = jnp.sum(mask_float * jax.nn.softplus(margins))
    factor = mask_float * jax.nn.sigmoid(margins) / pair_floor
    grad_own = (
        jnp.sum(factor[:, :, None] * pick_negative, axis=1)
        - jnp.sum(factor, axis=1)[:, None] * pick_positive
    )
    grad_group = lax.all_gather(grad_own, "psg", axis=0, tiled=True)
    grad_local = lax.dynamic_slice_in_dim(grad_group, member * PPD, PPD, 1)

    grad_own_split = grad_own.reshape(queries, 1, members, PPD).transpose(2, 0, 1, 3)
    ratio_own = (
        (TEMPER * grad_own_split) / totals_own.reshape(members, queries, SEG, PPD)
    ).reshape(members, query_rows, PPD)
    spread_own = jnp.einsum(
        "mqp,mtp->mqt", ratio_own.astype(BF), group_hot, preferred_element_type=F32
    )
    sims_own = (spread_own * weighted_own / TEMPER).astype(BF)
    grad_unit_query = jnp.einsum(
        "mqt,mtd->qd", sims_own, group_passage, preferred_element_type=F32
    )
    ratio = (
        (TEMPER * grad_local[:, None, :]) / totals.reshape(members * queries, SEG, PPD)
    ).reshape(members * query_rows, PPD)
    sims = (contract_cols(ratio.astype(BF), passage_hot) * weighted / TEMPER).astype(BF)
    grad_unit_passage = contract_rows(sims, group_query)
    grad_unit = jnp.concatenate([grad_unit_passage, grad_unit_query])

    grad_proj = (
        (grad_unit - unit * jnp.sum(grad_unit * unit, axis=-1, keepdims=True)) * scale_inverse
    ).astype(BF)
    grad_head = contract_rows(input_two, grad_proj)
    picks = one_hot(assignments[0], NCENT)
    centroid_part = contract_rows(picks, own_passage)
    count_part = jnp.sum(picks.astype(F32), axis=0)
    count_high, count_low = split_two(count_part)
    early = jnp.concatenate(
        [
            centroid_part.astype(BF).reshape(devices, -1),
            grad_head.astype(BF).reshape(devices, -1),
            count_high.reshape(devices, -1),
            count_low.reshape(devices, -1),
        ]
        + [spread(v) for v in split_three(numerator)],
        axis=1,
    )
    early_width = early.shape[1]
    early = jnp.pad(early, ((0, 0), (0, -early_width % 128)))
    early = lax.all_to_all(early, ALL, split_axis=0, concat_axis=0, tiled=True)
    early = jnp.sum(early.astype(F32), axis=0)
    cent_rows = NCENT // devices
    at = cent_rows * DC
    centroid_sums = early[:at].reshape(cent_rows, DC)
    head_reduced = early[at : at + head_rows * DC].reshape(head_rows, DC)
    at += head_rows * DC
    centroid_counts = early[at : at + cent_rows] + early[at + cent_rows : at + 2 * cent_rows]
    at += 2 * cent_rows
    loss = (early[at] + early[at + 1] + early[at + 2]) / pair_floor

    grad_hidden_two = contract_cols(grad_proj, head_full)
    grad_sum_two, grad_gain_two, grad_shift_two = norm_back(grad_hidden_two, norm_two, pieces[8])
    grad_two_low = grad_sum_two.astype(BF)
    down_reduced = reduce_rows(contract_rows(activated, grad_two_low), False)
    grad_activated = contract_cols(grad_two_low, down_rows)
    normal_cdf = 0.5 * (1.0 + lax.erf(inner / math.sqrt(2.0)))
    normal_pdf = jnp.exp(-0.5 * inner * inner) / math.sqrt(2.0 * math.pi)
    grad_inner = (grad_activated * (normal_cdf + inner * normal_pdf)).astype(BF)
    up_reduced = reduce_rows(contract_rows(grad_inner, input_one), True)
    grad_bias_up = jnp.sum(grad_inner.astype(F32), axis=0)
    grad_hidden_one = grad_sum_two + matmul(grad_inner, up_rows)
    grad_sum_one, grad_gain_one, grad_shift_one = norm_back(grad_hidden_one, norm_one, pieces[5])
    grad_one_low = grad_sum_one.astype(BF)
    grad_out_rows = contract_rows(grad_one_low, context)
    grad_context = matmul(grad_one_low, attn_rows[3 * D :]).astype(BF)
    grad_mixed = attention_backward(segment_column, segment_windows, mixed, grad_context, kept)
    grad_mixed_sum = jnp.sum(grad_mixed.astype(F32), axis=0)
    grad_hidden_zero = grad_sum_one + matmul(grad_mixed, attn_rows[: 3 * D])
    grad_embedded, grad_gain_zero, grad_shift_zero = norm_back(
        grad_hidden_zero, norm_zero, pieces[0]
    )
    grad_qkv_rows = contract_rows(grad_mixed, input_zero)
    attn_reduced = reduce_rows(jnp.concatenate([grad_qkv_rows, grad_out_rows], axis=0), False)

    grad_low = grad_embedded.astype(BF)
    grad_positions = contract_rows(position_hot, grad_low)
    grad_slots = contract_rows(slot_hot, grad_low).astype(BF).reshape(devices, capacity, D)
    grad_slots = lax.all_to_all(grad_slots, ALL, split_axis=0, concat_axis=0, tiled=True)

    def whole_table():
        table = jnp.zeros((shard_rows * devices, D), F32).at[tokens].add(grad_embedded)
        return lax.psum_scatter(table, ALL, scatter_dimension=0, tiled=True)

    table_reduced = lax.cond(
        overflow,
        whole_table,
        lambda: contract_rows(picked, grad_slots.reshape(devices * capacity, D)),
    )
    grad_small = jnp.concatenate(
        [
            grad_positions.reshape(-1),
            grad_gain_zero,
            grad_shift_zero,
            grad_mixed_sum[:D],
            grad_mixed_sum[2 * D :],
            jnp.sum(grad_sum_one, axis=0),
            grad_gain_one,
            grad_shift_one,
            jnp.sum(grad_sum_two, axis=0),
            grad_gain_two,
            grad_shift_two,
            grad_bias_up,
        ]
    ).reshape(devices, small_size)
    grad_small = jnp.pad(grad_small, ((0, 0), (0, -small_size % 128)))
    grad_small = lax.all_to_all(grad_small, ALL, split_axis=0, concat_axis=0, tiled=True)
    small_reduced = jnp.sum(grad_small, axis=0)[:small_size]

    count_steps = step_count[0].astype(F32)
    attn_reduced = attn_reduced.T
    up_reduced = up_reduced.T
    table_new, table_second_new = adam_update(
        embed_table, embed_table_moment, embed_table_second, table_reduced, RATE_TABLE, count_steps
    )
    attn_new, attn_second_new = adam_update(
        attention_weight,
        attention_weight_moment,
        attention_weight_second,
        attn_reduced,
        RATE_MATRIX,
        count_steps,
    )
    up_new, up_second_new = adam_update(
        up_weight, up_weight_moment, up_weight_second, up_reduced, RATE_MATRIX, count_steps
    )
    down_new, down_second_new = adam_update(
        down_weight, down_weight_moment, down_weight_second, down_reduced, RATE_MATRIX, count_steps
    )
    head_new, head_second_new = adam_update(
        head_weight, head_weight_moment, head_weight_second, head_reduced, RATE_MATRIX, count_steps
    )
    small_new, small_second_new = adam_update(
        small_params, small_params_moment, small_params_second, small_reduced, RATE_TABLE, count_steps
    )
    return (
        loss,
        centroid_sums,
        centroid_counts,
        table_new,
        table_reduced,
        table_second_new,
        attn_new,
        attn_reduced,
        attn_second_new,
        up_new,
        up_reduced,
        up_second_new,
        down_new,
        down_reduced,
        down_second_new,
        head_new,
        head_reduced,
        head_second_new,
        small_new,
        small_reduced,
        small_second_new,
    )


def solution(mesh):
    in_specs = (
        P(("grp", "psg"), None),
        P(("grp", "psg"), None),
        P(("grp", "psg"), None),
        P(("grp", "psg")),
        P(("grp", "psg"), None),
        P(("grp", "psg"), None),
        P(("grp", "psg"), None),
        P(),
        P(("grp", "psg"), None),
        P(("grp", "psg"), None),
        P(("grp", "psg"), None),
        P(None, ("grp", "psg")),
        P(None, ("grp", "psg")),
        P(None, ("grp", "psg")),
        P(None, ("grp", "psg")),
        P(None, ("grp", "psg")),
        P(None, ("grp", "psg")),
        P(("grp", "psg"), None),
        P(("grp", "psg"), None),
        P(("grp", "psg"), None),
        P(("grp", "psg"), None),
        P(("grp", "psg"), None),
        P(("grp", "psg"), None),
        P(("grp", "psg")),
        P(("grp", "psg")),
        P(("grp", "psg")),
    )
    out_specs = (
        P(),
        P(("grp", "psg"), None),
        P(("grp", "psg")),
        P(("grp", "psg"), None),
        P(("grp", "psg"), None),
        P(("grp", "psg"), None),
        P(None, ("grp", "psg")),
        P(None, ("grp", "psg")),
        P(None, ("grp", "psg")),
        P(None, ("grp", "psg")),
        P(None, ("grp", "psg")),
        P(None, ("grp", "psg")),
        P(("grp", "psg"), None),
        P(("grp", "psg"), None),
        P(("grp", "psg"), None),
        P(("grp", "psg"), None),
        P(("grp", "psg"), None),
        P(("grp", "psg"), None),
        P(("grp", "psg")),
        P(("grp", "psg")),
        P(("grp", "psg")),
    )
    return jax.shard_map(
        on_device, mesh=mesh, in_specs=in_specs, out_specs=out_specs, check_vma=False
    )
```

```python
import math

import jax
import jax.numpy as jnp
from jax import lax
from jax.experimental import pallas as pl
from jax.experimental.pallas import tpu as pltpu
from jax.sharding import PartitionSpec as P

D = 768
HEADS = 12
HD = 64
SEG = 32
PMAX = 64
ROW = 1024
PPD = 32
QDEV = 8
NCENT = 1024
DC = 128
BLK = 128
WIN = 256
ALL = ("grp", "psg")
BF = jnp.bfloat16
F32 = jnp.float32
MARK = 1e30


TEMPER = 0.2
MARGIN = 1.0
NORM_EPS = 1e-06
BETA_ONE = 0.9
BETA_TWO = 0.999
ADAM_EPS = 1e-08
WEIGHT_DECAY = 0.01
RATE_MATRIX = 0.01
RATE_TABLE = 0.1


def matmul(lhs_mat, rhs_mat):
    return jnp.dot(lhs_mat, rhs_mat, preferred_element_type=jnp.float32)


def contract_rows(lhs_mat, rhs_mat):
    return lax.dot_general(
        lhs_mat, rhs_mat, (((0,), (0,)), ((), ())), preferred_element_type=jnp.float32
    )


def contract_cols(lhs_mat, rhs_mat):
    return lax.dot_general(
        lhs_mat, rhs_mat, (((1,), (1,)), ((), ())), preferred_element_type=jnp.float32
    )


def layer_norm(values, scale_gain, shift_bias):
    average = jnp.mean(values, axis=-1, keepdims=True)
    centered = values - average
    inverse = lax.rsqrt(jnp.mean(centered * centered, axis=-1, keepdims=True) + NORM_EPS)
    normed = centered * inverse
    return (normed * (1.0 + scale_gain) + shift_bias, (normed, inverse))


def norm_back(upstream, stored, scale_gain):
    normed, inverse = stored
    scaled = upstream * (1.0 + scale_gain)
    back = inverse * (
        scaled
        - jnp.mean(scaled, axis=-1, keepdims=True)
        - normed * jnp.mean(scaled * normed, axis=-1, keepdims=True)
    )
    return (back, jnp.sum(upstream * normed, axis=0), jnp.sum(upstream, axis=0))


def starts_of(lengths):
    order = jnp.arange(PPD, dtype=jnp.int32)
    before = (order[:, None] > order[None, :]).astype(jnp.int32)
    return jnp.sum(before * lengths[..., None, :], axis=-1)


def layout_of(lengths):
    starts = starts_of(lengths)
    place = jnp.arange(ROW, dtype=jnp.int32)
    above = (place[:, None] >= starts[..., None, :]).astype(jnp.int32)
    segment = jnp.sum(above, axis=-1) - 1
    begin = jnp.max(above * starts[..., None, :], axis=-1)
    return segment, place - begin


def one_hot(index, depth):
    return (index[..., None] == jnp.arange(depth, dtype=jnp.int32)).astype(BF)


def split_two(values):
    high = lax.reduce_precision(values, 8, 7)
    return high.astype(BF), (values - high).astype(BF)


def split_three(values):
    high = lax.reduce_precision(values, 8, 7)
    middle = lax.reduce_precision(values - high, 8, 7)
    return high.astype(BF), middle.astype(BF), (values - high - middle).astype(BF)


def window_start(block, count):
    return min(max(block * BLK - (WIN - BLK) // 2, 0), count - WIN)


def attn_forward_kernel(count, segc_ref, segw_ref, z_ref, o_ref, lse_ref):
    block = pl.program_id(0)
    row = pl.multiple_of(block * BLK, BLK)
    first = pl.multiple_of(jnp.clip(row - (WIN - BLK) // 2, 0, count - WIN), 64)
    allowed = segc_ref[...] == segw_ref[0]
    lane = lax.broadcasted_iota(jnp.int32, (BLK, 2 * HD), 1)
    lane_head = lax.broadcasted_iota(jnp.int32, (BLK, 128), 1)
    kept = jnp.zeros((BLK, 128), F32)
    for pair in range(HEADS // 2):
        at = pair * 2 * HD
        query = z_ref[pl.ds(row, BLK), at : at + 2 * HD] * BF(HD ** (-0.5))
        key = z_ref[pl.ds(first, WIN), D + at : D + at + 2 * HD]
        value = z_ref[pl.ds(first, WIN), 2 * D + at : 2 * D + at + 2 * HD]
        parts = []
        for half in range(2):
            mine = (lane >= half * HD) & (lane < (half + 1) * HD)
            scores = contract_cols(jnp.where(mine, query, BF(0)), key)
            scores = jnp.where(allowed, scores, -1000000000.0)
            top = jnp.max(scores, axis=-1, keepdims=True)
            weight = jnp.exp(scores - top)
            total = jnp.sum(weight, axis=-1, keepdims=True)
            probs = (weight * (1.0 / total)).astype(BF)
            parts.append(matmul(probs, value))
            kept = jnp.where(lane_head == 2 * pair + half, top + jnp.log(total), kept)
        o_ref[:, at : at + 2 * HD] = jnp.where(lane < HD, parts[0], parts[1]).astype(BF)
    lse_ref[...] = kept


def attn_backward_kernel(
    count, blocks, segc_ref, segw_ref, z_ref, do_ref, lse_ref, dz_ref, dk_ref, dv_ref
):
    block = pl.program_id(0)
    row = pl.multiple_of(block * BLK, BLK)
    first = pl.multiple_of(jnp.clip(row - (WIN - BLK) // 2, 0, count - WIN), 64)

    @pl.when(block == 0)
    def _():
        dk_ref[...] = jnp.zeros_like(dk_ref)
        dv_ref[...] = jnp.zeros_like(dv_ref)

    allowed = segc_ref[...] == segw_ref[0]
    lane = lax.broadcasted_iota(jnp.int32, (BLK, 2 * HD), 1)
    kept = lse_ref[...]
    for pair in range(HEADS // 2):
        at = pair * 2 * HD
        query = z_ref[pl.ds(row, BLK), at : at + 2 * HD] * BF(HD ** (-0.5))
        key = z_ref[pl.ds(first, WIN), D + at : D + at + 2 * HD]
        value = z_ref[pl.ds(first, WIN), 2 * D + at : 2 * D + at + 2 * HD]
        upstream = do_ref[:, at : at + 2 * HD]
        grad_query = []
        grad_key = jnp.zeros((WIN, 2 * HD), F32)
        grad_value = jnp.zeros((WIN, 2 * HD), F32)
        for half in range(2):
            mine = (lane >= half * HD) & (lane < (half + 1) * HD)
            query_own = jnp.where(mine, query, BF(0))
            up_own = jnp.where(mine, upstream, BF(0))
            scores = jnp.where(allowed, contract_cols(query_own, key), -1000000000.0)
            probs = jnp.exp(scores - kept[:, 2 * pair + half : 2 * pair + half + 1])
            grad_probs = contract_cols(up_own, value)
            grad_value = grad_value + contract_rows(probs.astype(BF), up_own)
            inner = jnp.sum(grad_probs * probs, axis=-1, keepdims=True)
            grad_scores = (probs * (grad_probs - inner)).astype(BF)
            grad_query.append(matmul(grad_scores, key))
            grad_key = grad_key + contract_rows(grad_scores, query_own)
        own = jnp.where(lane < HD, grad_query[0], grad_query[1]) * HD ** (-0.5)
        dz_ref[pl.ds(row, BLK), at : at + 2 * HD] = own.astype(BF)
        dk_ref[pl.ds(first, WIN), at : at + 2 * HD] += grad_key
        dv_ref[pl.ds(first, WIN), at : at + 2 * HD] += grad_value

    @pl.when(block == blocks - 1)
    def _():
        dz_ref[:, D : 2 * D] = dk_ref[...].astype(BF)
        dz_ref[:, 2 * D :] = dv_ref[...].astype(BF)


def attention_specs(count):
    return [
        pl.BlockSpec((BLK, 1), lambda i: (i, 0)),
        pl.BlockSpec((1, 1, WIN), lambda i: (i, 0, 0)),
        pl.BlockSpec((count, 3 * D), lambda i: (0, 0)),
    ]


def attention_forward(segment_column, segment_windows, mixed):
    count = mixed.shape[0]
    blocks = count // BLK
    return pl.pallas_call(
        lambda *refs: attn_forward_kernel(count, *refs),
        grid=(blocks,),
        in_specs=attention_specs(count),
        out_specs=[
            pl.BlockSpec((BLK, D), lambda i: (i, 0)),
            pl.BlockSpec((BLK, 128), lambda i: (i, 0)),
        ],
        out_shape=[
            jax.ShapeDtypeStruct((count, D), BF),
            jax.ShapeDtypeStruct((count, 128), F32),
        ],
        compiler_params=pltpu.CompilerParams(vmem_limit_bytes=40 * 2**20),
        cost_estimate=pl.CostEstimate(
            flops=4 * count * WIN * 128 * HEADS, bytes_accessed=12000000, transcendentals=0
        ),
    )(segment_column, segment_windows, mixed)


def attention_backward(segment_column, segment_windows, mixed, upstream, kept):
    count = mixed.shape[0]
    blocks = count // BLK
    return pl.pallas_call(
        lambda *refs: attn_backward_kernel(count, blocks, *refs),
        grid=(blocks,),
        in_specs=attention_specs(count)
        + [
            pl.BlockSpec((BLK, D), lambda i: (i, 0)),
            pl.BlockSpec((BLK, 128), lambda i: (i, 0)),
        ],
        out_specs=pl.BlockSpec((count, 3 * D), lambda i: (0, 0)),
        out_shape=jax.ShapeDtypeStruct((count, 3 * D), BF),
        scratch_shapes=[pltpu.VMEM((count, D), F32), pltpu.VMEM((count, D), F32)],
        compiler_params=pltpu.CompilerParams(vmem_limit_bytes=56 * 2**20),
        cost_estimate=pl.CostEstimate(
            flops=10 * count * WIN * 128 * HEADS, bytes_accessed=18000000, transcendentals=0
        ),
    )(segment_column, segment_windows, mixed, upstream, kept)


def bits_of(axis_name):
    return [(axis_name, b) for b in range(lax.axis_size(axis_name).bit_length() - 1)]


def cut_chunks(gradient):
    names = bits_of("grp")[::-1] + bits_of("psg")[::-1]
    rows = gradient.shape[0] >> len(names)
    return gradient.reshape((2,) * len(names) + (rows, gradient.shape[1])), names


def halve_start(state, step):
    parts, names = state
    axis_name, bit = step
    at = names.index(step)
    mine = (lax.axis_index(axis_name) >> bit) & 1
    pairs = [(i, i ^ (1 << bit)) for i in range(lax.axis_size(axis_name))]
    sent = lax.dynamic_index_in_dim(parts, 1 - mine, at, keepdims=False).astype(BF)
    held = lax.dynamic_index_in_dim(parts, mine, at, keepdims=False)
    return held, lax.ppermute(sent, axis_name, pairs), names[:at] + names[at + 1 :]


def halve_end(flying):
    held, received, names = flying
    return held + received.astype(F32), names


def gate(value, *flying):
    value, received = lax.optimization_barrier((value, tuple(f[1] for f in flying)))
    return value, *((f[0], r, f[2]) for f, r in zip(flying, received))


def place_of():
    return lax.axis_index("grp") * lax.axis_size("psg") + lax.axis_index("psg")


def mesh_place(place):
    members = lax.axis_size("psg")
    return (place // members, place % members)


def flipped(place, mask):
    result, bit = place, 0
    while mask >> bit:
        if (mask >> bit) & 1:
            result = result + (1 - 2 * ((place // (1 << bit)) % 2)) * (1 << bit)
        bit += 1
    return result


def greet_all(devices, me):
    barrier = pltpu.get_barrier_semaphore()

    @pl.loop(1, devices)
    def _(i):
        pl.semaphore_signal(
            barrier,
            inc=1,
            device_id=mesh_place((me + i) % devices),
            device_id_type=pl.DeviceIdType.MESH,
        )

    pl.semaphore_wait(barrier, devices - 1)


def gather_plan(order, group):
    held, steps = [0], []
    for bit in order:
        fresh = [(1 << bit) | m for m in held]
        steps.append([fresh[i : i + group] for i in range(0, len(fresh), group)])
        held = held + fresh
    return steps


def pack_rows(asked, table, rank_ref, packed_ref):
    devices, capacity, _ = packed_ref.shape
    width = table.shape[0]
    asked = jnp.concatenate([asked[:, j, :] for j in range(width // 128)], axis=1)
    above = lax.broadcasted_iota(jnp.int32, (width, width), 0)
    earlier = (above < lax.broadcasted_iota(jnp.int32, (width, width), 1)).astype(F32).astype(BF)
    rank_ref[...] = jnp.where(asked > 0.5, matmul(asked.astype(BF), earlier), -1.0)
    most = jnp.max(jnp.sum(asked, axis=1, keepdims=True), axis=0, keepdims=True)
    together = 8

    @pl.loop(0, devices // together)
    def _(i):
        rank = rank_ref[pl.ds(pl.multiple_of(i * together, together), together), :]
        slot = lax.broadcasted_iota(jnp.int32, (together, capacity, width), 1).astype(F32)
        picked = jnp.where(rank[:, None, :] == slot, 1.0, 0.0)
        picked = picked.reshape(together * capacity, width).astype(BF)
        rows = matmul(picked, table[...]).reshape(together, capacity, D)
        place = lax.broadcasted_iota(jnp.int32, (together, capacity, D), 1)
        rows = jnp.where((place == capacity - 1) & (most > capacity)[:, :, None], MARK, rows)
        packed_ref[pl.ds(i * together, together)] = rows.astype(BF)


def gather_kernel(devices, pieces, *refs):
    matrices = 3
    sources, (needed, notes, table) = refs[:matrices], refs[matrices : matrices + 3]
    outs, (notes_out, rows_out, rank) = refs[6:9], refs[9:12]
    asked, packed, arrive, beside, leave, local, notes_sem, ask_sem, rows_sem = refs[12:]
    me = place_of()
    group = max(devices // 8, 1)
    greet_all(devices, me)

    def push(source, target_ref, target, send, recv):
        pltpu.make_async_remote_copy(
            src_ref=source,
            dst_ref=target_ref,
            send_sem=send,
            recv_sem=recv,
            device_id=mesh_place(target),
            device_id_type=pl.DeviceIdType.MESH,
        ).start()

    def settle(some, semaphore):
        pltpu.make_async_copy(some, some, semaphore).wait()

    @pl.loop(1, devices)
    def _(i):
        target = (me + i) % devices
        push(needed.at[target], asked.at[me], target, ask_sem.at[0], ask_sem.at[1])

    def start(piece, mask, target, semaphore):
        which, first, rows, _ = pieces[piece]
        there = outs[which].at[flipped(me, mask), pl.ds(first, rows)]
        here = sources[which].at[pl.ds(first, rows)] if mask == 0 else there
        push(here, there, flipped(me, target), leave.at[piece], semaphore)

    def wait(piece, blocks, semaphore):
        which, first, rows, _ = pieces[piece]
        settle(outs[which].at[pl.ds(0, blocks), pl.ds(first, rows)], semaphore)

    plans, numbers = [], []
    for piece in range(len(pieces)):
        plan = gather_plan(pieces[piece][3], group)
        number, count = {}, 0
        for groups in plan:
            for masks in groups:
                for mask in masks:
                    number[mask] = count
                count += 1
        plans.append(plan)
        numbers.append(number)

    def send_on(piece, mask, after):
        order = pieces[piece][3]
        for step in range(after + 1, len(order)):
            target = 1 << order[step]
            start(piece, mask, target, arrive.at[piece, numbers[piece][mask | target]])
        start(piece, mask, 1, beside.at[piece])

    def pass_on(piece, step):
        for masks in plans[piece][step]:
            wait(piece, len(masks), arrive.at[piece, numbers[piece][masks[0]]])
            for mask in masks:
                send_on(piece, mask, step)

    for piece in range(len(pieces)):
        send_on(piece, 0, -1)

    @pl.loop(1, devices)
    def _(i):
        target = (me + i) % devices
        push(notes, notes_out.at[me], target, notes_sem.at[0], notes_sem.at[1])

    own = [
        pltpu.make_async_copy(source, out.at[me], local.at[i])
        for i, (source, out) in enumerate(zip(sources, outs))
    ]
    own.append(pltpu.make_async_copy(notes, notes_out.at[me], local.at[matrices]))
    own_asked = pltpu.make_async_copy(needed.at[me], asked.at[me], local.at[matrices + 1])
    for copy in own:
        copy.start()
    own_asked.start()
    for piece in range(len(pieces)):
        pass_on(piece, 0)
    own_asked.wait()
    for i in range(2):
        settle(asked.at[pl.ds(0, devices - 1)], ask_sem.at[i])
    pack_rows(asked[...], table, rank, packed)

    masks = sorted(range(1, devices), key=lambda m: -bin(m).count("1"))
    steps = len(pieces[0][3])
    each = -(-(devices - 1) // (len(pieces) * (steps - 1)))
    kept_rows = pltpu.make_async_copy(packed.at[me], rows_out.at[me], local.at[matrices + 2])
    kept_rows.start()
    for step in range(1, steps):
        for piece in range(len(pieces)):
            pass_on(piece, step)
            now, masks = masks[:each], masks[each:]
            for mask in now:
                target = flipped(me, mask)
                push(packed.at[target], rows_out.at[me], target, rows_sem.at[0], rows_sem.at[1])
    for piece in range(len(pieces)):
        wait(piece, devices // 2, beside.at[piece])
        wait(piece, devices - 1, leave.at[piece])
    for copy in own:
        copy.wait()
    kept_rows.wait()
    for i in range(2):
        settle(notes_out.at[pl.ds(0, devices - 1)], notes_sem.at[i])
        settle(rows_out.at[pl.ds(0, devices - 1)], rows_sem.at[i])


def gather_all(sources, needed, notes, table, capacity):
    devices = needed.shape[0]
    rows = sources[0].shape[0]
    bits = devices.bit_length() - 1
    high = list(range(3, bits))[::-1]
    one, other = (*high, 2, 1), (*high, 1, 2)
    cut = rows // 32 * 16
    pieces = [(0, 0, rows, one), (2, 0, rows, other), (1, cut, rows - cut, one)]
    if cut:
        pieces.append((1, 0, cut, other))
    count = max(sum(map(len, gather_plan(p[3], max(devices // 8, 1)))) for p in pieces)
    anywhere = pl.BlockSpec(memory_space=pl.ANY)
    inside = pl.BlockSpec(memory_space=pltpu.VMEM)
    dma = pltpu.SemaphoreType.DMA
    *gathered, noted, arrived, rank = pl.pallas_call(
        lambda *refs: gather_kernel(devices, pieces, *refs),
        in_specs=[anywhere] * 3 + [inside] * 3,
        out_specs=[anywhere] * 5 + [inside],
        out_shape=[jax.ShapeDtypeStruct((devices, *s.shape), s.dtype) for s in (*sources, notes)]
        + [
            jax.ShapeDtypeStruct((devices, capacity, D), BF),
            jax.ShapeDtypeStruct((devices, table.shape[0]), F32),
        ],
        scratch_shapes=[
            pltpu.VMEM(needed.shape, F32),
            pltpu.VMEM((devices, capacity, D), BF),
            dma((len(pieces), count)),
            dma((len(pieces),)),
            dma((len(pieces),)),
            dma((6,)),
            dma((2,)),
            dma((2,)),
            dma((2,)),
        ],
        compiler_params=pltpu.CompilerParams(
            collective_id=0, has_side_effects=True, vmem_limit_bytes=48 * 2**20
        ),
    )(*sources, needed, notes, table)
    return gathered, noted, arrived, rank


def adam_update(weight, moment, second, gradient, rate, count_steps):
    moment_new = BETA_ONE * moment + (1.0 - BETA_ONE) * gradient
    second_new = BETA_TWO * second + (1.0 - BETA_TWO) * gradient * gradient
    corrected = moment_new / (1.0 - BETA_ONE**count_steps)
    scaled = second_new / (1.0 - BETA_TWO**count_steps)
    weight_new = weight - rate * (corrected / (jnp.sqrt(scaled) + ADAM_EPS) + WEIGHT_DECAY * weight)
    return (weight_new, second_new)


def on_device(
    query_ids,
    passage_ids,
    passage_lengths,
    positives,
    negatives,
    pair_mask,
    assignments,
    step_count,
    embed_table,
    embed_table_moment,
    embed_table_second,
    attention_weight,
    attention_weight_moment,
    attention_weight_second,
    up_weight,
    up_weight_moment,
    up_weight_second,
    down_weight,
    down_weight_moment,
    down_weight_second,
    head_weight,
    head_weight_moment,
    head_weight_second,
    small_params,
    small_params_moment,
    small_params_second,
):
    devices = lax.axis_size("grp") * lax.axis_size("psg")
    members = lax.axis_size("psg")
    member = lax.axis_index("psg")
    group = lax.axis_index("grp")
    shard_rows = embed_table.shape[0]
    queries = query_ids.shape[0]
    negative_count = negatives.shape[1]
    query_rows = queries * SEG
    count = ROW + query_rows
    capacity = 16 * ((count // devices + 8 + 15) // 16)
    small_size = small_params.shape[0]
    head_rows = head_weight.shape[0]
    mask_float = pair_mask.astype(F32)

    tokens = jnp.concatenate([passage_ids.reshape(-1), query_ids.reshape(-1)])
    passage_segment, passage_position = layout_of(passage_lengths[0])
    query_place = jnp.arange(query_rows, dtype=jnp.int32)
    segment = jnp.concatenate([passage_segment, PPD + query_place // SEG])
    position = jnp.concatenate([passage_position, query_place % SEG])
    segment_column = segment[:, None]
    segment_windows = jnp.stack(
        [
            segment[window_start(i, count) : window_start(i, count) + WIN][None]
            for i in range(count // BLK)
        ]
    )

    def shard_of(rows):
        return jnp.pad(rows.astype(BF), ((0, -rows.shape[0] % 16), (0, 0)))

    matrix_rows = down_weight.shape[0]
    shards = [shard_of(attention_weight.T), shard_of(up_weight.T), shard_of(down_weight)]

    owner = tokens // shard_rows
    local_row = tokens - owner * shard_rows
    owner_hot = one_hot(owner, devices)
    row_hot = one_hot(local_row, shard_rows)
    needed = jnp.minimum(contract_rows(owner_hot, row_hot), 1.0)
    width = -(-shard_rows // 1024) * 1024
    table = jnp.pad(embed_table.astype(BF), ((0, width - shard_rows), (0, 0)))
    notes = jnp.concatenate(
        [
            v.reshape(-1).astype(BF)
            for v in (small_params, head_weight, passage_lengths, jnp.sum(mask_float))
        ]
    )
    notes = jnp.pad(notes, (0, -notes.size % 2048)).reshape(-1, 128)
    gathered, noted, packed, asked_rank = gather_all(
        shards,
        jnp.pad(needed, ((0, 0), (0, width - shard_rows))).reshape(devices, width // 128, 128),
        notes,
        table,
        capacity,
    )
    asked_rank = asked_rank[:, :shard_rows]
    attn_rows, up_rows, down_rows = (g[:, :matrix_rows].reshape(-1, D) for g in gathered)
    noted = noted.reshape(devices, -1)
    cut = [0, small_size, head_rows * DC, PPD, 1]
    for i in range(1, len(cut)):
        cut[i] += cut[i - 1]
    small_all, head_all, lengths_all, pairs_all = (noted[:, cut[i] : cut[i + 1]] for i in range(4))
    small_all = small_all.reshape(-1)
    head_full = head_all.reshape(D, DC)
    pair_floor = jnp.maximum(jnp.sum(pairs_all.astype(F32)), 1.0)
    place_row = jnp.arange(shard_rows, dtype=jnp.int32)
    earlier = (place_row[:, None] < place_row[None, :]).astype(BF)
    overflow = jnp.max(packed[:, capacity - 1, :].astype(F32)) > 0.5 * MARK
    packed = packed.reshape(devices * capacity, D)
    needed_rank = jnp.minimum(matmul(needed.astype(BF), earlier), 255.0)
    token_rank = jnp.sum(matmul(owner_hot, needed_rank.astype(BF)) * row_hot.astype(F32), axis=1)
    slot = owner * capacity + jnp.minimum(token_rank.astype(jnp.int32), capacity - 1)
    slot_hot = one_hot(slot, devices * capacity)
    looked_up = lax.cond(
        overflow,
        lambda: lax.all_gather(embed_table.astype(BF), ALL, axis=0, tiled=True)[tokens].astype(F32),
        lambda: matmul(slot_hot, packed),
    )

    positions = small_all[: PMAX * D].reshape(PMAX, D)
    remainder = small_all[PMAX * D :].astype(F32)
    pieces = [remainder[i * D : (i + 1) * D] for i in range(10)]
    bias_up = remainder[10 * D :]
    position_hot = one_hot(position, PMAX)
    embedded = looked_up + matmul(position_hot, positions)
    hidden_zero, norm_zero = layer_norm(embedded, pieces[0], pieces[1])
    input_zero = hidden_zero.astype(BF)
    bias_mixed = jnp.concatenate([pieces[2], jnp.zeros((D,), F32), pieces[3]])
    mixed = (contract_cols(input_zero, attn_rows[: 3 * D]) + bias_mixed).astype(BF)
    context, kept = attention_forward(segment_column, segment_windows, mixed)
    hidden_one, norm_one = layer_norm(
        hidden_zero + contract_cols(context, attn_rows[3 * D :]) + pieces[4], pieces[5], pieces[6]
    )
    input_one = hidden_one.astype(BF)
    inner = contract_cols(input_one, up_rows) + bias_up
    activated = (0.5 * inner * (1.0 + lax.erf(inner / math.sqrt(2.0)))).astype(BF)
    hidden_two, norm_two = layer_norm(
        hidden_one + matmul(activated, down_rows) + pieces[7], pieces[8], pieces[9]
    )
    input_two = hidden_two.astype(BF)
    projected = matmul(input_two, head_full)
    scale_inverse = lax.rsqrt(jnp.sum(projected * projected, axis=-1, keepdims=True) + NORM_EPS)
    unit = projected * scale_inverse
    unit_low = unit.astype(BF)

    units = lax.all_gather(unit_low, "psg", axis=0)
    group_passage = units[:, :ROW]
    group_query = units[:, ROW:].reshape(members * query_rows, DC)
    own_query = unit_low[ROW:]
    own_passage = unit_low[:ROW]
    group_lengths = lax.dynamic_slice_in_dim(lengths_all, group * members, members, 0)
    group_segment, _ = layout_of(group_lengths.astype(jnp.int32))
    group_hot = one_hot(group_segment, PPD)
    passage_hot = one_hot(passage_segment, PPD)

    weighted_own = jnp.exp(
        jnp.einsum("qd,mtd->mqt", own_query, group_passage, preferred_element_type=F32) / TEMPER
    )
    sum_own = lambda part: jnp.einsum(
        "mqt,mtp->mqp", part, group_hot, preferred_element_type=F32
    )
    high, low = split_two(weighted_own)
    totals_own = sum_own(high) + sum_own(low)
    weighted = jnp.exp(contract_cols(group_query, own_passage) / TEMPER)
    high, low = split_two(weighted)
    totals = matmul(high, passage_hot) + matmul(low, passage_hot)
    own_scores = jnp.sum(
        (TEMPER * jnp.log(totals_own)).reshape(members, queries, SEG, PPD), axis=2
    )
    own_scores = own_scores.transpose(1, 0, 2).reshape(queries, members * PPD)
    columns = jnp.arange(members * PPD, dtype=jnp.int32)
    pick_positive = (positives[:, None] == columns[None, :]).astype(F32)
    pick_negative = (negatives[:, :, None] == columns[None, None, :]).astype(F32)
    pos_score = jnp.sum(own_scores * pick_positive, axis=1)
    neg_score = jnp.sum(pick_negative * own_scores[:, None, :], axis=2)
    margins = MARGIN - pos_score[:, None] + neg_score
    numerator = jnp.sum(mask_float * jax.nn.softplus(margins))
    factor = mask_float * jax.nn.sigmoid(margins) / pair_floor
    grad_own = (
        jnp.sum(factor[:, :, None] * pick_negative, axis=1)
        - jnp.sum(factor, axis=1)[:, None] * pick_positive
    )
    grad_group = lax.all_gather(grad_own, "psg", axis=0, tiled=True)
    grad_local = lax.dynamic_slice_in_dim(grad_group, member * PPD, PPD, 1)

    grad_own_split = grad_own.reshape(queries, 1, members, PPD).transpose(2, 0, 1, 3)
    ratio_own = (
        (TEMPER * grad_own_split) / totals_own.reshape(members, queries, SEG, PPD)
    ).reshape(members, query_rows, PPD)
    spread_own = jnp.einsum(
        "mqp,mtp->mqt", ratio_own.astype(BF), group_hot, preferred_element_type=F32
    )
    sims_own = (spread_own * weighted_own / TEMPER).astype(BF)
    grad_unit_query = jnp.einsum(
        "mqt,mtd->qd", sims_own, group_passage, preferred_element_type=F32
    )
    ratio = (
        (TEMPER * grad_local[:, None, :]) / totals.reshape(members * queries, SEG, PPD)
    ).reshape(members * query_rows, PPD)
    sims = (contract_cols(ratio.astype(BF), passage_hot) * weighted / TEMPER).astype(BF)
    grad_unit_passage = contract_rows(sims, group_query)
    grad_unit = jnp.concatenate([grad_unit_passage, grad_unit_query])

    grad_proj = (
        (grad_unit - unit * jnp.sum(grad_unit * unit, axis=-1, keepdims=True)) * scale_inverse
    ).astype(BF)
    grad_head = contract_rows(input_two, grad_proj)
    picks = one_hot(assignments[0], NCENT)
    centroid_part = contract_rows(picks, own_passage)
    count_part = jnp.sum(picks.astype(F32), axis=0)
    count_high, count_low = split_two(count_part)
    early = jnp.concatenate(
        [
            centroid_part.astype(BF).reshape(devices, -1),
            grad_head.astype(BF).reshape(devices, -1),
            count_high.reshape(devices, -1),
            count_low.reshape(devices, -1),
        ]
        + [jnp.broadcast_to(v, (devices, 1)) for v in split_three(numerator)],
        axis=1,
    )
    early_width = early.shape[1]
    early = jnp.pad(early, ((0, 0), (0, -early_width % 128)))
    early = lax.all_to_all(early, ALL, split_axis=0, concat_axis=0, tiled=True)
    early = jnp.sum(early.astype(F32), axis=0)
    cent_rows = NCENT // devices
    at = cent_rows * DC
    centroid_sums = early[:at].reshape(cent_rows, DC)
    head_reduced = early[at : at + head_rows * DC].reshape(head_rows, DC)
    at += head_rows * DC
    centroid_counts = early[at : at + cent_rows] + early[at + cent_rows : at + 2 * cent_rows]
    at += 2 * cent_rows
    loss = (early[at] + early[at + 1] + early[at + 2]) / pair_floor

    grad_hidden_two = contract_cols(grad_proj, head_full)
    grad_sum_two, grad_gain_two, grad_shift_two = norm_back(grad_hidden_two, norm_two, pieces[8])
    grad_two_low = grad_sum_two.astype(BF)
    member_bits, group_bits = bits_of("psg"), bits_of("grp")
    member_first = member_bits + group_bits
    group_first = member_bits[:1] + group_bits[:1] + member_bits[1:] + group_bits[1:]
    down = halve_start(cut_chunks(contract_rows(activated, grad_two_low)), member_first[0])
    grad_activated = contract_cols(grad_two_low, down_rows)
    normal_cdf = 0.5 * (1.0 + lax.erf(inner / math.sqrt(2.0)))
    normal_pdf = jnp.exp(-0.5 * inner * inner) / math.sqrt(2.0 * math.pi)
    grad_inner = (grad_activated * (normal_cdf + inner * normal_pdf)).astype(BF)
    grad_inner, down = gate(grad_inner, down)
    down = halve_start(halve_end(down), member_first[1])
    up = halve_start(cut_chunks(contract_rows(grad_inner, input_one)), group_first[0])
    grad_bias_up = jnp.sum(grad_inner.astype(F32), axis=0)
    grad_hidden_one = grad_sum_two + matmul(grad_inner, up_rows)
    grad_hidden_one, up = gate(grad_hidden_one, up)
    up = halve_start(halve_end(up), group_first[1])
    grad_sum_one, grad_gain_one, grad_shift_one = norm_back(grad_hidden_one, norm_one, pieces[5])
    grad_one_low = grad_sum_one.astype(BF)
    grad_out_rows = contract_rows(grad_one_low, context)
    grad_context = matmul(grad_one_low, attn_rows[3 * D :]).astype(BF)
    grad_context, down = gate(grad_context, down)
    down = halve_start(halve_end(down), member_first[2])
    grad_mixed = attention_backward(segment_column, segment_windows, mixed, grad_context, kept)
    grad_mixed, down, up = gate(grad_mixed, down, up)
    down = halve_start(halve_end(down), member_first[3])
    up = halve_start(halve_end(up), group_first[2])
    grad_qkv_rows = contract_rows(grad_mixed, input_zero)
    attn = halve_start(
        cut_chunks(jnp.concatenate([grad_qkv_rows, grad_out_rows], axis=0)), member_first[0]
    )
    grad_mixed_sum = jnp.sum(grad_mixed.astype(F32), axis=0)
    grad_hidden_zero = grad_sum_one + matmul(grad_mixed, attn_rows[: 3 * D])
    grad_hidden_zero, down, up, attn = gate(grad_hidden_zero, down, up, attn)
    down = halve_start(halve_end(down), member_first[4])
    up = halve_start(halve_end(up), group_first[3])
    attn = halve_start(halve_end(attn), member_first[1])
    grad_embedded, grad_gain_zero, grad_shift_zero = norm_back(
        grad_hidden_zero, norm_zero, pieces[0]
    )

    grad_low = grad_embedded.astype(BF)
    grad_positions = contract_rows(position_hot, grad_low)
    grad_slots = contract_rows(slot_hot, grad_low).astype(BF).reshape(devices, capacity, D)
    grad_small = jnp.concatenate(
        [
            grad_positions.reshape(-1),
            grad_gain_zero,
            grad_shift_zero,
            grad_mixed_sum[:D],
            grad_mixed_sum[2 * D :],
            jnp.sum(grad_sum_one, axis=0),
            grad_gain_one,
            grad_shift_one,
            jnp.sum(grad_sum_two, axis=0),
            grad_gain_two,
            grad_shift_two,
            grad_bias_up,
        ]
    ).reshape(devices, small_size)
    grad_small = jnp.pad(grad_small.astype(BF), ((0, 0), (0, -small_size % D)))
    grad_slots = jnp.concatenate([grad_slots, grad_small.reshape(devices, -1, D)], axis=1)
    grad_slots, down, up = gate(grad_slots, down, up)
    grad_slots = lax.all_to_all(grad_slots, ALL, split_axis=0, concat_axis=0, tiled=True)
    small_reduced = jnp.sum(grad_slots[:, capacity:].astype(F32), axis=0).reshape(-1)[:small_size]
    grad_slots = grad_slots[:, :capacity]
    down = halve_end(down)
    up = halve_end(halve_start(halve_end(up), group_first[4]))
    attn = halve_end(attn)
    for step in member_first[2:]:
        attn = halve_end(halve_start(attn, step))
    for step in member_first[5:]:
        down = halve_end(halve_start(down, step))
    for step in group_first[5:]:
        up = halve_end(halve_start(up, step))
    down_reduced, up_reduced, attn_reduced = down[0], up[0], attn[0]

    def whole_table():
        table = jnp.zeros((shard_rows * devices, D), F32).at[tokens].add(grad_embedded)
        return lax.psum_scatter(table, ALL, scatter_dimension=0, tiled=True)

    def own_rows():
        slots = jnp.arange(capacity, dtype=jnp.int32).astype(F32)
        picked = (asked_rank[:, None, :] == slots[None, :, None]).astype(BF)
        return contract_rows(
            picked.reshape(devices * capacity, shard_rows),
            grad_slots.reshape(devices * capacity, D),
        )

    table_reduced = lax.cond(
        overflow,
        whole_table,
        own_rows,
    )

    count_steps = step_count[0].astype(F32)
    attn_reduced = attn_reduced.T
    up_reduced = up_reduced.T
    table_new, table_second_new = adam_update(
        embed_table, embed_table_moment, embed_table_second, table_reduced, RATE_TABLE, count_steps
    )
    attn_new, attn_second_new = adam_update(
        attention_weight,
        attention_weight_moment,
        attention_weight_second,
        attn_reduced,
        RATE_MATRIX,
        count_steps,
    )
    up_new, up_second_new = adam_update(
        up_weight, up_weight_moment, up_weight_second, up_reduced, RATE_MATRIX, count_steps
    )
    down_new, down_second_new = adam_update(
        down_weight, down_weight_moment, down_weight_second, down_reduced, RATE_MATRIX, count_steps
    )
    head_new, head_second_new = adam_update(
        head_weight, head_weight_moment, head_weight_second, head_reduced, RATE_MATRIX, count_steps
    )
    small_new, small_second_new = adam_update(
        small_params, small_params_moment, small_params_second, small_reduced, RATE_TABLE, count_steps
    )
    return (
        loss,
        centroid_sums,
        centroid_counts,
        table_new,
        table_reduced,
        table_second_new,
        attn_new,
        attn_reduced,
        attn_second_new,
        up_new,
        up_reduced,
        up_second_new,
        down_new,
        down_reduced,
        down_second_new,
        head_new,
        head_reduced,
        head_second_new,
        small_new,
        small_reduced,
        small_second_new,
    )


def solution(mesh):
    in_specs = (
        P(("grp", "psg"), None),
        P(("grp", "psg"), None),
        P(("grp", "psg"), None),
        P(("grp", "psg")),
        P(("grp", "psg"), None),
        P(("grp", "psg"), None),
        P(("grp", "psg"), None),
        P(),
        P(("grp", "psg"), None),
        P(("grp", "psg"), None),
        P(("grp", "psg"), None),
        P(None, ("grp", "psg")),
        P(None, ("grp", "psg")),
        P(None, ("grp", "psg")),
        P(None, ("grp", "psg")),
        P(None, ("grp", "psg")),
        P(None, ("grp", "psg")),
        P(("grp", "psg"), None),
        P(("grp", "psg"), None),
        P(("grp", "psg"), None),
        P(("grp", "psg"), None),
        P(("grp", "psg"), None),
        P(("grp", "psg"), None),
        P(("grp", "psg")),
        P(("grp", "psg")),
        P(("grp", "psg")),
    )
    out_specs = (
        P(),
        P(("grp", "psg"), None),
        P(("grp", "psg")),
        P(("grp", "psg"), None),
        P(("grp", "psg"), None),
        P(("grp", "psg"), None),
        P(None, ("grp", "psg")),
        P(None, ("grp", "psg")),
        P(None, ("grp", "psg")),
        P(None, ("grp", "psg")),
        P(None, ("grp", "psg")),
        P(None, ("grp", "psg")),
        P(("grp", "psg"), None),
        P(("grp", "psg"), None),
        P(("grp", "psg"), None),
        P(("grp", "psg"), None),
        P(("grp", "psg"), None),
        P(("grp", "psg"), None),
        P(("grp", "psg")),
        P(("grp", "psg")),
        P(("grp", "psg")),
    )
    return jax.shard_map(
        on_device, mesh=mesh, in_specs=in_specs, out_specs=out_specs, check_vma=False
    )
```

```python
import math

import jax
import jax.numpy as jnp
from jax import lax
from jax.experimental import pallas as pl
from jax.experimental.pallas import tpu as pltpu
from jax.sharding import PartitionSpec as P

D = 768
HEADS = 12
HD = 64
SEG = 32
PMAX = 64
ROW = 1024
PPD = 32
QDEV = 8
NCENT = 1024
DC = 128
BLK = 128
WIN = 256
ALL = ("grp", "psg")
BF = jnp.bfloat16
F32 = jnp.float32
MARK = 1e30


TEMPER = 0.2
MARGIN = 1.0
NORM_EPS = 1e-06
BETA_ONE = 0.9
BETA_TWO = 0.999
ADAM_EPS = 1e-08
WEIGHT_DECAY = 0.01
RATE_MATRIX = 0.01
RATE_TABLE = 0.1


def matmul(lhs_mat, rhs_mat):
    return jnp.dot(lhs_mat, rhs_mat, preferred_element_type=jnp.float32)


def contract_rows(lhs_mat, rhs_mat):
    return lax.dot_general(
        lhs_mat, rhs_mat, (((0,), (0,)), ((), ())), preferred_element_type=jnp.float32
    )


def contract_cols(lhs_mat, rhs_mat):
    return lax.dot_general(
        lhs_mat, rhs_mat, (((1,), (1,)), ((), ())), preferred_element_type=jnp.float32
    )


def layer_norm(values, scale_gain, shift_bias):
    average = jnp.mean(values, axis=-1, keepdims=True)
    centered = values - average
    inverse = lax.rsqrt(jnp.mean(centered * centered, axis=-1, keepdims=True) + NORM_EPS)
    normed = centered * inverse
    return (normed * (1.0 + scale_gain) + shift_bias, (normed, inverse))


def norm_back(upstream, stored, scale_gain):
    normed, inverse = stored
    scaled = upstream * (1.0 + scale_gain)
    back = inverse * (
        scaled
        - jnp.mean(scaled, axis=-1, keepdims=True)
        - normed * jnp.mean(scaled * normed, axis=-1, keepdims=True)
    )
    return (back, jnp.sum(upstream * normed, axis=0), jnp.sum(upstream, axis=0))


def starts_of(lengths):
    order = jnp.arange(PPD, dtype=jnp.int32)
    before = (order[:, None] > order[None, :]).astype(jnp.int32)
    return jnp.sum(before * lengths[..., None, :], axis=-1)


def layout_of(lengths):
    starts = starts_of(lengths)
    place = jnp.arange(ROW, dtype=jnp.int32)
    above = (place[:, None] >= starts[..., None, :]).astype(jnp.int32)
    segment = jnp.sum(above, axis=-1) - 1
    begin = jnp.max(above * starts[..., None, :], axis=-1)
    return segment, place - begin


def one_hot(index, depth):
    return (index[..., None] == jnp.arange(depth, dtype=jnp.int32)).astype(BF)


def split_two(values):
    high = lax.reduce_precision(values, 8, 7)
    return high.astype(BF), (values - high).astype(BF)


def split_three(values):
    high = lax.reduce_precision(values, 8, 7)
    middle = lax.reduce_precision(values - high, 8, 7)
    return high.astype(BF), middle.astype(BF), (values - high - middle).astype(BF)


def window_start(block, count):
    return min(max(block * BLK - (WIN - BLK) // 2, 0), count - WIN)


def attn_forward_kernel(count, segc_ref, segw_ref, z_ref, o_ref, lse_ref):
    block = pl.program_id(0)
    row = pl.multiple_of(block * BLK, BLK)
    first = pl.multiple_of(jnp.clip(row - (WIN - BLK) // 2, 0, count - WIN), 64)
    allowed = segc_ref[...] == segw_ref[0]
    lane = lax.broadcasted_iota(jnp.int32, (BLK, 2 * HD), 1)
    lane_head = lax.broadcasted_iota(jnp.int32, (BLK, 128), 1)
    kept = jnp.zeros((BLK, 128), F32)
    for pair in range(HEADS // 2):
        at = pair * 2 * HD
        query = z_ref[pl.ds(row, BLK), at : at + 2 * HD] * BF(HD ** (-0.5))
        key = z_ref[pl.ds(first, WIN), D + at : D + at + 2 * HD]
        value = z_ref[pl.ds(first, WIN), 2 * D + at : 2 * D + at + 2 * HD]
        parts = []
        for half in range(2):
            mine = (lane >= half * HD) & (lane < (half + 1) * HD)
            scores = contract_cols(jnp.where(mine, query, BF(0)), key)
            scores = jnp.where(allowed, scores, -1000000000.0)
            top = jnp.max(scores, axis=-1, keepdims=True)
            weight = jnp.exp(scores - top)
            total = jnp.sum(weight, axis=-1, keepdims=True)
            probs = (weight * (1.0 / total)).astype(BF)
            parts.append(matmul(probs, value))
            kept = jnp.where(lane_head == 2 * pair + half, top + jnp.log(total), kept)
        o_ref[:, at : at + 2 * HD] = jnp.where(lane < HD, parts[0], parts[1]).astype(BF)
    lse_ref[...] = kept


def attn_backward_kernel(
    count, blocks, segc_ref, segw_ref, z_ref, do_ref, lse_ref, dz_ref, dk_ref, dv_ref
):
    block = pl.program_id(0)
    row = pl.multiple_of(block * BLK, BLK)
    first = pl.multiple_of(jnp.clip(row - (WIN - BLK) // 2, 0, count - WIN), 64)

    @pl.when(block == 0)
    def _():
        dk_ref[...] = jnp.zeros_like(dk_ref)
        dv_ref[...] = jnp.zeros_like(dv_ref)

    allowed = segc_ref[...] == segw_ref[0]
    lane = lax.broadcasted_iota(jnp.int32, (BLK, 2 * HD), 1)
    kept = lse_ref[...]
    for pair in range(HEADS // 2):
        at = pair * 2 * HD
        query = z_ref[pl.ds(row, BLK), at : at + 2 * HD] * BF(HD ** (-0.5))
        key = z_ref[pl.ds(first, WIN), D + at : D + at + 2 * HD]
        value = z_ref[pl.ds(first, WIN), 2 * D + at : 2 * D + at + 2 * HD]
        upstream = do_ref[:, at : at + 2 * HD]
        grad_query = []
        grad_key = jnp.zeros((WIN, 2 * HD), F32)
        grad_value = jnp.zeros((WIN, 2 * HD), F32)
        for half in range(2):
            mine = (lane >= half * HD) & (lane < (half + 1) * HD)
            query_own = jnp.where(mine, query, BF(0))
            up_own = jnp.where(mine, upstream, BF(0))
            scores = jnp.where(allowed, contract_cols(query_own, key), -1000000000.0)
            probs = jnp.exp(scores - kept[:, 2 * pair + half : 2 * pair + half + 1])
            grad_probs = contract_cols(up_own, value)
            grad_value = grad_value + contract_rows(probs.astype(BF), up_own)
            inner = jnp.sum(grad_probs * probs, axis=-1, keepdims=True)
            grad_scores = (probs * (grad_probs - inner)).astype(BF)
            grad_query.append(matmul(grad_scores, key))
            grad_key = grad_key + contract_rows(grad_scores, query_own)
        own = jnp.where(lane < HD, grad_query[0], grad_query[1]) * HD ** (-0.5)
        dz_ref[pl.ds(row, BLK), at : at + 2 * HD] = own.astype(BF)
        dk_ref[pl.ds(first, WIN), at : at + 2 * HD] += grad_key
        dv_ref[pl.ds(first, WIN), at : at + 2 * HD] += grad_value

    @pl.when(block == blocks - 1)
    def _():
        dz_ref[:, D : 2 * D] = dk_ref[...].astype(BF)
        dz_ref[:, 2 * D :] = dv_ref[...].astype(BF)


def attention_specs(count):
    return [
        pl.BlockSpec((BLK, 1), lambda i: (i, 0)),
        pl.BlockSpec((1, 1, WIN), lambda i: (i, 0, 0)),
        pl.BlockSpec((count, 3 * D), lambda i: (0, 0)),
    ]


def attention_forward(segment_column, segment_windows, mixed):
    count = mixed.shape[0]
    blocks = count // BLK
    return pl.pallas_call(
        lambda *refs: attn_forward_kernel(count, *refs),
        grid=(blocks,),
        in_specs=attention_specs(count),
        out_specs=[
            pl.BlockSpec((BLK, D), lambda i: (i, 0)),
            pl.BlockSpec((BLK, 128), lambda i: (i, 0)),
        ],
        out_shape=[
            jax.ShapeDtypeStruct((count, D), BF),
            jax.ShapeDtypeStruct((count, 128), F32),
        ],
        compiler_params=pltpu.CompilerParams(vmem_limit_bytes=40 * 2**20),
        cost_estimate=pl.CostEstimate(
            flops=4 * count * WIN * 128 * HEADS, bytes_accessed=12000000, transcendentals=0
        ),
    )(segment_column, segment_windows, mixed)


def attention_backward(segment_column, segment_windows, mixed, upstream, kept):
    count = mixed.shape[0]
    blocks = count // BLK
    return pl.pallas_call(
        lambda *refs: attn_backward_kernel(count, blocks, *refs),
        grid=(blocks,),
        in_specs=attention_specs(count)
        + [
            pl.BlockSpec((BLK, D), lambda i: (i, 0)),
            pl.BlockSpec((BLK, 128), lambda i: (i, 0)),
        ],
        out_specs=pl.BlockSpec((count, 3 * D), lambda i: (0, 0)),
        out_shape=jax.ShapeDtypeStruct((count, 3 * D), BF),
        scratch_shapes=[pltpu.VMEM((count, D), F32), pltpu.VMEM((count, D), F32)],
        compiler_params=pltpu.CompilerParams(vmem_limit_bytes=56 * 2**20),
        cost_estimate=pl.CostEstimate(
            flops=10 * count * WIN * 128 * HEADS, bytes_accessed=18000000, transcendentals=0
        ),
    )(segment_column, segment_windows, mixed, upstream, kept)


def place_of():
    return lax.axis_index("grp") * lax.axis_size("psg") + lax.axis_index("psg")


def mesh_place(place):
    members = lax.axis_size("psg")
    return (place // members, place % members)


def flipped(place, mask):
    result, bit = place, 0
    while mask >> bit:
        if (mask >> bit) & 1:
            result = result + (1 - 2 * ((place // (1 << bit)) % 2)) * (1 << bit)
        bit += 1
    return result


def greet_all(devices, me):
    barrier = pltpu.get_barrier_semaphore()

    @pl.loop(1, devices)
    def _(i):
        pl.semaphore_signal(
            barrier,
            inc=1,
            device_id=mesh_place((me + i) % devices),
            device_id_type=pl.DeviceIdType.MESH,
        )

    pl.semaphore_wait(barrier, devices - 1)


def gather_plan(order, group):
    held, steps = [0], []
    for bit in order:
        fresh = [(1 << bit) | m for m in held]
        steps.append([fresh[i : i + group] for i in range(0, len(fresh), group)])
        held = held + fresh
    return steps


def pack_rows(asked, table, rank_ref, packed_ref):
    devices, capacity, _ = packed_ref.shape
    width = table.shape[0]
    asked = jnp.concatenate([asked[:, j, :] for j in range(width // 128)], axis=1)
    above = lax.broadcasted_iota(jnp.int32, (width, width), 0)
    earlier = (above < lax.broadcasted_iota(jnp.int32, (width, width), 1)).astype(F32).astype(BF)
    rank_ref[...] = jnp.where(asked > 0.5, matmul(asked.astype(BF), earlier), -1.0)
    most = jnp.max(jnp.sum(asked, axis=1, keepdims=True), axis=0, keepdims=True)
    together = 8

    @pl.loop(0, devices // together)
    def _(i):
        rank = rank_ref[pl.ds(pl.multiple_of(i * together, together), together), :]
        slot = lax.broadcasted_iota(jnp.int32, (together, capacity, width), 1).astype(F32)
        picked = jnp.where(rank[:, None, :] == slot, 1.0, 0.0)
        picked = picked.reshape(together * capacity, width).astype(BF)
        rows = matmul(picked, table[...]).reshape(together, capacity, D)
        place = lax.broadcasted_iota(jnp.int32, (together, capacity, D), 1)
        rows = jnp.where((place == capacity - 1) & (most > capacity)[:, :, None], MARK, rows)
        packed_ref[pl.ds(i * together, together)] = rows.astype(BF)


def gather_kernel(devices, pieces, *refs):
    matrices = 3
    sources, (needed, notes, table) = refs[:matrices], refs[matrices : matrices + 3]
    outs, (notes_out, rows_out, rank) = refs[6:9], refs[9:12]
    asked, packed, arrive, beside, leave, local, notes_sem, ask_sem, rows_sem = refs[12:]
    me = place_of()
    group = max(devices // 8, 1)
    greet_all(devices, me)

    def push(source, target_ref, target, send, recv):
        pltpu.make_async_remote_copy(
            src_ref=source,
            dst_ref=target_ref,
            send_sem=send,
            recv_sem=recv,
            device_id=mesh_place(target),
            device_id_type=pl.DeviceIdType.MESH,
        ).start()

    def settle(some, semaphore):
        pltpu.make_async_copy(some, some, semaphore).wait()

    @pl.loop(1, devices)
    def _(i):
        target = (me + i) % devices
        push(needed.at[target], asked.at[me], target, ask_sem.at[0], ask_sem.at[1])

    def start(piece, mask, target, semaphore):
        which, first, rows, _ = pieces[piece]
        there = outs[which].at[flipped(me, mask), pl.ds(first, rows)]
        here = sources[which].at[pl.ds(first, rows)] if mask == 0 else there
        push(here, there, flipped(me, target), leave.at[piece], semaphore)

    def wait(piece, blocks, semaphore):
        which, first, rows, _ = pieces[piece]
        settle(outs[which].at[pl.ds(0, blocks), pl.ds(first, rows)], semaphore)

    plans, numbers = [], []
    for piece in range(len(pieces)):
        plan = gather_plan(pieces[piece][3], group)
        number, count = {}, 0
        for groups in plan:
            for masks in groups:
                for mask in masks:
                    number[mask] = count
                count += 1
        plans.append(plan)
        numbers.append(number)

    def send_on(piece, mask, after):
        order = pieces[piece][3]
        for step in range(after + 1, len(order)):
            target = 1 << order[step]
            start(piece, mask, target, arrive.at[piece, numbers[piece][mask | target]])
        start(piece, mask, 1, beside.at[piece])

    def pass_on(piece, step):
        for masks in plans[piece][step]:
            wait(piece, len(masks), arrive.at[piece, numbers[piece][masks[0]]])
            for mask in masks:
                send_on(piece, mask, step)

    for piece in range(len(pieces)):
        send_on(piece, 0, -1)

    @pl.loop(1, devices)
    def _(i):
        target = (me + i) % devices
        push(notes, notes_out.at[me], target, notes_sem.at[0], notes_sem.at[1])

    own = [
        pltpu.make_async_copy(source, out.at[me], local.at[i])
        for i, (source, out) in enumerate(zip(sources, outs))
    ]
    own.append(pltpu.make_async_copy(notes, notes_out.at[me], local.at[matrices]))
    own_asked = pltpu.make_async_copy(needed.at[me], asked.at[me], local.at[matrices + 1])
    for copy in own:
        copy.start()
    own_asked.start()
    for piece in range(len(pieces)):
        pass_on(piece, 0)
    own_asked.wait()
    for i in range(2):
        settle(asked.at[pl.ds(0, devices - 1)], ask_sem.at[i])
    pack_rows(asked[...], table, rank, packed)

    masks = sorted(range(1, devices), key=lambda m: -bin(m).count("1"))
    steps = len(pieces[0][3])
    each = -(-(devices - 1) // (len(pieces) * (steps - 1)))
    kept_rows = pltpu.make_async_copy(packed.at[me], rows_out.at[me], local.at[matrices + 2])
    kept_rows.start()
    for step in range(1, steps):
        for piece in range(len(pieces)):
            pass_on(piece, step)
            now, masks = masks[:each], masks[each:]
            for mask in now:
                target = flipped(me, mask)
                push(packed.at[target], rows_out.at[me], target, rows_sem.at[0], rows_sem.at[1])
    for piece in range(len(pieces)):
        wait(piece, devices // 2, beside.at[piece])
        wait(piece, devices - 1, leave.at[piece])
    for copy in own:
        copy.wait()
    kept_rows.wait()
    for i in range(2):
        settle(notes_out.at[pl.ds(0, devices - 1)], notes_sem.at[i])
        settle(rows_out.at[pl.ds(0, devices - 1)], rows_sem.at[i])


def gather_all(sources, needed, notes, table, capacity):
    devices = needed.shape[0]
    rows = sources[0].shape[0]
    bits = devices.bit_length() - 1
    high = list(range(3, bits))[::-1]
    one, other = (*high, 2, 1), (*high, 1, 2)
    cut = rows // 32 * 16
    pieces = [(0, 0, rows, one), (2, 0, rows, other), (1, cut, rows - cut, one)]
    if cut:
        pieces.append((1, 0, cut, other))
    count = max(sum(map(len, gather_plan(p[3], max(devices // 8, 1)))) for p in pieces)
    anywhere = pl.BlockSpec(memory_space=pl.ANY)
    inside = pl.BlockSpec(memory_space=pltpu.VMEM)
    dma = pltpu.SemaphoreType.DMA
    *gathered, noted, arrived, rank = pl.pallas_call(
        lambda *refs: gather_kernel(devices, pieces, *refs),
        in_specs=[anywhere] * 3 + [inside] * 3,
        out_specs=[anywhere] * 5 + [inside],
        out_shape=[jax.ShapeDtypeStruct((devices, *s.shape), s.dtype) for s in (*sources, notes)]
        + [
            jax.ShapeDtypeStruct((devices, capacity, D), BF),
            jax.ShapeDtypeStruct((devices, table.shape[0]), F32),
        ],
        scratch_shapes=[
            pltpu.VMEM(needed.shape, F32),
            pltpu.VMEM((devices, capacity, D), BF),
            dma((len(pieces), count)),
            dma((len(pieces),)),
            dma((len(pieces),)),
            dma((6,)),
            dma((2,)),
            dma((2,)),
            dma((2,)),
        ],
        compiler_params=pltpu.CompilerParams(
            collective_id=0, has_side_effects=True, vmem_limit_bytes=48 * 2**20
        ),
    )(*sources, needed, notes, table)
    return gathered, noted, arrived, rank


def reduce_plan(order, group):
    held = [0]
    for bit in reversed(order):
        held = [m | (1 << bit) for m in held] + held
    steps = []
    for step in range(len(order) + 1):
        if step:
            held = [m for m in held if not (m >> order[step - 1]) & 1]
        steps.append([held[i : i + group] for i in range(0, len(held), group)])
    return steps


def reduce_kernel(devices, pieces, spread, *refs):
    count = len({p[0] for p in pieces})
    sources, rows_in = refs[:count], refs[count]
    outs, rows_out = refs[count + 1 : 2 * count + 1], refs[2 * count + 1]
    held, landed = refs[2 * count + 2 : 3 * count + 2], refs[3 * count + 2 : 4 * count + 2]
    arrive, leave, load, rows_sem, own_sem = refs[4 * count + 2 :]
    me = place_of()
    group = max(devices // 16, 1)
    greet_all(devices, me)

    def push(source, target_ref, target, send, recv):
        pltpu.make_async_remote_copy(
            src_ref=source,
            dst_ref=target_ref,
            send_sem=send,
            recv_sem=recv,
            device_id=mesh_place(target),
            device_id_type=pl.DeviceIdType.MESH,
        ).start()

    def settle(some, semaphore):
        pltpu.make_async_copy(some, some, semaphore).wait()

    plans, slots, places, numbers = [], [], [], []
    for piece in pieces:
        plan = reduce_plan(piece[3], group)
        slots.append({m: i for i, m in enumerate(sum(plan[0], []))})
        place, number, at, count = {}, {}, 0, 0
        for step, groups in enumerate(plan):
            for masks in groups:
                for mask in masks:
                    place[step, mask], number[step, mask] = at, count
                    at += 1
                count += 1
        plans.append(plan)
        places.append(place)
        numbers.append(number)

    def rows_of(piece):
        return pl.ds(pieces[piece][1], pieces[piece][2])

    def send(piece, step, mask, bit, source):
        which = pieces[piece][0]
        kept = mask & ~(1 << bit)
        push(
            source,
            landed[which].at[places[piece][step, kept], rows_of(piece)],
            flipped(me, 1 << bit),
            leave.at[piece],
            arrive.at[piece, numbers[piece][step, kept]],
        )

    order = sorted(range(1, devices), key=lambda m: -bin(m).count("1"))

    def send_rows(amount):
        for _ in range(min(amount, len(order))):
            target = flipped(me, order.pop(0))
            push(rows_in.at[target], rows_out.at[me], target, rows_sem.at[0], rows_sem.at[1])

    own_rows = pltpu.make_async_copy(rows_in.at[me], rows_out.at[me], own_sem)
    own_rows.start()
    send_rows(spread[0])
    for masks in plans[0][0]:
        for piece in range(len(pieces)):
            which = pieces[piece][0]
            for mask in plans[piece][0][plans[0][0].index(masks)]:
                source = sources[which].at[flipped(me, mask | 1), rows_of(piece)]
                send(piece, 0, mask | 1, 0, source)
    for piece in range(len(pieces)):
        which = pieces[piece][0]
        for mask in slots[piece]:
            pltpu.make_async_copy(
                sources[which].at[flipped(me, mask), rows_of(piece)],
                held[which].at[slots[piece][mask], rows_of(piece)],
                load.at[piece],
            ).start()
    turn = 1
    for step in range(len(pieces[0][3]) + 1):
        for at in range(len(plans[0][step])):
            for piece in range(len(pieces)):
                which, _, _, bits = pieces[piece]
                rows = rows_of(piece)
                if step == 0 and at == 0:
                    settle(held[which].at[pl.ds(0, devices // 2), rows], load.at[piece])
                masks = plans[piece][step][at]
                some = landed[which].at[pl.ds(0, len(masks)), rows]
                settle(some, arrive.at[piece, numbers[piece][step, masks[0]]])
                for mask in masks:
                    slot = slots[piece][mask]
                    total = held[which][slot, rows].astype(F32)
                    total = total + landed[which][places[piece][step, mask], rows].astype(F32)
                    if step == len(bits):
                        outs[which][rows] = total
                        continue
                    held[which][slot, rows] = total.astype(held[which].dtype)
                    if (mask >> bits[step]) & 1:
                        send(piece, step + 1, mask, bits[step], held[which].at[slot, rows])
            send_rows(spread[turn] if turn < len(spread) else 0)
            turn += 1
    send_rows(devices)
    for piece in range(len(pieces)):
        which = pieces[piece][0]
        settle(landed[which].at[pl.ds(0, devices - 1), rows_of(piece)], leave.at[piece])
    own_rows.wait()
    for i in range(2):
        settle(rows_out.at[pl.ds(0, devices - 1)], rows_sem.at[i])


def reduce_all(sources, rows_in):
    devices = rows_in.shape[0]
    bits = devices.bit_length() - 1
    high = list(range(3, bits))
    one, other = (1, 2, *high), (2, 1, *high)
    pieces = []
    for i in (0, 2, 1, 3, 4):
        rows = sources[i].shape[1]
        cut = rows // 32 * 16 if i == 1 else 0
        pieces.append((i, cut, rows - cut, one if i in (0, 1, 3) else other))
        if cut:
            pieces.append((i, 0, cut, other))
    spread = [6] + [2] * devices
    count = max(sum(map(len, reduce_plan(p[3], max(devices // 16, 1)))) for p in pieces)
    anywhere = pl.BlockSpec(memory_space=pl.ANY)
    inside = pl.BlockSpec(memory_space=pltpu.VMEM)
    dma = pltpu.SemaphoreType.DMA
    *reduced, arrived = pl.pallas_call(
        lambda *refs: reduce_kernel(devices, pieces, spread, *refs),
        in_specs=[anywhere] * (len(sources) + 1),
        out_specs=[inside] * len(sources) + [anywhere],
        out_shape=[jax.ShapeDtypeStruct(s.shape[1:], F32) for s in sources]
        + [jax.ShapeDtypeStruct(rows_in.shape, rows_in.dtype)],
        scratch_shapes=[pltpu.VMEM((devices // 2, *s.shape[1:]), s.dtype) for s in sources]
        + [pltpu.VMEM((devices - 1, *s.shape[1:]), s.dtype) for s in sources]
        + [dma((len(pieces), count)), dma((len(pieces),)), dma((len(pieces),)), dma((2,)), dma],
        compiler_params=pltpu.CompilerParams(
            collective_id=1, has_side_effects=True, vmem_limit_bytes=48 * 2**20
        ),
    )(*sources, rows_in)
    return reduced, arrived


def adam_update(weight, moment, second, gradient, rate, count_steps):
    moment_new = BETA_ONE * moment + (1.0 - BETA_ONE) * gradient
    second_new = BETA_TWO * second + (1.0 - BETA_TWO) * gradient * gradient
    corrected = moment_new / (1.0 - BETA_ONE**count_steps)
    scaled = second_new / (1.0 - BETA_TWO**count_steps)
    weight_new = weight - rate * (corrected / (jnp.sqrt(scaled) + ADAM_EPS) + WEIGHT_DECAY * weight)
    return (weight_new, second_new)


def on_device(
    query_ids,
    passage_ids,
    passage_lengths,
    positives,
    negatives,
    pair_mask,
    assignments,
    step_count,
    embed_table,
    embed_table_moment,
    embed_table_second,
    attention_weight,
    attention_weight_moment,
    attention_weight_second,
    up_weight,
    up_weight_moment,
    up_weight_second,
    down_weight,
    down_weight_moment,
    down_weight_second,
    head_weight,
    head_weight_moment,
    head_weight_second,
    small_params,
    small_params_moment,
    small_params_second,
):
    devices = lax.axis_size("grp") * lax.axis_size("psg")
    members = lax.axis_size("psg")
    member = lax.axis_index("psg")
    group = lax.axis_index("grp")
    shard_rows = embed_table.shape[0]
    queries = query_ids.shape[0]
    negative_count = negatives.shape[1]
    query_rows = queries * SEG
    count = ROW + query_rows
    capacity = 16 * ((count // devices + 8 + 15) // 16)
    small_size = small_params.shape[0]
    head_rows = head_weight.shape[0]
    mask_float = pair_mask.astype(F32)

    tokens = jnp.concatenate([passage_ids.reshape(-1), query_ids.reshape(-1)])
    passage_segment, passage_position = layout_of(passage_lengths[0])
    query_place = jnp.arange(query_rows, dtype=jnp.int32)
    segment = jnp.concatenate([passage_segment, PPD + query_place // SEG])
    position = jnp.concatenate([passage_position, query_place % SEG])
    segment_column = segment[:, None]
    segment_windows = jnp.stack(
        [
            segment[window_start(i, count) : window_start(i, count) + WIN][None]
            for i in range(count // BLK)
        ]
    )

    def shard_of(rows):
        return jnp.pad(rows.astype(BF), ((0, -rows.shape[0] % 16), (0, 0)))

    matrix_rows = down_weight.shape[0]
    shards = [shard_of(attention_weight.T), shard_of(up_weight.T), shard_of(down_weight)]

    owner = tokens // shard_rows
    local_row = tokens - owner * shard_rows
    owner_hot = one_hot(owner, devices)
    row_hot = one_hot(local_row, shard_rows)
    needed = jnp.minimum(contract_rows(owner_hot, row_hot), 1.0)
    width = -(-shard_rows // 1024) * 1024
    table = jnp.pad(embed_table.astype(BF), ((0, width - shard_rows), (0, 0)))
    notes = jnp.concatenate(
        [
            v.reshape(-1).astype(BF)
            for v in (small_params, head_weight, passage_lengths, jnp.sum(mask_float))
        ]
    )
    notes = jnp.pad(notes, (0, -notes.size % 2048)).reshape(-1, 128)
    gathered, noted, packed, asked_rank = gather_all(
        shards,
        jnp.pad(needed, ((0, 0), (0, width - shard_rows))).reshape(devices, width // 128, 128),
        notes,
        table,
        capacity,
    )
    asked_rank = asked_rank[:, :shard_rows]
    attn_rows, up_rows, down_rows = (g[:, :matrix_rows].reshape(-1, D) for g in gathered)
    noted = noted.reshape(devices, -1)
    cut = [0, small_size, head_rows * DC, PPD, 1]
    for i in range(1, len(cut)):
        cut[i] += cut[i - 1]
    small_all, head_all, lengths_all, pairs_all = (noted[:, cut[i] : cut[i + 1]] for i in range(4))
    small_all = small_all.reshape(-1)
    head_full = head_all.reshape(D, DC)
    pair_floor = jnp.maximum(jnp.sum(pairs_all.astype(F32)), 1.0)
    place_row = jnp.arange(shard_rows, dtype=jnp.int32)
    earlier = (place_row[:, None] < place_row[None, :]).astype(BF)
    overflow = jnp.max(packed[:, capacity - 1, :].astype(F32)) > 0.5 * MARK
    packed = packed.reshape(devices * capacity, D)
    needed_rank = jnp.minimum(matmul(needed.astype(BF), earlier), 255.0)
    token_rank = jnp.sum(matmul(owner_hot, needed_rank.astype(BF)) * row_hot.astype(F32), axis=1)
    slot = owner * capacity + jnp.minimum(token_rank.astype(jnp.int32), capacity - 1)
    slot_hot = one_hot(slot, devices * capacity)
    looked_up = lax.cond(
        overflow,
        lambda: lax.all_gather(embed_table.astype(BF), ALL, axis=0, tiled=True)[tokens].astype(F32),
        lambda: matmul(slot_hot, packed),
    )

    positions = small_all[: PMAX * D].reshape(PMAX, D)
    remainder = small_all[PMAX * D :].astype(F32)
    pieces = [remainder[i * D : (i + 1) * D] for i in range(10)]
    bias_up = remainder[10 * D :]
    position_hot = one_hot(position, PMAX)
    embedded = looked_up + matmul(position_hot, positions)
    hidden_zero, norm_zero = layer_norm(embedded, pieces[0], pieces[1])
    input_zero = hidden_zero.astype(BF)
    bias_mixed = jnp.concatenate([pieces[2], jnp.zeros((D,), F32), pieces[3]])
    mixed = (contract_cols(input_zero, attn_rows[: 3 * D]) + bias_mixed).astype(BF)
    context, kept = attention_forward(segment_column, segment_windows, mixed)
    hidden_one, norm_one = layer_norm(
        hidden_zero + contract_cols(context, attn_rows[3 * D :]) + pieces[4], pieces[5], pieces[6]
    )
    input_one = hidden_one.astype(BF)
    inner = contract_cols(input_one, up_rows) + bias_up
    activated = (0.5 * inner * (1.0 + lax.erf(inner / math.sqrt(2.0)))).astype(BF)
    hidden_two, norm_two = layer_norm(
        hidden_one + matmul(activated, down_rows) + pieces[7], pieces[8], pieces[9]
    )
    input_two = hidden_two.astype(BF)
    projected = matmul(input_two, head_full)
    scale_inverse = lax.rsqrt(jnp.sum(projected * projected, axis=-1, keepdims=True) + NORM_EPS)
    unit = projected * scale_inverse
    unit_low = unit.astype(BF)

    units = lax.all_gather(unit_low, "psg", axis=0)
    group_passage = units[:, :ROW]
    group_query = units[:, ROW:].reshape(members * query_rows, DC)
    own_query = unit_low[ROW:]
    own_passage = unit_low[:ROW]
    group_lengths = lax.dynamic_slice_in_dim(lengths_all, group * members, members, 0)
    group_segment, _ = layout_of(group_lengths.astype(jnp.int32))
    group_hot = one_hot(group_segment, PPD)
    passage_hot = one_hot(passage_segment, PPD)

    weighted_own = jnp.exp(
        jnp.einsum("qd,mtd->mqt", own_query, group_passage, preferred_element_type=F32) / TEMPER
    )
    sum_own = lambda part: jnp.einsum(
        "mqt,mtp->mqp", part, group_hot, preferred_element_type=F32
    )
    high, low = split_two(weighted_own)
    totals_own = sum_own(high) + sum_own(low)
    weighted = jnp.exp(contract_cols(group_query, own_passage) / TEMPER)
    high, low = split_two(weighted)
    totals = matmul(high, passage_hot) + matmul(low, passage_hot)
    own_scores = jnp.sum(
        (TEMPER * jnp.log(totals_own)).reshape(members, queries, SEG, PPD), axis=2
    )
    own_scores = own_scores.transpose(1, 0, 2).reshape(queries, members * PPD)
    columns = jnp.arange(members * PPD, dtype=jnp.int32)
    pick_positive = (positives[:, None] == columns[None, :]).astype(F32)
    pick_negative = (negatives[:, :, None] == columns[None, None, :]).astype(F32)
    pos_score = jnp.sum(own_scores * pick_positive, axis=1)
    neg_score = jnp.sum(pick_negative * own_scores[:, None, :], axis=2)
    margins = MARGIN - pos_score[:, None] + neg_score
    numerator = jnp.sum(mask_float * jax.nn.softplus(margins))
    factor = mask_float * jax.nn.sigmoid(margins) / pair_floor
    grad_own = (
        jnp.sum(factor[:, :, None] * pick_negative, axis=1)
        - jnp.sum(factor, axis=1)[:, None] * pick_positive
    )
    grad_group = lax.all_gather(grad_own, "psg", axis=0, tiled=True)
    grad_local = lax.dynamic_slice_in_dim(grad_group, member * PPD, PPD, 1)

    grad_own_split = grad_own.reshape(queries, 1, members, PPD).transpose(2, 0, 1, 3)
    ratio_own = (
        (TEMPER * grad_own_split) / totals_own.reshape(members, queries, SEG, PPD)
    ).reshape(members, query_rows, PPD)
    spread_own = jnp.einsum(
        "mqp,mtp->mqt", ratio_own.astype(BF), group_hot, preferred_element_type=F32
    )
    sims_own = (spread_own * weighted_own / TEMPER).astype(BF)
    grad_unit_query = jnp.einsum(
        "mqt,mtd->qd", sims_own, group_passage, preferred_element_type=F32
    )
    ratio = (
        (TEMPER * grad_local[:, None, :]) / totals.reshape(members * queries, SEG, PPD)
    ).reshape(members * query_rows, PPD)
    sims = (contract_cols(ratio.astype(BF), passage_hot) * weighted / TEMPER).astype(BF)
    grad_unit_passage = contract_rows(sims, group_query)
    grad_unit = jnp.concatenate([grad_unit_passage, grad_unit_query])

    grad_proj = (
        (grad_unit - unit * jnp.sum(grad_unit * unit, axis=-1, keepdims=True)) * scale_inverse
    ).astype(BF)
    grad_head = contract_rows(input_two, grad_proj)
    picks = one_hot(assignments[0], NCENT)
    centroid_part = contract_rows(picks, own_passage)
    count_part = jnp.sum(picks.astype(F32), axis=0)

    grad_hidden_two = contract_cols(grad_proj, head_full)
    grad_sum_two, grad_gain_two, grad_shift_two = norm_back(grad_hidden_two, norm_two, pieces[8])
    grad_two_low = grad_sum_two.astype(BF)
    grad_down_rows = contract_rows(activated, grad_two_low)
    grad_activated = contract_cols(grad_two_low, down_rows)
    normal_cdf = 0.5 * (1.0 + lax.erf(inner / math.sqrt(2.0)))
    normal_pdf = jnp.exp(-0.5 * inner * inner) / math.sqrt(2.0 * math.pi)
    grad_inner = (grad_activated * (normal_cdf + inner * normal_pdf)).astype(BF)
    grad_up_rows = contract_rows(grad_inner, input_one)
    grad_bias_up = jnp.sum(grad_inner.astype(F32), axis=0)
    grad_hidden_one = grad_sum_two + matmul(grad_inner, up_rows)
    grad_sum_one, grad_gain_one, grad_shift_one = norm_back(grad_hidden_one, norm_one, pieces[5])
    grad_one_low = grad_sum_one.astype(BF)
    grad_out_rows = contract_rows(grad_one_low, context)
    grad_context = matmul(grad_one_low, attn_rows[3 * D :]).astype(BF)
    grad_mixed = attention_backward(segment_column, segment_windows, mixed, grad_context, kept)
    grad_qkv_rows = contract_rows(grad_mixed, input_zero)
    grad_mixed_sum = jnp.sum(grad_mixed.astype(F32), axis=0)
    grad_hidden_zero = grad_sum_one + matmul(grad_mixed, attn_rows[: 3 * D])
    grad_embedded, grad_gain_zero, grad_shift_zero = norm_back(
        grad_hidden_zero, norm_zero, pieces[0]
    )
    grad_low = grad_embedded.astype(BF)
    grad_positions = contract_rows(position_hot, grad_low)
    grad_slots = contract_rows(slot_hot, grad_low).astype(BF).reshape(devices, capacity, D)
    grad_small = jnp.concatenate(
        [
            grad_positions.reshape(-1),
            grad_gain_zero,
            grad_shift_zero,
            grad_mixed_sum[:D],
            grad_mixed_sum[2 * D :],
            jnp.sum(grad_sum_one, axis=0),
            grad_gain_one,
            grad_shift_one,
            jnp.sum(grad_sum_two, axis=0),
            grad_gain_two,
            grad_shift_two,
            grad_bias_up,
        ]
    )

    def chunks(rows):
        rows = rows.astype(BF).reshape(devices, matrix_rows, D)
        return jnp.pad(rows, ((0, 0), (0, -matrix_rows % 16), (0, 0)))

    def side_by_side(parts, sublanes):
        joined = jnp.concatenate([p.reshape(devices, -1) for p in parts], axis=1)
        joined = jnp.pad(joined, ((0, 0), (0, -joined.shape[1] % (sublanes * 128))))
        return joined.reshape(devices, -1, 128)

    reduced, grad_slots = reduce_all(
        [
            chunks(jnp.concatenate([grad_qkv_rows.astype(BF), grad_out_rows.astype(BF)])),
            chunks(grad_up_rows),
            chunks(grad_down_rows),
            side_by_side([centroid_part.astype(BF), grad_head.astype(BF)], 16),
            side_by_side(
                [grad_small, count_part, jnp.broadcast_to(numerator, (devices, 1))], 8
            ),
        ],
        grad_slots,
    )
    attn_reduced, up_reduced, down_reduced = (r[:matrix_rows] for r in reduced[:3])
    wide, fine = reduced[3].reshape(-1), reduced[4].reshape(-1)
    centroid_rows = NCENT // devices
    centroid_sums = wide[: centroid_rows * DC].reshape(centroid_rows, DC)
    head_reduced = wide[centroid_rows * DC :][: head_rows * DC].reshape(head_rows, DC)
    small_reduced = fine[:small_size]
    centroid_counts = fine[small_size:][:centroid_rows]
    loss = fine[small_size + centroid_rows] / pair_floor

    def whole_table():
        table = jnp.zeros((shard_rows * devices, D), F32).at[tokens].add(grad_embedded)
        return lax.psum_scatter(table, ALL, scatter_dimension=0, tiled=True)

    def own_rows():
        slots = jnp.arange(capacity, dtype=jnp.int32).astype(F32)
        picked = (asked_rank[:, None, :] == slots[None, :, None]).astype(BF)
        return contract_rows(
            picked.reshape(devices * capacity, shard_rows),
            grad_slots.reshape(devices * capacity, D),
        )

    table_reduced = lax.cond(
        overflow,
        whole_table,
        own_rows,
    )

    count_steps = step_count[0].astype(F32)
    attn_reduced = attn_reduced.T
    up_reduced = up_reduced.T
    table_new, table_second_new = adam_update(
        embed_table, embed_table_moment, embed_table_second, table_reduced, RATE_TABLE, count_steps
    )
    attn_new, attn_second_new = adam_update(
        attention_weight,
        attention_weight_moment,
        attention_weight_second,
        attn_reduced,
        RATE_MATRIX,
        count_steps,
    )
    up_new, up_second_new = adam_update(
        up_weight, up_weight_moment, up_weight_second, up_reduced, RATE_MATRIX, count_steps
    )
    down_new, down_second_new = adam_update(
        down_weight, down_weight_moment, down_weight_second, down_reduced, RATE_MATRIX, count_steps
    )
    head_new, head_second_new = adam_update(
        head_weight, head_weight_moment, head_weight_second, head_reduced, RATE_MATRIX, count_steps
    )
    small_new, small_second_new = adam_update(
        small_params, small_params_moment, small_params_second, small_reduced, RATE_TABLE, count_steps
    )
    return (
        loss,
        centroid_sums,
        centroid_counts,
        table_new,
        table_reduced,
        table_second_new,
        attn_new,
        attn_reduced,
        attn_second_new,
        up_new,
        up_reduced,
        up_second_new,
        down_new,
        down_reduced,
        down_second_new,
        head_new,
        head_reduced,
        head_second_new,
        small_new,
        small_reduced,
        small_second_new,
    )


def solution(mesh):
    in_specs = (
        P(("grp", "psg"), None),
        P(("grp", "psg"), None),
        P(("grp", "psg"), None),
        P(("grp", "psg")),
        P(("grp", "psg"), None),
        P(("grp", "psg"), None),
        P(("grp", "psg"), None),
        P(),
        P(("grp", "psg"), None),
        P(("grp", "psg"), None),
        P(("grp", "psg"), None),
        P(None, ("grp", "psg")),
        P(None, ("grp", "psg")),
        P(None, ("grp", "psg")),
        P(None, ("grp", "psg")),
        P(None, ("grp", "psg")),
        P(None, ("grp", "psg")),
        P(("grp", "psg"), None),
        P(("grp", "psg"), None),
        P(("grp", "psg"), None),
        P(("grp", "psg"), None),
        P(("grp", "psg"), None),
        P(("grp", "psg"), None),
        P(("grp", "psg")),
        P(("grp", "psg")),
        P(("grp", "psg")),
    )
    out_specs = (
        P(),
        P(("grp", "psg"), None),
        P(("grp", "psg")),
        P(("grp", "psg"), None),
        P(("grp", "psg"), None),
        P(("grp", "psg"), None),
        P(None, ("grp", "psg")),
        P(None, ("grp", "psg")),
        P(None, ("grp", "psg")),
        P(None, ("grp", "psg")),
        P(None, ("grp", "psg")),
        P(None, ("grp", "psg")),
        P(("grp", "psg"), None),
        P(("grp", "psg"), None),
        P(("grp", "psg"), None),
        P(("grp", "psg"), None),
        P(("grp", "psg"), None),
        P(("grp", "psg"), None),
        P(("grp", "psg")),
        P(("grp", "psg")),
        P(("grp", "psg")),
    )
    return jax.shard_map(
        on_device, mesh=mesh, in_specs=in_specs, out_specs=out_specs, check_vma=False
    )
```

```python
import math

import jax
import jax.numpy as jnp
from jax import lax
from jax.experimental import pallas as pl
from jax.experimental.pallas import tpu as pltpu
from jax.sharding import PartitionSpec as P

D = 768
HEADS = 12
HD = 64
SEG = 32
PMAX = 64
ROW = 1024
PPD = 32
QDEV = 8
NCENT = 1024
DC = 128
BLK = 128
WIN = 256
ALL = ("grp", "psg")
BF = jnp.bfloat16
F32 = jnp.float32
MARK = 1e30


TEMPER = 0.2
MARGIN = 1.0
NORM_EPS = 1e-06
BETA_ONE = 0.9
BETA_TWO = 0.999
ADAM_EPS = 1e-08
WEIGHT_DECAY = 0.01
RATE_MATRIX = 0.01
RATE_TABLE = 0.1


def matmul(lhs_mat, rhs_mat):
    return jnp.dot(lhs_mat, rhs_mat, preferred_element_type=jnp.float32)


def contract_rows(lhs_mat, rhs_mat):
    return lax.dot_general(
        lhs_mat, rhs_mat, (((0,), (0,)), ((), ())), preferred_element_type=jnp.float32
    )


def contract_cols(lhs_mat, rhs_mat):
    return lax.dot_general(
        lhs_mat, rhs_mat, (((1,), (1,)), ((), ())), preferred_element_type=jnp.float32
    )


def layer_norm(values, scale_gain, shift_bias):
    average = jnp.mean(values, axis=-1, keepdims=True)
    centered = values - average
    inverse = lax.rsqrt(jnp.mean(centered * centered, axis=-1, keepdims=True) + NORM_EPS)
    normed = centered * inverse
    return (normed * (1.0 + scale_gain) + shift_bias, (normed, inverse))


def norm_back(upstream, stored, scale_gain):
    normed, inverse = stored
    scaled = upstream * (1.0 + scale_gain)
    back = inverse * (
        scaled
        - jnp.mean(scaled, axis=-1, keepdims=True)
        - normed * jnp.mean(scaled * normed, axis=-1, keepdims=True)
    )
    return (back, jnp.sum(upstream * normed, axis=0), jnp.sum(upstream, axis=0))


def starts_of(lengths):
    order = jnp.arange(PPD, dtype=jnp.int32)
    before = (order[:, None] > order[None, :]).astype(jnp.int32)
    return jnp.sum(before * lengths[..., None, :], axis=-1)


def layout_of(lengths):
    starts = starts_of(lengths)
    place = jnp.arange(ROW, dtype=jnp.int32)
    above = (place[:, None] >= starts[..., None, :]).astype(jnp.int32)
    segment = jnp.sum(above, axis=-1) - 1
    begin = jnp.max(above * starts[..., None, :], axis=-1)
    return segment, place - begin


def one_hot(index, depth):
    return (index[..., None] == jnp.arange(depth, dtype=jnp.int32)).astype(BF)


def split_two(values):
    high = lax.reduce_precision(values, 8, 7)
    return high.astype(BF), (values - high).astype(BF)


def split_three(values):
    high = lax.reduce_precision(values, 8, 7)
    middle = lax.reduce_precision(values - high, 8, 7)
    return high.astype(BF), middle.astype(BF), (values - high - middle).astype(BF)


def window_start(block, count):
    return min(max(block * BLK - (WIN - BLK) // 2, 0), count - WIN)


def attn_forward_kernel(count, segc_ref, segw_ref, z_ref, o_ref, lse_ref):
    block = pl.program_id(0)
    row = pl.multiple_of(block * BLK, BLK)
    first = pl.multiple_of(jnp.clip(row - (WIN - BLK) // 2, 0, count - WIN), 64)
    allowed = segc_ref[...] == segw_ref[0]
    lane = lax.broadcasted_iota(jnp.int32, (BLK, 2 * HD), 1)
    lane_head = lax.broadcasted_iota(jnp.int32, (BLK, 128), 1)
    kept = jnp.zeros((BLK, 128), F32)
    for pair in range(HEADS // 2):
        at = pair * 2 * HD
        query = z_ref[pl.ds(row, BLK), at : at + 2 * HD] * BF(HD ** (-0.5))
        key = z_ref[pl.ds(first, WIN), D + at : D + at + 2 * HD]
        value = z_ref[pl.ds(first, WIN), 2 * D + at : 2 * D + at + 2 * HD]
        parts = []
        for half in range(2):
            mine = (lane >= half * HD) & (lane < (half + 1) * HD)
            scores = contract_cols(jnp.where(mine, query, BF(0)), key)
            scores = jnp.where(allowed, scores, -1000000000.0)
            top = jnp.max(scores, axis=-1, keepdims=True)
            weight = jnp.exp(scores - top)
            total = jnp.sum(weight, axis=-1, keepdims=True)
            probs = (weight * (1.0 / total)).astype(BF)
            parts.append(matmul(probs, value))
            kept = jnp.where(lane_head == 2 * pair + half, top + jnp.log(total), kept)
        o_ref[:, at : at + 2 * HD] = jnp.where(lane < HD, parts[0], parts[1]).astype(BF)
    lse_ref[...] = kept


def attn_backward_kernel(
    count, blocks, segc_ref, segw_ref, z_ref, do_ref, lse_ref, one_ref, dz_ref, dk_ref, dv_ref
):
    block = pl.program_id(0)
    row = pl.multiple_of(block * BLK, BLK)
    first = pl.multiple_of(jnp.clip(row - (WIN - BLK) // 2, 0, count - WIN), 64)

    @pl.when(block == 0)
    def _():
        dk_ref[...] = jnp.zeros_like(dk_ref)
        dv_ref[...] = jnp.zeros_like(dv_ref)

    allowed = segc_ref[...] == segw_ref[0]
    lane = lax.broadcasted_iota(jnp.int32, (BLK, 2 * HD), 1)
    kept = lse_ref[...]
    for pair in range(HEADS // 2):
        at = pair * 2 * HD
        query = z_ref[pl.ds(row, BLK), at : at + 2 * HD] * BF(HD ** (-0.5))
        key = z_ref[pl.ds(first, WIN), D + at : D + at + 2 * HD]
        value = z_ref[pl.ds(first, WIN), 2 * D + at : 2 * D + at + 2 * HD]
        upstream = do_ref[:, at : at + 2 * HD]
        grad_query = []
        grad_key = jnp.zeros((WIN, 2 * HD), F32)
        grad_value = jnp.zeros((WIN, 2 * HD), F32)
        for half in range(2):
            mine = (lane >= half * HD) & (lane < (half + 1) * HD)
            query_own = jnp.where(mine, query, BF(0))
            up_own = jnp.where(mine, upstream, BF(0))
            scores = jnp.where(allowed, contract_cols(query_own, key), -1000000000.0)
            probs = jnp.exp(scores - kept[:, 2 * pair + half : 2 * pair + half + 1])
            grad_probs = contract_cols(up_own, value)
            grad_value = grad_value + contract_rows(probs.astype(BF), up_own)
            inner = jnp.sum(grad_probs * probs, axis=-1, keepdims=True)
            grad_scores = (probs * (grad_probs - inner)).astype(BF)
            grad_query.append(matmul(grad_scores, key))
            grad_key = grad_key + contract_rows(grad_scores, query_own)
        own = jnp.where(lane < HD, grad_query[0], grad_query[1]) * HD ** (-0.5)
        dz_ref[pl.ds(row, BLK), at : at + 2 * HD] = own.astype(BF)
        dk_ref[pl.ds(first, WIN), at : at + 2 * HD] += grad_key
        dv_ref[pl.ds(first, WIN), at : at + 2 * HD] += grad_value

    dz_ref[pl.ds(row, BLK), 3 * D :] = one_ref[...]

    @pl.when(block == blocks - 1)
    def _():
        dz_ref[:, D : 2 * D] = dk_ref[...].astype(BF)
        dz_ref[:, 2 * D : 3 * D] = dv_ref[...].astype(BF)


def attention_specs(count):
    return [
        pl.BlockSpec((BLK, 1), lambda i: (i, 0)),
        pl.BlockSpec((1, 1, WIN), lambda i: (i, 0, 0)),
        pl.BlockSpec((count, 3 * D), lambda i: (0, 0)),
    ]


def attention_forward(segment_column, segment_windows, mixed):
    count = mixed.shape[0]
    blocks = count // BLK
    return pl.pallas_call(
        lambda *refs: attn_forward_kernel(count, *refs),
        grid=(blocks,),
        in_specs=attention_specs(count),
        out_specs=[
            pl.BlockSpec((BLK, D), lambda i: (i, 0)),
            pl.BlockSpec((BLK, 128), lambda i: (i, 0)),
        ],
        out_shape=[
            jax.ShapeDtypeStruct((count, D), BF),
            jax.ShapeDtypeStruct((count, 128), F32),
        ],
        compiler_params=pltpu.CompilerParams(vmem_limit_bytes=40 * 2**20),
        cost_estimate=pl.CostEstimate(
            flops=4 * count * WIN * 128 * HEADS, bytes_accessed=12000000, transcendentals=0
        ),
    )(segment_column, segment_windows, mixed)


def attention_backward(segment_column, segment_windows, mixed, upstream, kept, beside):
    count = mixed.shape[0]
    blocks = count // BLK
    return pl.pallas_call(
        lambda *refs: attn_backward_kernel(count, blocks, *refs),
        grid=(blocks,),
        in_specs=attention_specs(count)
        + [
            pl.BlockSpec((BLK, D), lambda i: (i, 0)),
            pl.BlockSpec((BLK, 128), lambda i: (i, 0)),
            pl.BlockSpec((BLK, D), lambda i: (i, 0)),
        ],
        out_specs=pl.BlockSpec((count, 4 * D), lambda i: (0, 0)),
        out_shape=jax.ShapeDtypeStruct((count, 4 * D), BF),
        scratch_shapes=[pltpu.VMEM((count, D), F32), pltpu.VMEM((count, D), F32)],
        compiler_params=pltpu.CompilerParams(vmem_limit_bytes=56 * 2**20),
        cost_estimate=pl.CostEstimate(
            flops=10 * count * WIN * 128 * HEADS, bytes_accessed=18000000, transcendentals=0
        ),
    )(segment_column, segment_windows, mixed, upstream, kept, beside)


def place_of():
    return lax.axis_index("grp") * lax.axis_size("psg") + lax.axis_index("psg")


def mesh_place(place):
    members = lax.axis_size("psg")
    return (place // members, place % members)


def flipped(place, mask):
    result, bit = place, 0
    while mask >> bit:
        if (mask >> bit) & 1:
            result = result + (1 - 2 * ((place // (1 << bit)) % 2)) * (1 << bit)
        bit += 1
    return result


def greet_all(devices, me):
    barrier = pltpu.get_barrier_semaphore()

    @pl.loop(1, devices)
    def _(i):
        pl.semaphore_signal(
            barrier,
            inc=1,
            device_id=mesh_place((me + i) % devices),
            device_id_type=pl.DeviceIdType.MESH,
        )

    pl.semaphore_wait(barrier, devices - 1)


def gather_plan(order, group):
    held, steps = [0], []
    for bit in order:
        fresh = [(1 << bit) | m for m in held]
        steps.append([fresh[i : i + group] for i in range(0, len(fresh), group)])
        held = held + fresh
    return steps


def earlier_rows(width):
    above = lax.broadcasted_iota(jnp.int32, (width, width), 0)
    return (above < lax.broadcasted_iota(jnp.int32, (width, width), 1)).astype(F32).astype(BF)


def rank_rows(asked, earlier, rank_ref):
    width = earlier.shape[0]
    asked = jnp.concatenate([asked[:, j, :] for j in range(width // 128)], axis=1)
    rank_ref[...] = jnp.where(asked > 0.5, matmul(asked.astype(BF), earlier), -1.0)
    return jnp.max(jnp.sum(asked, axis=1, keepdims=True), axis=0, keepdims=True)


def pack_rows(places, slot, most, table, rank_ref, packed_ref):
    capacity, width = packed_ref.shape[1], table.shape[0]
    at = lax.broadcasted_iota(jnp.int32, (capacity, width), 0).astype(F32)
    picked = [
        jnp.where(rank_ref[pl.ds(place, 1), :] == at, 1.0, 0.0).astype(BF) for place in places
    ]
    rows = matmul(jnp.concatenate(picked), table[...]).reshape(len(places), capacity, D)
    last = lax.broadcasted_iota(jnp.int32, (len(places), capacity, D), 1) == capacity - 1
    rows = jnp.where(last & (most > capacity)[:, :, None], MARK, rows)
    packed_ref[slot : slot + len(places)] = rows.astype(BF)


def gather_kernel(devices, pieces, *refs):
    matrices = 3
    sources, (needed, notes, table) = refs[:matrices], refs[matrices : matrices + 3]
    outs, (notes_out, rows_out, rank) = refs[6:9], refs[9:12]
    asked, earlier, packed, arrive, beside, leave, local, notes_sem, ask_sem, rows_sem = refs[12:]
    me = place_of()
    group = max(devices // 8, 1)
    greet_all(devices, me)

    def push(source, target_ref, target, send, recv):
        pltpu.make_async_remote_copy(
            src_ref=source,
            dst_ref=target_ref,
            send_sem=send,
            recv_sem=recv,
            device_id=mesh_place(target),
            device_id_type=pl.DeviceIdType.MESH,
        ).start()

    def settle(some, semaphore):
        pltpu.make_async_copy(some, some, semaphore).wait()

    @pl.loop(1, devices)
    def _(i):
        target = (me + i) % devices
        push(needed.at[target], asked.at[me], target, ask_sem.at[0], ask_sem.at[1])

    def start(piece, mask, target, semaphore):
        which, first, rows, _ = pieces[piece]
        there = outs[which].at[flipped(me, mask), pl.ds(first, rows)]
        here = sources[which].at[pl.ds(first, rows)] if mask == 0 else there
        push(here, there, flipped(me, target), leave.at[piece], semaphore)

    def wait(piece, blocks, semaphore):
        which, first, rows, _ = pieces[piece]
        settle(outs[which].at[pl.ds(0, blocks), pl.ds(first, rows)], semaphore)

    plans, numbers = [], []
    for piece in range(len(pieces)):
        plan = gather_plan(pieces[piece][3], group)
        number, count = {}, 0
        for groups in plan:
            for masks in groups:
                for mask in masks:
                    number[mask] = count
                count += 1
        plans.append(plan)
        numbers.append(number)

    def send_on(piece, mask, after):
        order = pieces[piece][3]
        for step in range(after + 1, len(order)):
            target = 1 << order[step]
            start(piece, mask, target, arrive.at[piece, numbers[piece][mask | target]])
        start(piece, mask, 1, beside.at[piece])

    def pass_on(piece, step):
        for masks in plans[piece][step]:
            wait(piece, len(masks), arrive.at[piece, numbers[piece][masks[0]]])
            for mask in masks:
                send_on(piece, mask, step)

    for piece in range(len(pieces)):
        send_on(piece, 0, -1)

    @pl.loop(1, devices)
    def _(i):
        target = (me + i) % devices
        push(notes, notes_out.at[me], target, notes_sem.at[0], notes_sem.at[1])

    own = [
        pltpu.make_async_copy(source, out.at[me], local.at[i])
        for i, (source, out) in enumerate(zip(sources, outs))
    ]
    own.append(pltpu.make_async_copy(notes, notes_out.at[me], local.at[matrices]))
    own_asked = pltpu.make_async_copy(needed.at[me], asked.at[me], local.at[matrices + 1])
    for copy in own:
        copy.start()
    own_asked.start()
    earlier[...] = earlier_rows(table.shape[0])
    for piece in range(len(pieces)):
        pass_on(piece, 0)
    own_asked.wait()
    for i in range(2):
        settle(asked.at[pl.ds(0, devices - 1)], ask_sem.at[i])
    most = rank_rows(asked[...], earlier[...], rank)

    masks = sorted(range(devices), key=lambda m: -bin(m).count("1"))
    steps = len(pieces[0][3])
    each = -(-(devices - 1) // (len(pieces) * (steps - 1)))
    kept_rows = pltpu.make_async_copy(
        packed.at[devices - 1], rows_out.at[me], local.at[matrices + 2]
    )
    sent, made, together = 0, 0, 8
    for step in range(1, steps):
        for piece in range(len(pieces)):
            now = min(sent + each, devices)
            while made < now:
                group_now = masks[made : made + together]
                places = [flipped(me, m) for m in group_now]
                pack_rows(places, made, most, table, rank, packed)
                made += together
            pass_on(piece, step)
            for i in range(sent, now):
                target = flipped(me, masks[i])
                if masks[i]:
                    push(packed.at[i], rows_out.at[me], target, rows_sem.at[0], rows_sem.at[1])
                else:
                    kept_rows.start()
            sent = now
    for piece in range(len(pieces)):
        wait(piece, devices // 2, beside.at[piece])
        wait(piece, devices - 1, leave.at[piece])
    for copy in own:
        copy.wait()
    kept_rows.wait()
    for i in range(2):
        settle(notes_out.at[pl.ds(0, devices - 1)], notes_sem.at[i])
        settle(rows_out.at[pl.ds(0, devices - 1)], rows_sem.at[i])


def gather_all(sources, needed, notes, table, capacity):
    devices = needed.shape[0]
    rows = sources[0].shape[0]
    bits = devices.bit_length() - 1
    high = list(range(3, bits))[::-1]
    one, other = (*high, 2, 1), (*high, 1, 2)
    cut = rows // 32 * 16
    pieces = [(0, 0, rows, one), (2, 0, rows, other), (1, cut, rows - cut, one)]
    if cut:
        pieces.append((1, 0, cut, other))
    count = max(sum(map(len, gather_plan(p[3], max(devices // 8, 1)))) for p in pieces)
    anywhere = pl.BlockSpec(memory_space=pl.ANY)
    inside = pl.BlockSpec(memory_space=pltpu.VMEM)
    dma = pltpu.SemaphoreType.DMA
    *gathered, noted, arrived, rank = pl.pallas_call(
        lambda *refs: gather_kernel(devices, pieces, *refs),
        in_specs=[anywhere] * 3 + [inside] * 3,
        out_specs=[anywhere] * 5 + [inside],
        out_shape=[jax.ShapeDtypeStruct((devices, *s.shape), s.dtype) for s in (*sources, notes)]
        + [
            jax.ShapeDtypeStruct((devices, capacity, D), BF),
            jax.ShapeDtypeStruct((devices, table.shape[0]), F32),
        ],
        scratch_shapes=[
            pltpu.VMEM(needed.shape, F32),
            pltpu.VMEM((table.shape[0], table.shape[0]), BF),
            pltpu.VMEM((devices, capacity, D), BF),
            dma((len(pieces), count)),
            dma((len(pieces),)),
            dma((len(pieces),)),
            dma((6,)),
            dma((2,)),
            dma((2,)),
            dma((2,)),
        ],
        compiler_params=pltpu.CompilerParams(
            collective_id=0, has_side_effects=True, vmem_limit_bytes=48 * 2**20
        ),
    )(*sources, needed, notes, table)
    return gathered, noted, arrived, rank


def reduce_plan(order, group):
    held = [0]
    for bit in reversed(order):
        held = [m | (1 << bit) for m in held] + held
    steps = []
    for step in range(len(order) + 1):
        if step:
            held = [m for m in held if not (m >> order[step - 1]) & 1]
        steps.append([held[i : i + group] for i in range(0, len(held), group)])
    return steps


def reduce_kernel(devices, pieces, spread, *refs):
    count = len({p[0] for p in pieces})
    sources, rows_in = refs[:count], refs[count]
    outs, rows_out = refs[count + 1 : 2 * count + 1], refs[2 * count + 1]
    held, landed = refs[2 * count + 2 : 3 * count + 2], refs[3 * count + 2 : 4 * count + 2]
    arrive, leave, load, rows_sem, own_sem = refs[4 * count + 2 :]
    me = place_of()
    group = max(devices // 16, 1)
    greet_all(devices, me)

    def push(source, target_ref, target, send, recv):
        pltpu.make_async_remote_copy(
            src_ref=source,
            dst_ref=target_ref,
            send_sem=send,
            recv_sem=recv,
            device_id=mesh_place(target),
            device_id_type=pl.DeviceIdType.MESH,
        ).start()

    def settle(some, semaphore):
        pltpu.make_async_copy(some, some, semaphore).wait()

    plans, slots, places, numbers = [], [], [], []
    for piece in pieces:
        plan = reduce_plan(piece[3], group)
        slots.append({m: i for i, m in enumerate(sum(plan[0], []))})
        place, number, at, count = {}, {}, 0, 0
        for step, groups in enumerate(plan):
            for masks in groups:
                for mask in masks:
                    place[step, mask], number[step, mask] = at, count
                    at += 1
                count += 1
        plans.append(plan)
        places.append(place)
        numbers.append(number)

    def rows_of(piece):
        return pl.ds(pieces[piece][1], pieces[piece][2])

    def send(piece, step, mask, bit, source):
        which = pieces[piece][0]
        kept = mask & ~(1 << bit)
        push(
            source,
            landed[which].at[places[piece][step, kept], rows_of(piece)],
            flipped(me, 1 << bit),
            leave.at[piece],
            arrive.at[piece, numbers[piece][step, kept]],
        )

    order = sorted(range(1, devices), key=lambda m: -bin(m).count("1"))

    def send_rows(amount):
        for _ in range(min(amount, len(order))):
            target = flipped(me, order.pop(0))
            push(rows_in.at[target], rows_out.at[me], target, rows_sem.at[0], rows_sem.at[1])

    own_rows = pltpu.make_async_copy(rows_in.at[me], rows_out.at[me], own_sem)
    own_rows.start()
    send_rows(spread[0])
    for masks in plans[0][0]:
        for piece in range(len(pieces)):
            which = pieces[piece][0]
            for mask in plans[piece][0][plans[0][0].index(masks)]:
                source = sources[which].at[flipped(me, mask | 1), rows_of(piece)]
                send(piece, 0, mask | 1, 0, source)
    for piece in range(len(pieces)):
        which = pieces[piece][0]
        for mask in slots[piece]:
            pltpu.make_async_copy(
                sources[which].at[flipped(me, mask), rows_of(piece)],
                held[which].at[slots[piece][mask], rows_of(piece)],
                load.at[piece],
            ).start()
    turn = 1
    for step in range(len(pieces[0][3]) + 1):
        for at in range(len(plans[0][step])):
            for piece in range(len(pieces)):
                which, _, _, bits = pieces[piece]
                rows = rows_of(piece)
                if step == 0 and at == 0:
                    settle(held[which].at[pl.ds(0, devices // 2), rows], load.at[piece])
                masks = plans[piece][step][at]
                some = landed[which].at[pl.ds(0, len(masks)), rows]
                settle(some, arrive.at[piece, numbers[piece][step, masks[0]]])
                for mask in masks:
                    slot = slots[piece][mask]
                    total = held[which][slot, rows].astype(F32)
                    total = total + landed[which][places[piece][step, mask], rows].astype(F32)
                    if step == len(bits):
                        outs[which][rows] = total
                        continue
                    held[which][slot, rows] = total.astype(held[which].dtype)
                    if (mask >> bits[step]) & 1:
                        send(piece, step + 1, mask, bits[step], held[which].at[slot, rows])
            send_rows(spread[turn] if turn < len(spread) else 0)
            turn += 1
    send_rows(devices)
    for piece in range(len(pieces)):
        which = pieces[piece][0]
        settle(landed[which].at[pl.ds(0, devices - 1), rows_of(piece)], leave.at[piece])
    own_rows.wait()
    for i in range(2):
        settle(rows_out.at[pl.ds(0, devices - 1)], rows_sem.at[i])


def reduce_all(sources, rows_in):
    devices = rows_in.shape[0]
    bits = devices.bit_length() - 1
    high = list(range(3, bits))
    one, other = (1, 2, *high), (2, 1, *high)
    pieces = []
    for i in (0, 2, 1, 3, 4):
        rows = sources[i].shape[1]
        cut = rows // 32 * 16 if i == 1 else 0
        pieces.append((i, cut, rows - cut, one if i in (0, 1, 3) else other))
        if cut:
            pieces.append((i, 0, cut, other))
    spread = [6] + [2] * devices
    count = max(sum(map(len, reduce_plan(p[3], max(devices // 16, 1)))) for p in pieces)
    anywhere = pl.BlockSpec(memory_space=pl.ANY)
    inside = pl.BlockSpec(memory_space=pltpu.VMEM)
    dma = pltpu.SemaphoreType.DMA
    *reduced, arrived = pl.pallas_call(
        lambda *refs: reduce_kernel(devices, pieces, spread, *refs),
        in_specs=[anywhere] * (len(sources) + 1),
        out_specs=[inside] * len(sources) + [anywhere],
        out_shape=[jax.ShapeDtypeStruct(s.shape[1:], F32) for s in sources]
        + [jax.ShapeDtypeStruct(rows_in.shape, rows_in.dtype)],
        scratch_shapes=[pltpu.VMEM((devices // 2, *s.shape[1:]), s.dtype) for s in sources]
        + [pltpu.VMEM((devices - 1, *s.shape[1:]), s.dtype) for s in sources]
        + [dma((len(pieces), count)), dma((len(pieces),)), dma((len(pieces),)), dma((2,)), dma],
        compiler_params=pltpu.CompilerParams(
            collective_id=1, has_side_effects=True, vmem_limit_bytes=48 * 2**20
        ),
    )(*sources, rows_in)
    return reduced, arrived


def product_kernel(devices, pieces, spread, *refs):
    count, computed = len({p[0] for p in pieces}), 3
    lefts, rights, others, rows_in = refs[:3], refs[3:6], refs[6 : count + 3], refs[count + 3]
    refs = refs[count + 4 :]
    outs, rows_out = refs[:count], refs[count]
    held, landed = refs[count + 1 : 2 * count + 1], refs[2 * count + 1 : 3 * count + 1]
    refs = refs[3 * count + 1 :]
    ready, refs = refs[:computed], refs[computed:]
    slab, slab_sem, arrive, leave, load, rows_sem, own_sem = refs
    me = place_of()
    groups = devices // 4
    half = groups // 2
    depth = groups.bit_length() - 1
    chunk = outs[0].shape[0]
    greet_all(devices, me)

    def push(source, target_ref, target, send, recv):
        pltpu.make_async_remote_copy(
            src_ref=source,
            dst_ref=target_ref,
            send_sem=send,
            recv_sem=recv,
            device_id=mesh_place(target),
            device_id_type=pl.DeviceIdType.MESH,
        ).start()

    def settle(some, semaphore):
        pltpu.make_async_copy(some, some, semaphore).wait()

    plans, slots, places = [], [], []
    for piece in pieces:
        plan = [sum(step, []) for step in reduce_plan(piece[3], 1)]
        slots.append({m: i for i, m in enumerate(plan[0])})
        place, at = {}, 0
        for step, masks in enumerate(plan):
            for mask in masks:
                place[step, mask] = at
                at += 1
        plans.append(plan)
        places.append(place)

    def rows_of(piece):
        return pl.ds(pieces[piece][1], pieces[piece][2])

    def send(piece, step, mask, bit, source):
        where = places[piece][step, mask & ~(1 << bit)]
        push(
            source,
            landed[pieces[piece][0]].at[where, rows_of(piece)],
            flipped(me, 1 << bit),
            leave.at[piece],
            arrive.at[piece, where],
        )

    order = sorted(range(1, devices), key=lambda m: -bin(m).count("1"))

    def send_rows(amount):
        for _ in range(min(amount, len(order))):
            target = flipped(me, order.pop(0))
            push(rows_in.at[target], rows_out.at[me], target, rows_sem.at[0], rows_sem.at[1])

    def group_of(turn):
        own, place = me // 4, 0
        for bit in range(depth):
            differs = 1 - (turn // (1 << (depth - 1 - bit))) % 2
            place = place + ((own // (1 << bit) + differs) % 2) * (1 << bit)
        return place

    def slab_copy(which, turn):
        width = 4 * chunk
        columns = pl.ds(pl.multiple_of(group_of(turn) * width, width), width)
        return pltpu.make_async_copy(
            lefts[which].at[:, columns],
            slab.at[turn % 2, which],
            slab_sem.at[turn % 2, which],
        )

    def slot_of(piece, turn, side):
        if pieces[piece][3][0] == 1:
            return (1 - side) * groups + turn
        return (turn // half) * groups + (1 - side) * half + turn % half

    big = [p for p in range(len(pieces)) if pieces[p][0] < computed]
    small = [p for p in range(len(pieces)) if pieces[p][0] >= computed]
    own_rows = pltpu.make_async_copy(rows_in.at[me], rows_out.at[me], own_sem)
    own_rows.start()
    for which in range(computed):
        slab_copy(which, 0).start()
    send_rows(spread[0])
    for piece in small:
        source = others[pieces[piece][0] - computed]
        for mask in plans[piece][0]:
            send(piece, 0, mask | 1, 0, source.at[flipped(me, mask | 1)])
            pltpu.make_async_copy(
                source.at[flipped(me, mask)],
                held[pieces[piece][0]].at[slots[piece][mask]],
                load.at[piece],
            ).start()

    def add(piece, slot, where):
        which, rows = pieces[piece][0], rows_of(piece)
        some = landed[which].at[pl.ds(where, 1), rows]
        settle(some, arrive.at[piece, where])
        total = held[which][slot, rows].astype(F32)
        return total + landed[which][where, rows].astype(F32)

    def first_add(turn):
        for side in (1, 0):
            for piece in big:
                which, rows, bits = pieces[piece][0], rows_of(piece), pieces[piece][3]
                slot = slot_of(piece, turn, side)
                held[which][slot, rows] = add(piece, slot, slot).astype(BF)

                def on():
                    sent = len(plans[piece][0])
                    push(
                        held[which].at[slot, rows],
                        landed[which].at[sent + slot, rows],
                        flipped(me, 1 << bits[0]),
                        leave.at[piece],
                        arrive.at[piece, sent + slot],
                    )

                if bits[0] == 1 and side:
                    on()
                elif bits[0] == 2:
                    pl.when(turn < half)(on)

    @pl.loop(0, groups)
    def _(turn):
        @pl.when(turn + 1 < groups)
        def _():
            for which in range(computed):
                slab_copy(which, turn + 1).start()

        near = (me // 2) % 2
        core = me % 2
        for which in (0, 2, 1):
            slab_copy(which, turn).wait()
            if which == 0:
                right = rights[0].at[(group_of(turn) * 4 * chunk) // (3 * D)]
            else:
                right = rights[which]
            block = contract_rows(slab[turn % 2, which], right[...])
            block = block.astype(BF).reshape(4, chunk, D)
            for side in range(2):
                for same in range(2):
                    ready[which][turn * 4 + side * 2 + same] = block[side * 2 + same]
            for piece in big:
                if pieces[piece][0] != which:
                    continue
                rows = rows_of(piece)
                for side in range(2):
                    line = (near + side) % 2
                    slot = slot_of(piece, turn, side)
                    kept = ready[which].at[turn * 4 + line * 2 + core, rows]
                    held[which][slot, rows] = kept[...]
                    push(
                        ready[which].at[turn * 4 + line * 2 + 1 - core, rows],
                        landed[which].at[slot, rows],
                        flipped(me, 1),
                        leave.at[piece],
                        arrive.at[piece, slot],
                    )

        @pl.when(turn > 0)
        def _():
            first_add(turn - 1)

    first_add(groups - 1)
    turn = 1
    for step in range(len(pieces[0][3]) + 1):
        for at in range(len(plans[0][step])):
            for piece in small if step == 0 else (*big, *small):
                which, _, _, bits = pieces[piece]
                rows = rows_of(piece)
                if step == 0 and at == 0:
                    settle(held[which].at[pl.ds(0, devices // 2), rows], load.at[piece])
                mask = plans[piece][step][at]
                slot = slots[piece][mask]
                total = add(piece, slot, places[piece][step, mask])
                if step == len(bits):
                    outs[which][rows] = total
                    continue
                held[which][slot, rows] = total.astype(held[which].dtype)
                if (mask >> bits[step]) & 1:
                    send(piece, step + 1, mask, bits[step], held[which].at[slot, rows])
            if step or at == 0:
                send_rows(spread[turn] if turn < len(spread) else 0)
                turn += 1
    send_rows(devices)
    for piece in range(len(pieces)):
        which = pieces[piece][0]
        settle(landed[which].at[pl.ds(0, devices - 1), rows_of(piece)], leave.at[piece])
    own_rows.wait()
    for i in range(2):
        settle(rows_out.at[pl.ds(0, devices - 1)], rows_sem.at[i])


def reduce_products(lefts, rights, others, rows_in):
    devices = rows_in.shape[0]
    count, wide = lefts[0].shape
    chunk = wide // devices
    bits = devices.bit_length() - 1
    high = list(range(3, bits))
    one, other = (1, 2, *high), (2, 1, *high)
    cut = chunk // 32 * 16
    pieces = [(0, 0, chunk, one), (2, 0, chunk, other), (1, cut, chunk - cut, one)]
    pieces += [(1, 0, cut, other), (3, 0, others[0].shape[1], one), (4, 0, others[1].shape[1], other)]
    spread = [12] + [2] * devices
    anywhere = pl.BlockSpec(memory_space=pl.ANY)
    inside = pl.BlockSpec(memory_space=pltpu.VMEM)
    dma = pltpu.SemaphoreType.DMA
    kinds = [((chunk, D), BF)] * 3 + [(o.shape[1:], o.dtype) for o in others]
    *reduced, arrived = pl.pallas_call(
        lambda *refs: product_kernel(devices, pieces, spread, *refs),
        in_specs=[anywhere] * 3 + [inside] * 3 + [anywhere] * (len(others) + 1),
        out_specs=[inside] * len(kinds) + [anywhere],
        out_shape=[jax.ShapeDtypeStruct(shape, F32) for shape, _ in kinds]
        + [jax.ShapeDtypeStruct(rows_in.shape, rows_in.dtype)],
        scratch_shapes=[pltpu.VMEM((devices // 2, *shape), kind) for shape, kind in kinds]
        + [pltpu.VMEM((devices - 1, *shape), kind) for shape, kind in kinds]
        + [pltpu.VMEM((devices, chunk, D), BF)] * 3
        + [pltpu.VMEM((2, 3, count, 4 * chunk), BF), dma((2, 3))]
        + [dma((len(pieces), devices - 1)), dma((len(pieces),)), dma((len(pieces),)), dma((2,)), dma],
        compiler_params=pltpu.CompilerParams(
            collective_id=2, has_side_effects=True, vmem_limit_bytes=60 * 2**20
        ),
    )(*lefts, jnp.stack(rights[:2]), *rights[2:], *others, rows_in)
    return reduced, arrived


TOK = 256


def normalize(values):
    average = jnp.mean(values, axis=-1, keepdims=True)
    centered = values - average
    inverse = lax.rsqrt(jnp.mean(centered * centered, axis=-1, keepdims=True) + NORM_EPS)
    return centered * inverse, inverse


def normalize_back(upstream, normed, inverse, gain):
    scaled = upstream * (1.0 + gain)
    return inverse * (
        scaled
        - jnp.mean(scaled, axis=-1, keepdims=True)
        - normed * jnp.mean(scaled * normed, axis=-1, keepdims=True)
    )


def vector(vec_ref, i):
    return vec_ref[i : i + 1, :]


def first_kernel(looked_ref, place_ref, table_ref, vec_ref, qkv_ref, normed_ref, inv_ref, low_ref, z_ref):
    hot = place_ref[...] == lax.broadcasted_iota(jnp.int32, (TOK, PMAX), 1)
    values = looked_ref[...] + matmul(hot.astype(F32).astype(BF), table_ref[...])
    normed, inverse = normalize(values)
    normed_ref[...] = normed
    inv_ref[...] = inverse
    low = (normed * (1.0 + vector(vec_ref, 0)) + vector(vec_ref, 1)).astype(BF)
    low_ref[...] = low
    for part, bias in ((0, 2), (1, None), (2, 3)):
        at = slice(part * D, (part + 1) * D)
        mixed = contract_cols(low, qkv_ref[at, :])
        if bias is not None:
            mixed = mixed + vector(vec_ref, bias)
        z_ref[:, at] = mixed.astype(BF)


def middle_kernel(
    context_ref, zero_ref, vec_ref, bias_ref, out_ref, up_ref, down_ref, head_ref, *results
):
    one_ref, one_inv_ref, one_low_ref, act_ref, slope_ref = results[:5]
    two_ref, two_inv_ref, two_low_ref, unit_ref, scale_ref, unit_low_ref = results[5:]
    hidden = zero_ref[...] * (1.0 + vector(vec_ref, 0)) + vector(vec_ref, 1)
    hidden = hidden + contract_cols(context_ref[...], out_ref[...]) + vector(vec_ref, 4)
    normed, inverse = normalize(hidden)
    one_ref[...] = normed
    one_inv_ref[...] = inverse
    hidden = normed * (1.0 + vector(vec_ref, 5)) + vector(vec_ref, 6)
    low = hidden.astype(BF)
    one_low_ref[...] = low
    total = hidden + vector(vec_ref, 7)
    for part in range(up_ref.shape[0] // D):
        at = slice(part * D, (part + 1) * D)
        inner = contract_cols(low, up_ref[at, :]) + bias_ref[:, at]
        cdf = 0.5 + 0.5 * lax.erf(inner * math.sqrt(0.5))
        activated = (inner * cdf).astype(BF)
        act_ref[:, at] = activated
        pdf = jnp.exp(-0.5 * inner * inner) * (1.0 / math.sqrt(2.0 * math.pi))
        slope_ref[:, at] = (cdf + inner * pdf).astype(BF)
        total = total + matmul(activated, down_ref[at, :])
    normed, inverse = normalize(total)
    two_ref[...] = normed
    two_inv_ref[...] = inverse
    low = (normed * (1.0 + vector(vec_ref, 8)) + vector(vec_ref, 9)).astype(BF)
    two_low_ref[...] = low
    projected = matmul(low, head_ref[...])
    scale = lax.rsqrt(jnp.sum(projected * projected, axis=-1, keepdims=True) + NORM_EPS)
    unit_ref[...] = projected * scale
    scale_ref[...] = scale
    unit_low_ref[...] = (projected * scale).astype(BF)


def column_sum(values):
    return jnp.sum(values, axis=0, keepdims=True)


def middle_back_kernel(
    grad_ref,
    unit_ref,
    scale_ref,
    two_ref,
    two_inv_ref,
    slope_ref,
    one_ref,
    one_inv_ref,
    vec_ref,
    out_ref,
    up_ref,
    down_ref,
    head_ref,
    *results,
):
    proj_ref, dtwo_ref, inner_ref, done_ref, done_low_ref, context_ref, sums_ref, bias_ref = results

    @pl.when(pl.program_id(0) == 0)
    def _():
        sums_ref[...] = jnp.zeros_like(sums_ref)
        bias_ref[...] = jnp.zeros_like(bias_ref)

    grad, unit = grad_ref[...], unit_ref[...]
    proj = (grad - unit * jnp.sum(grad * unit, axis=-1, keepdims=True)) * scale_ref[...]
    proj = proj.astype(BF)
    proj_ref[...] = proj
    upstream, normed = contract_cols(proj, head_ref[...]), two_ref[...]
    dtwo = normalize_back(upstream, normed, two_inv_ref[...], vector(vec_ref, 8))
    sums_ref[0:1, :] += column_sum(upstream * normed)
    sums_ref[1:2, :] += column_sum(upstream)
    sums_ref[2:3, :] += column_sum(dtwo)
    low = dtwo.astype(BF)
    dtwo_ref[...] = low
    upstream = dtwo
    for part in range(up_ref.shape[0] // D):
        at = slice(part * D, (part + 1) * D)
        inner = contract_cols(low, down_ref[at, :]) * slope_ref[:, at].astype(F32)
        bias_ref[:, at] += column_sum(inner)
        inner = inner.astype(BF)
        inner_ref[:, at] = inner
        upstream = upstream + matmul(inner, up_ref[at, :])
    normed = one_ref[...]
    done = normalize_back(upstream, normed, one_inv_ref[...], vector(vec_ref, 5))
    sums_ref[3:4, :] += column_sum(upstream * normed)
    sums_ref[4:5, :] += column_sum(upstream)
    sums_ref[5:6, :] += column_sum(done)
    done_ref[...] = done
    low = done.astype(BF)
    done_low_ref[...] = low
    context_ref[...] = matmul(low, out_ref[...]).astype(BF)


def first_back_kernel(
    z_ref, done_ref, zero_ref, inv_ref, place_ref, vec_ref, qkv_ref, low_ref, places_ref, sums_ref
):
    @pl.when(pl.program_id(0) == 0)
    def _():
        sums_ref[...] = jnp.zeros_like(sums_ref)
        places_ref[...] = jnp.zeros_like(places_ref)

    upstream, normed = done_ref[...], zero_ref[...]
    for part in range(3):
        at = slice(part * D, (part + 1) * D)
        upstream = upstream + matmul(z_ref[:, at], qkv_ref[at, :])
    grad = normalize_back(upstream, normed, inv_ref[...], vector(vec_ref, 0))
    sums_ref[0:1, :] += column_sum(upstream * normed)
    sums_ref[1:2, :] += column_sum(upstream)
    sums_ref[2:3, :] += column_sum(z_ref[:, :D].astype(F32))
    sums_ref[3:4, :] += column_sum(z_ref[:, 2 * D : 3 * D].astype(F32))
    low = grad.astype(BF)
    low_ref[...] = low
    hot = place_ref[...] == lax.broadcasted_iota(jnp.int32, (TOK, PMAX), 1)
    places_ref[...] += contract_rows(hot.astype(F32).astype(BF), low)


def by_tokens(width):
    return pl.BlockSpec((TOK, width), lambda i: (i, 0))


def resident(rows, width, at=0):
    return pl.BlockSpec((rows, width), lambda i: (at, 0), pipeline_mode=pl.Buffered(1))


def token_call(kernel, count, in_specs, outs, flops):
    return pl.pallas_call(
        kernel,
        grid=(count // TOK,),
        in_specs=in_specs,
        out_specs=[
            by_tokens(width) if rows is None else pl.BlockSpec((rows, width), lambda i: (0, 0))
            for rows, width, _ in outs
        ],
        out_shape=[
            jax.ShapeDtypeStruct((count if rows is None else rows, width), kind)
            for rows, width, kind in outs
        ],
        compiler_params=pltpu.CompilerParams(vmem_limit_bytes=56 * 2**20),
        cost_estimate=pl.CostEstimate(flops=flops, bytes_accessed=30000000, transcendentals=0),
    )


def adam_update(weight, moment, second, gradient, rate, count_steps):
    moment_new = BETA_ONE * moment + (1.0 - BETA_ONE) * gradient
    second_new = BETA_TWO * second + (1.0 - BETA_TWO) * gradient * gradient
    corrected = moment_new / (1.0 - BETA_ONE**count_steps)
    scaled = second_new / (1.0 - BETA_TWO**count_steps)
    weight_new = weight - rate * (corrected / (jnp.sqrt(scaled) + ADAM_EPS) + WEIGHT_DECAY * weight)
    return (weight_new, second_new)


def on_device(
    query_ids,
    passage_ids,
    passage_lengths,
    positives,
    negatives,
    pair_mask,
    assignments,
    step_count,
    embed_table,
    embed_table_moment,
    embed_table_second,
    attention_weight,
    attention_weight_moment,
    attention_weight_second,
    up_weight,
    up_weight_moment,
    up_weight_second,
    down_weight,
    down_weight_moment,
    down_weight_second,
    head_weight,
    head_weight_moment,
    head_weight_second,
    small_params,
    small_params_moment,
    small_params_second,
):
    devices = lax.axis_size("grp") * lax.axis_size("psg")
    members = lax.axis_size("psg")
    member = lax.axis_index("psg")
    group = lax.axis_index("grp")
    shard_rows = embed_table.shape[0]
    queries = query_ids.shape[0]
    negative_count = negatives.shape[1]
    query_rows = queries * SEG
    count = ROW + query_rows
    capacity = 16 * ((count // devices + 8 + 15) // 16)
    small_size = small_params.shape[0]
    head_rows = head_weight.shape[0]
    mask_float = pair_mask.astype(F32)

    tokens = jnp.concatenate([passage_ids.reshape(-1), query_ids.reshape(-1)])
    passage_segment, passage_position = layout_of(passage_lengths[0])
    query_place = jnp.arange(query_rows, dtype=jnp.int32)
    segment = jnp.concatenate([passage_segment, PPD + query_place // SEG])
    position = jnp.concatenate([passage_position, query_place % SEG])
    segment_column = segment[:, None]
    segment_windows = jnp.stack(
        [
            segment[window_start(i, count) : window_start(i, count) + WIN][None]
            for i in range(count // BLK)
        ]
    )

    def shard_of(rows):
        return jnp.pad(rows.astype(BF), ((0, -rows.shape[0] % 16), (0, 0)))

    matrix_rows = down_weight.shape[0]
    shards = [shard_of(attention_weight.T), shard_of(up_weight.T), shard_of(down_weight)]

    owner = tokens // shard_rows
    local_row = tokens - owner * shard_rows
    owner_hot = one_hot(owner, devices)
    row_hot = one_hot(local_row, shard_rows)
    needed = jnp.minimum(contract_rows(owner_hot, row_hot), 1.0)
    width = -(-shard_rows // 1024) * 1024
    table = jnp.pad(embed_table.astype(BF), ((0, width - shard_rows), (0, 0)))
    notes = jnp.concatenate(
        [
            v.reshape(-1).astype(BF)
            for v in (small_params, head_weight, passage_lengths, jnp.sum(mask_float))
        ]
    )
    notes = jnp.pad(notes, (0, -notes.size % 2048)).reshape(-1, 128)
    gathered, noted, packed, asked_rank = gather_all(
        shards,
        jnp.pad(needed, ((0, 0), (0, width - shard_rows))).reshape(devices, width // 128, 128),
        notes,
        table,
        capacity,
    )
    asked_rank = asked_rank[:, :shard_rows]
    attn_rows, up_rows, down_rows = (g[:, :matrix_rows].reshape(-1, D) for g in gathered)
    noted = noted.reshape(devices, -1)
    cut = [0, small_size, head_rows * DC, PPD, 1]
    for i in range(1, len(cut)):
        cut[i] += cut[i - 1]
    small_all, head_all, lengths_all, pairs_all = (noted[:, cut[i] : cut[i + 1]] for i in range(4))
    small_all = small_all.reshape(-1)
    head_full = head_all.reshape(D, DC)
    pair_floor = jnp.maximum(jnp.sum(pairs_all.astype(F32)), 1.0)
    place_row = jnp.arange(shard_rows, dtype=jnp.int32)
    earlier = (place_row[:, None] < place_row[None, :]).astype(BF)
    overflow = jnp.max(packed[:, capacity - 1, :].astype(F32)) > 0.5 * MARK
    packed = packed.reshape(devices * capacity, D)
    needed_rank = jnp.minimum(matmul(needed.astype(BF), earlier), 255.0)
    token_rank = jnp.sum(matmul(owner_hot, needed_rank.astype(BF)) * row_hot.astype(F32), axis=1)
    slot = owner * capacity + jnp.minimum(token_rank.astype(jnp.int32), capacity - 1)
    slot_hot = one_hot(slot, devices * capacity)
    looked_up = lax.cond(
        overflow,
        lambda: lax.all_gather(embed_table.astype(BF), ALL, axis=0, tiled=True)[tokens].astype(F32),
        lambda: matmul(slot_hot, packed),
    )

    positions = small_all[: PMAX * D].reshape(PMAX, D)
    remainder = small_all[PMAX * D :].astype(F32)
    vectors = jnp.pad(remainder[: 10 * D].reshape(10, D), ((0, 6), (0, 0)))
    bias_up = remainder[None, 10 * D :]
    inner_width = up_rows.shape[0]
    place_column = position[:, None]
    norm_zero, inverse_zero, input_zero, mixed = token_call(
        first_kernel,
        count,
        [by_tokens(D), by_tokens(1), resident(PMAX, D), resident(16, D), resident(3 * D, D)],
        [(None, D, F32), (None, 1, F32), (None, D, BF), (None, 3 * D, BF)],
        2 * count * D * (3 * D + PMAX),
    )(looked_up, place_column, positions, vectors, attn_rows)
    context, kept = attention_forward(segment_column, segment_windows, mixed)
    weight_specs = [
        resident(D, D, 3),
        resident(inner_width, D),
        resident(inner_width, D),
        resident(D, DC),
    ]
    weights = (attn_rows, up_rows, down_rows, head_full)
    middle_flops = 2 * count * D * (D + 2 * inner_width + DC)
    (
        norm_one,
        inverse_one,
        input_one,
        activated,
        slope,
        norm_two,
        inverse_two,
        input_two,
        unit,
        scale_inverse,
        unit_low,
    ) = token_call(
        middle_kernel,
        count,
        [by_tokens(D), by_tokens(D), resident(16, D), resident(1, inner_width), *weight_specs],
        [(None, D, F32), (None, 1, F32), (None, D, BF)]
        + [(None, inner_width, BF)] * 2
        + [(None, D, F32), (None, 1, F32), (None, D, BF)]
        + [(None, DC, F32), (None, 1, F32), (None, DC, BF)],
        middle_flops,
    )(context, norm_zero, vectors, bias_up, *weights)

    units = lax.all_gather(unit_low, "psg", axis=0)
    group_passage = units[:, :ROW]
    group_query = units[:, ROW:].reshape(members * query_rows, DC)
    own_query = unit_low[ROW:]
    own_passage = unit_low[:ROW]
    group_lengths = lax.dynamic_slice_in_dim(lengths_all, group * members, members, 0)
    group_segment, _ = layout_of(group_lengths.astype(jnp.int32))
    group_hot = one_hot(group_segment, PPD)
    passage_hot = one_hot(passage_segment, PPD)

    weighted_own = jnp.exp(
        jnp.einsum("qd,mtd->mqt", own_query, group_passage, preferred_element_type=F32) / TEMPER
    )
    sum_own = lambda part: jnp.einsum(
        "mqt,mtp->mqp", part, group_hot, preferred_element_type=F32
    )
    high, low = split_two(weighted_own)
    totals_own = sum_own(high) + sum_own(low)
    weighted = jnp.exp(contract_cols(group_query, own_passage) / TEMPER)
    high, low = split_two(weighted)
    totals = matmul(high, passage_hot) + matmul(low, passage_hot)
    own_scores = jnp.sum(
        (TEMPER * jnp.log(totals_own)).reshape(members, queries, SEG, PPD), axis=2
    )
    own_scores = own_scores.transpose(1, 0, 2).reshape(queries, members * PPD)
    columns = jnp.arange(members * PPD, dtype=jnp.int32)
    pick_positive = (positives[:, None] == columns[None, :]).astype(F32)
    pick_negative = (negatives[:, :, None] == columns[None, None, :]).astype(F32)
    pos_score = jnp.sum(own_scores * pick_positive, axis=1)
    neg_score = jnp.sum(pick_negative * own_scores[:, None, :], axis=2)
    margins = MARGIN - pos_score[:, None] + neg_score
    numerator = jnp.sum(mask_float * jax.nn.softplus(margins))
    factor = mask_float * jax.nn.sigmoid(margins) / pair_floor
    grad_own = (
        jnp.sum(factor[:, :, None] * pick_negative, axis=1)
        - jnp.sum(factor, axis=1)[:, None] * pick_positive
    )
    grad_group = lax.all_gather(grad_own, "psg", axis=0, tiled=True)
    grad_local = lax.dynamic_slice_in_dim(grad_group, member * PPD, PPD, 1)

    grad_own_split = grad_own.reshape(queries, 1, members, PPD).transpose(2, 0, 1, 3)
    ratio_own = (
        (TEMPER * grad_own_split) / totals_own.reshape(members, queries, SEG, PPD)
    ).reshape(members, query_rows, PPD)
    spread_own = jnp.einsum(
        "mqp,mtp->mqt", ratio_own.astype(BF), group_hot, preferred_element_type=F32
    )
    sims_own = (spread_own * weighted_own / TEMPER).astype(BF)
    grad_unit_query = jnp.einsum(
        "mqt,mtd->qd", sims_own, group_passage, preferred_element_type=F32
    )
    ratio = (
        (TEMPER * grad_local[:, None, :]) / totals.reshape(members * queries, SEG, PPD)
    ).reshape(members * query_rows, PPD)
    sims = (contract_cols(ratio.astype(BF), passage_hot) * weighted / TEMPER).astype(BF)
    grad_unit_passage = contract_rows(sims, group_query)
    grad_unit = jnp.concatenate([grad_unit_passage, grad_unit_query])

    picks = one_hot(assignments[0], NCENT)
    centroid_part = contract_rows(picks, own_passage)
    count_part = jnp.sum(picks.astype(F32), axis=0)
    (
        grad_proj,
        grad_two_low,
        grad_inner,
        grad_sum_one,
        grad_one_low,
        grad_context,
        sums,
        grad_bias_up,
    ) = token_call(
        middle_back_kernel,
        count,
        [by_tokens(DC), by_tokens(DC), by_tokens(1), by_tokens(D), by_tokens(1)]
        + [by_tokens(inner_width), by_tokens(D), by_tokens(1), resident(16, D), *weight_specs],
        [(None, DC, BF), (None, D, BF), (None, inner_width, BF), (None, D, F32)]
        + [(None, D, BF), (None, D, BF), (8, D, F32), (1, inner_width, F32)],
        middle_flops,
    )(
        grad_unit,
        unit,
        scale_inverse,
        norm_two,
        inverse_two,
        slope,
        norm_one,
        inverse_one,
        vectors,
        *weights,
    )
    grad_head = contract_rows(input_two, grad_proj)
    grad_attn = attention_backward(
        segment_column, segment_windows, mixed, grad_context, kept, grad_one_low
    )
    grad_low, grad_positions, sums_zero = token_call(
        first_back_kernel,
        count,
        [by_tokens(3 * D), by_tokens(D), by_tokens(D), by_tokens(1), by_tokens(1)]
        + [resident(16, D), resident(3 * D, D)],
        [(None, D, BF), (PMAX, D, F32), (8, D, F32)],
        2 * count * D * (3 * D + PMAX),
    )(grad_attn, grad_sum_one, norm_zero, inverse_zero, place_column, vectors, attn_rows)
    grad_slots = contract_rows(slot_hot, grad_low).astype(BF).reshape(devices, capacity, D)
    grad_small = jnp.concatenate(
        [
            grad_positions.reshape(-1),
            sums_zero[:4].reshape(-1),
            sums[5],
            sums[3],
            sums[4],
            sums[2],
            sums[0],
            sums[1],
            grad_bias_up[0],
        ]
    )

    def side_by_side(parts, sublanes):
        joined = jnp.concatenate([p.reshape(devices, -1) for p in parts], axis=1)
        joined = jnp.pad(joined, ((0, 0), (0, -joined.shape[1] % (sublanes * 128))))
        return joined.reshape(devices, -1, 128)

    lefts = [grad_attn, grad_inner, activated]
    rights = [input_zero, context, input_one, grad_two_low]
    others = [
        side_by_side([centroid_part.astype(BF), grad_head.astype(BF)], 16),
        side_by_side([grad_small, count_part, jnp.broadcast_to(numerator, (devices, 1))], 8),
    ]
    if members * matrix_rows % 128 == 0 and members == 4:
        reduced, grad_slots = reduce_products(lefts, rights, others, grad_slots)
    else:
        right_of = [rights[:2], rights[2:3], rights[3:]]
        sums = []
        for left, right in zip(lefts, right_of):
            if len(right) == 2:
                rows = jnp.concatenate(
                    [
                        contract_rows(left[:, : 3 * D], right[0]),
                        contract_rows(left[:, 3 * D :], right[1]),
                    ]
                )
            else:
                rows = contract_rows(left, right[0])
            rows = rows.astype(BF).reshape(devices, matrix_rows, D)
            sums.append(jnp.pad(rows, ((0, 0), (0, -matrix_rows % 16), (0, 0))))
        reduced, grad_slots = reduce_all(sums + others, grad_slots)
    attn_reduced, up_reduced, down_reduced = (r[:matrix_rows] for r in reduced[:3])
    wide, fine = reduced[3].reshape(-1), reduced[4].reshape(-1)
    centroid_rows = NCENT // devices
    centroid_sums = wide[: centroid_rows * DC].reshape(centroid_rows, DC)
    head_reduced = wide[centroid_rows * DC :][: head_rows * DC].reshape(head_rows, DC)
    small_reduced = fine[:small_size]
    centroid_counts = fine[small_size:][:centroid_rows]
    loss = fine[small_size + centroid_rows] / pair_floor

    def whole_table():
        table = jnp.zeros((shard_rows * devices, D), F32).at[tokens].add(grad_low.astype(F32))
        return lax.psum_scatter(table, ALL, scatter_dimension=0, tiled=True)

    def own_rows():
        slots = jnp.arange(capacity, dtype=jnp.int32).astype(F32)
        picked = (asked_rank[:, None, :] == slots[None, :, None]).astype(BF)
        return contract_rows(
            picked.reshape(devices * capacity, shard_rows),
            grad_slots.reshape(devices * capacity, D),
        )

    table_reduced = lax.cond(
        overflow,
        whole_table,
        own_rows,
    )

    count_steps = step_count[0].astype(F32)
    attn_reduced = attn_reduced.T
    up_reduced = up_reduced.T
    table_new, table_second_new = adam_update(
        embed_table, embed_table_moment, embed_table_second, table_reduced, RATE_TABLE, count_steps
    )
    attn_new, attn_second_new = adam_update(
        attention_weight,
        attention_weight_moment,
        attention_weight_second,
        attn_reduced,
        RATE_MATRIX,
        count_steps,
    )
    up_new, up_second_new = adam_update(
        up_weight, up_weight_moment, up_weight_second, up_reduced, RATE_MATRIX, count_steps
    )
    down_new, down_second_new = adam_update(
        down_weight, down_weight_moment, down_weight_second, down_reduced, RATE_MATRIX, count_steps
    )
    head_new, head_second_new = adam_update(
        head_weight, head_weight_moment, head_weight_second, head_reduced, RATE_MATRIX, count_steps
    )
    small_new, small_second_new = adam_update(
        small_params, small_params_moment, small_params_second, small_reduced, RATE_TABLE, count_steps
    )
    return (
        loss,
        centroid_sums,
        centroid_counts,
        table_new,
        table_reduced,
        table_second_new,
        attn_new,
        attn_reduced,
        attn_second_new,
        up_new,
        up_reduced,
        up_second_new,
        down_new,
        down_reduced,
        down_second_new,
        head_new,
        head_reduced,
        head_second_new,
        small_new,
        small_reduced,
        small_second_new,
    )


def solution(mesh):
    in_specs = (
        P(("grp", "psg"), None),
        P(("grp", "psg"), None),
        P(("grp", "psg"), None),
        P(("grp", "psg")),
        P(("grp", "psg"), None),
        P(("grp", "psg"), None),
        P(("grp", "psg"), None),
        P(),
        P(("grp", "psg"), None),
        P(("grp", "psg"), None),
        P(("grp", "psg"), None),
        P(None, ("grp", "psg")),
        P(None, ("grp", "psg")),
        P(None, ("grp", "psg")),
        P(None, ("grp", "psg")),
        P(None, ("grp", "psg")),
        P(None, ("grp", "psg")),
        P(("grp", "psg"), None),
        P(("grp", "psg"), None),
        P(("grp", "psg"), None),
        P(("grp", "psg"), None),
        P(("grp", "psg"), None),
        P(("grp", "psg"), None),
        P(("grp", "psg")),
        P(("grp", "psg")),
        P(("grp", "psg")),
    )
    out_specs = (
        P(),
        P(("grp", "psg"), None),
        P(("grp", "psg")),
        P(("grp", "psg"), None),
        P(("grp", "psg"), None),
        P(("grp", "psg"), None),
        P(None, ("grp", "psg")),
        P(None, ("grp", "psg")),
        P(None, ("grp", "psg")),
        P(None, ("grp", "psg")),
        P(None, ("grp", "psg")),
        P(None, ("grp", "psg")),
        P(("grp", "psg"), None),
        P(("grp", "psg"), None),
        P(("grp", "psg"), None),
        P(("grp", "psg"), None),
        P(("grp", "psg"), None),
        P(("grp", "psg"), None),
        P(("grp", "psg")),
        P(("grp", "psg")),
        P(("grp", "psg")),
    )
    return jax.shard_map(
        on_device, mesh=mesh, in_specs=in_specs, out_specs=out_specs, check_vma=False
    )
```

```python
import math

import jax
import jax.numpy as jnp
from jax import lax
from jax.experimental import pallas as pl
from jax.experimental.pallas import tpu as pltpu
from jax.sharding import PartitionSpec as P

D = 768
HEADS = 12
HD = 64
SEG = 32
PMAX = 64
ROW = 1024
PPD = 32
QDEV = 8
NCENT = 1024
DC = 128
BLK = 128
WIN = 256
ALL = ("grp", "psg")
BF = jnp.bfloat16
F32 = jnp.float32
MARK = 1e30


TEMPER = 0.2
MARGIN = 1.0
NORM_EPS = 1e-06
BETA_ONE = 0.9
BETA_TWO = 0.999
ADAM_EPS = 1e-08
WEIGHT_DECAY = 0.01
RATE_MATRIX = 0.01
RATE_TABLE = 0.1


def matmul(lhs_mat, rhs_mat):
    return jnp.dot(lhs_mat, rhs_mat, preferred_element_type=jnp.float32)


def contract_rows(lhs_mat, rhs_mat):
    return lax.dot_general(
        lhs_mat, rhs_mat, (((0,), (0,)), ((), ())), preferred_element_type=jnp.float32
    )


def contract_cols(lhs_mat, rhs_mat):
    return lax.dot_general(
        lhs_mat, rhs_mat, (((1,), (1,)), ((), ())), preferred_element_type=jnp.float32
    )


def layer_norm(values, scale_gain, shift_bias):
    average = jnp.mean(values, axis=-1, keepdims=True)
    centered = values - average
    inverse = lax.rsqrt(jnp.mean(centered * centered, axis=-1, keepdims=True) + NORM_EPS)
    normed = centered * inverse
    return (normed * (1.0 + scale_gain) + shift_bias, (normed, inverse))


def norm_back(upstream, stored, scale_gain):
    normed, inverse = stored
    scaled = upstream * (1.0 + scale_gain)
    back = inverse * (
        scaled
        - jnp.mean(scaled, axis=-1, keepdims=True)
        - normed * jnp.mean(scaled * normed, axis=-1, keepdims=True)
    )
    return (back, jnp.sum(upstream * normed, axis=0), jnp.sum(upstream, axis=0))


def starts_of(lengths):
    order = jnp.arange(PPD, dtype=jnp.int32)
    before = (order[:, None] > order[None, :]).astype(jnp.int32)
    return jnp.sum(before * lengths[..., None, :], axis=-1)


def layout_of(lengths):
    starts = starts_of(lengths)
    place = jnp.arange(ROW, dtype=jnp.int32)
    above = (place[:, None] >= starts[..., None, :]).astype(jnp.int32)
    segment = jnp.sum(above, axis=-1) - 1
    begin = jnp.max(above * starts[..., None, :], axis=-1)
    return segment, place - begin


def one_hot(index, depth):
    return (index[..., None] == jnp.arange(depth, dtype=jnp.int32)).astype(BF)


def split_two(values):
    high = lax.reduce_precision(values, 8, 7)
    return high.astype(BF), (values - high).astype(BF)


def split_three(values):
    high = lax.reduce_precision(values, 8, 7)
    middle = lax.reduce_precision(values - high, 8, 7)
    return high.astype(BF), middle.astype(BF), (values - high - middle).astype(BF)


def window_start(block, count):
    return min(max(block * BLK - (WIN - BLK) // 2, 0), count - WIN)


def attn_forward_kernel(count, segc_ref, segw_ref, z_ref, o_ref, lse_ref):
    block = pl.program_id(0)
    row = pl.multiple_of(block * BLK, BLK)
    first = pl.multiple_of(jnp.clip(row - (WIN - BLK) // 2, 0, count - WIN), 64)
    allowed = segc_ref[...] == segw_ref[0]
    lane = lax.broadcasted_iota(jnp.int32, (BLK, 2 * HD), 1)
    lane_head = lax.broadcasted_iota(jnp.int32, (BLK, 128), 1)
    kept = jnp.zeros((BLK, 128), F32)
    for pair in range(HEADS // 2):
        at = pair * 2 * HD
        query = z_ref[pl.ds(row, BLK), at : at + 2 * HD] * BF(HD ** (-0.5))
        key = z_ref[pl.ds(first, WIN), D + at : D + at + 2 * HD]
        value = z_ref[pl.ds(first, WIN), 2 * D + at : 2 * D + at + 2 * HD]
        parts = []
        for half in range(2):
            mine = (lane >= half * HD) & (lane < (half + 1) * HD)
            scores = contract_cols(jnp.where(mine, query, BF(0)), key)
            scores = jnp.where(allowed, scores, -1000000000.0)
            top = jnp.max(scores, axis=-1, keepdims=True)
            weight = jnp.exp(scores - top)
            total = jnp.sum(weight, axis=-1, keepdims=True)
            probs = (weight * (1.0 / total)).astype(BF)
            parts.append(matmul(probs, value))
            kept = jnp.where(lane_head == 2 * pair + half, top + jnp.log(total), kept)
        o_ref[:, at : at + 2 * HD] = jnp.where(lane < HD, parts[0], parts[1]).astype(BF)
    lse_ref[...] = kept.T[:16]


def attn_backward_kernel(
    count, blocks, segr_ref, segw_ref, z_ref, do_ref, lse_ref, one_ref, dz_ref, dk_ref, dv_ref
):
    block = pl.program_id(0)
    row = pl.multiple_of(block * BLK, BLK)
    first = pl.multiple_of(jnp.clip(row - (WIN - BLK) // 2, 0, count - WIN), 64)

    @pl.when(block == 0)
    def _():
        dk_ref[...] = jnp.zeros_like(dk_ref)
        dv_ref[...] = jnp.zeros_like(dv_ref)

    allowed = segw_ref[0] == segr_ref[0]
    lane = lax.broadcasted_iota(jnp.int32, (BLK, 2 * HD), 1)
    for pair in range(HEADS // 2):
        at = pair * 2 * HD
        query = z_ref[pl.ds(row, BLK), at : at + 2 * HD] * BF(HD ** (-0.5))
        key = z_ref[pl.ds(first, WIN), D + at : D + at + 2 * HD]
        value = z_ref[pl.ds(first, WIN), 2 * D + at : 2 * D + at + 2 * HD]
        upstream = do_ref[:, at : at + 2 * HD]
        grad_query = []
        grad_key = jnp.zeros((WIN, 2 * HD), F32)
        grad_value = jnp.zeros((WIN, 2 * HD), F32)
        for half in range(2):
            mine = (lane >= half * HD) & (lane < (half + 1) * HD)
            query_own = jnp.where(mine, query, BF(0))
            up_own = jnp.where(mine, upstream, BF(0))
            head = 2 * pair + half
            scores = jnp.where(allowed, contract_cols(key, query_own), -1000000000.0)
            probs = jnp.exp(scores - lse_ref[head : head + 1, :])
            grad_probs = contract_cols(value, up_own)
            grad_value = grad_value + matmul(probs.astype(BF), up_own)
            inner = jnp.sum(grad_probs * probs, axis=0, keepdims=True)
            grad_scores = (probs * (grad_probs - inner)).astype(BF)
            grad_query.append(contract_rows(grad_scores, key))
            grad_key = grad_key + matmul(grad_scores, query_own)
        own = jnp.where(lane < HD, grad_query[0], grad_query[1]) * HD ** (-0.5)
        dz_ref[pl.ds(row, BLK), at : at + 2 * HD] = own.astype(BF)
        dk_ref[pl.ds(first, WIN), at : at + 2 * HD] += grad_key
        dv_ref[pl.ds(first, WIN), at : at + 2 * HD] += grad_value

    dz_ref[pl.ds(row, BLK), 3 * D :] = one_ref[...]

    @pl.when(block == blocks - 1)
    def _():
        dz_ref[:, D : 2 * D] = dk_ref[...].astype(BF)
        dz_ref[:, 2 * D : 3 * D] = dv_ref[...].astype(BF)


def attention_specs(count):
    return [
        pl.BlockSpec((BLK, 1), lambda i: (i, 0)),
        pl.BlockSpec((1, 1, WIN), lambda i: (i, 0, 0)),
        pl.BlockSpec((count, 3 * D), lambda i: (0, 0)),
    ]


def attention_forward(segment_column, segment_windows, mixed):
    count = mixed.shape[0]
    blocks = count // BLK
    return pl.pallas_call(
        lambda *refs: attn_forward_kernel(count, *refs),
        grid=(blocks,),
        in_specs=attention_specs(count),
        out_specs=[
            pl.BlockSpec((BLK, D), lambda i: (i, 0)),
            pl.BlockSpec((16, BLK), lambda i: (0, i)),
        ],
        out_shape=[
            jax.ShapeDtypeStruct((count, D), BF),
            jax.ShapeDtypeStruct((16, count), F32),
        ],
        compiler_params=pltpu.CompilerParams(vmem_limit_bytes=40 * 2**20),
        cost_estimate=pl.CostEstimate(
            flops=4 * count * WIN * 128 * HEADS, bytes_accessed=12000000, transcendentals=0
        ),
    )(segment_column, segment_windows, mixed)


def attention_backward(segment_rows, segment_windows, mixed, upstream, kept, beside):
    count = mixed.shape[0]
    blocks = count // BLK
    return pl.pallas_call(
        lambda *refs: attn_backward_kernel(count, blocks, *refs),
        grid=(blocks,),
        in_specs=[
            pl.BlockSpec((1, 1, BLK), lambda i: (i, 0, 0)),
            pl.BlockSpec((1, WIN, 1), lambda i: (i, 0, 0)),
            pl.BlockSpec((count, 3 * D), lambda i: (0, 0), pipeline_mode=pl.Buffered(1)),
            pl.BlockSpec((BLK, D), lambda i: (i, 0)),
            pl.BlockSpec((16, BLK), lambda i: (0, i)),
            pl.BlockSpec((BLK, D), lambda i: (i, 0)),
        ],
        out_specs=pl.BlockSpec((count, 4 * D), lambda i: (0, 0)),
        out_shape=jax.ShapeDtypeStruct((count, 4 * D), BF),
        scratch_shapes=[pltpu.VMEM((count, D), F32), pltpu.VMEM((count, D), F32)],
        compiler_params=pltpu.CompilerParams(vmem_limit_bytes=56 * 2**20),
        cost_estimate=pl.CostEstimate(
            flops=10 * count * WIN * 128 * HEADS, bytes_accessed=18000000, transcendentals=0
        ),
    )(segment_rows, segment_windows, mixed, upstream, kept, beside)


def place_of():
    return lax.axis_index("grp") * lax.axis_size("psg") + lax.axis_index("psg")


def mesh_place(place):
    members = lax.axis_size("psg")
    return (place // members, place % members)


def flipped(place, mask):
    result, bit = place, 0
    while mask >> bit:
        if (mask >> bit) & 1:
            result = result + (1 - 2 * ((place // (1 << bit)) % 2)) * (1 << bit)
        bit += 1
    return result


def greet_all(devices, me):
    barrier = pltpu.get_barrier_semaphore()

    @pl.loop(1, devices)
    def _(i):
        pl.semaphore_signal(
            barrier,
            inc=1,
            device_id=mesh_place((me + i) % devices),
            device_id_type=pl.DeviceIdType.MESH,
        )

    pl.semaphore_wait(barrier, devices - 1)


def gather_plan(order, group):
    held, steps = [0], []
    for bit in order:
        fresh = [(1 << bit) | m for m in held]
        steps.append([fresh[i : i + group] for i in range(0, len(fresh), group)])
        held = held + fresh
    return steps


def earlier_rows(width):
    above = lax.broadcasted_iota(jnp.int32, (width, width), 0)
    return (above < lax.broadcasted_iota(jnp.int32, (width, width), 1)).astype(F32).astype(BF)


def rank_rows(asked, earlier, rank_ref):
    width = earlier.shape[0]
    asked = jnp.concatenate([asked[:, j, :] for j in range(width // 128)], axis=1)
    rank_ref[...] = jnp.where(asked > 0.5, matmul(asked.astype(BF), earlier), -1.0)
    return jnp.max(jnp.sum(asked, axis=1, keepdims=True), axis=0, keepdims=True)


def pack_rows(places, slot, most, table, rank_ref, packed_ref):
    capacity, width = packed_ref.shape[1], table.shape[0]
    at = lax.broadcasted_iota(jnp.int32, (capacity, width), 0).astype(F32)
    picked = [
        jnp.where(rank_ref[pl.ds(place, 1), :] == at, 1.0, 0.0).astype(BF) for place in places
    ]
    rows = matmul(jnp.concatenate(picked), table[...]).reshape(len(places), capacity, D)
    last = lax.broadcasted_iota(jnp.int32, (len(places), capacity, D), 1) == capacity - 1
    rows = jnp.where(last & (most > capacity)[:, :, None], MARK, rows)
    packed_ref[slot : slot + len(places)] = rows.astype(BF)


def gather_kernel(devices, pieces, *refs):
    matrices = 4
    sources, (needed, table) = refs[:matrices], refs[matrices : matrices + 2]
    outs, (rows_out, rank) = refs[6:10], refs[10:12]
    asked, earlier, packed, arrive, beside, leave, local, ask_sem, rows_sem = refs[12:]
    me = place_of()
    group = max(devices // 8, 1)
    greet_all(devices, me)

    def push(source, target_ref, target, send, recv):
        pltpu.make_async_remote_copy(
            src_ref=source,
            dst_ref=target_ref,
            send_sem=send,
            recv_sem=recv,
            device_id=mesh_place(target),
            device_id_type=pl.DeviceIdType.MESH,
        ).start()

    def settle(some, semaphore):
        pltpu.make_async_copy(some, some, semaphore).wait()

    @pl.loop(1, devices)
    def _(i):
        target = (me + i) % devices
        push(needed.at[target], asked.at[me], target, ask_sem.at[0], ask_sem.at[1])

    def start(piece, mask, target, semaphore):
        which, first, rows, _ = pieces[piece]
        there = outs[which].at[flipped(me, mask), pl.ds(first, rows)]
        here = sources[which].at[pl.ds(first, rows)] if mask == 0 else there
        push(here, there, flipped(me, target), leave.at[piece], semaphore)

    def wait(piece, blocks, semaphore):
        which, first, rows, _ = pieces[piece]
        settle(outs[which].at[pl.ds(0, blocks), pl.ds(first, rows)], semaphore)

    plans, numbers = [], []
    for piece in range(len(pieces)):
        plan = gather_plan(pieces[piece][3], group)
        number, count = {}, 0
        for groups in plan:
            for masks in groups:
                for mask in masks:
                    number[mask] = count
                count += 1
        plans.append(plan)
        numbers.append(number)

    def send_on(piece, mask, after):
        order = pieces[piece][3]
        for step in range(after + 1, len(order)):
            target = 1 << order[step]
            start(piece, mask, target, arrive.at[piece, numbers[piece][mask | target]])
        start(piece, mask, 1, beside.at[piece])

    def pass_on(piece, step):
        for masks in plans[piece][step]:
            wait(piece, len(masks), arrive.at[piece, numbers[piece][masks[0]]])
            for mask in masks:
                send_on(piece, mask, step)

    for piece in range(len(pieces)):
        send_on(piece, 0, -1)

    own = [
        pltpu.make_async_copy(source, out.at[me], local.at[i])
        for i, (source, out) in enumerate(zip(sources, outs))
    ]
    own_asked = pltpu.make_async_copy(needed.at[me], asked.at[me], local.at[matrices])
    for copy in own:
        copy.start()
    own_asked.start()
    earlier[...] = earlier_rows(table.shape[0])
    for piece in range(len(pieces)):
        pass_on(piece, 0)
    own_asked.wait()
    for i in range(2):
        settle(asked.at[pl.ds(0, devices - 1)], ask_sem.at[i])
    most = rank_rows(asked[...], earlier[...], rank)

    masks = sorted(range(devices), key=lambda m: -bin(m).count("1"))
    steps = len(pieces[0][3])
    each = -(-(devices - 1) // (len(pieces) * (steps - 1)))
    kept_rows = pltpu.make_async_copy(
        packed.at[devices - 1], rows_out.at[me], local.at[matrices + 1]
    )
    sent, made, together = 0, 0, 8
    for step in range(1, steps):
        for piece in range(len(pieces)):
            now = min(sent + each, devices)
            while made < now:
                group_now = masks[made : made + together]
                places = [flipped(me, m) for m in group_now]
                pack_rows(places, made, most, table, rank, packed)
                made += together
            pass_on(piece, step)
            for i in range(sent, now):
                target = flipped(me, masks[i])
                if masks[i]:
                    push(packed.at[i], rows_out.at[me], target, rows_sem.at[0], rows_sem.at[1])
                else:
                    kept_rows.start()
            sent = now
    for piece in range(len(pieces)):
        wait(piece, devices // 2, beside.at[piece])
        wait(piece, devices - 1, leave.at[piece])
    for copy in own:
        copy.wait()
    kept_rows.wait()
    for i in range(2):
        settle(rows_out.at[pl.ds(0, devices - 1)], rows_sem.at[i])


def gather_all(sources, needed, table, capacity):
    devices = needed.shape[0]
    rows = sources[0].shape[0]
    bits = devices.bit_length() - 1
    high = list(range(3, bits))[::-1]
    one, other = (*high, 2, 1), (*high, 1, 2)
    cut = rows // 32 * 16
    pieces = [(0, 0, rows, one), (2, 0, rows, other), (1, cut, rows - cut, one)]
    if cut:
        pieces.append((1, 0, cut, other))
    pieces.append((3, 0, sources[3].shape[0], one))
    count = max(sum(map(len, gather_plan(p[3], max(devices // 8, 1)))) for p in pieces)
    anywhere = pl.BlockSpec(memory_space=pl.ANY)
    inside = pl.BlockSpec(memory_space=pltpu.VMEM)
    dma = pltpu.SemaphoreType.DMA
    *gathered, arrived, rank = pl.pallas_call(
        lambda *refs: gather_kernel(devices, pieces, *refs),
        in_specs=[anywhere] * 4 + [inside] * 2,
        out_specs=[anywhere] * 5 + [inside],
        out_shape=[jax.ShapeDtypeStruct((devices, *s.shape), s.dtype) for s in sources]
        + [
            jax.ShapeDtypeStruct((devices, capacity, D), BF),
            jax.ShapeDtypeStruct((devices, table.shape[0]), F32),
        ],
        scratch_shapes=[
            pltpu.VMEM(needed.shape, F32),
            pltpu.VMEM((table.shape[0], table.shape[0]), BF),
            pltpu.VMEM((devices, capacity, D), BF),
            dma((len(pieces), count)),
            dma((len(pieces),)),
            dma((len(pieces),)),
            dma((6,)),
            dma((2,)),
            dma((2,)),
        ],
        compiler_params=pltpu.CompilerParams(
            collective_id=0, has_side_effects=True, vmem_limit_bytes=48 * 2**20
        ),
    )(*sources, needed, table)
    return gathered, arrived, rank


def reduce_plan(order, group):
    held = [0]
    for bit in reversed(order):
        held = [m | (1 << bit) for m in held] + held
    steps = []
    for step in range(len(order) + 1):
        if step:
            held = [m for m in held if not (m >> order[step - 1]) & 1]
        steps.append([held[i : i + group] for i in range(0, len(held), group)])
    return steps


def reduce_kernel(devices, pieces, spread, *refs):
    count = len({p[0] for p in pieces})
    sources, rows_in = refs[:count], refs[count]
    outs, rows_out = refs[count + 1 : 2 * count + 1], refs[2 * count + 1]
    held, landed = refs[2 * count + 2 : 3 * count + 2], refs[3 * count + 2 : 4 * count + 2]
    arrive, leave, load, rows_sem, own_sem = refs[4 * count + 2 :]
    me = place_of()
    group = max(devices // 16, 1)
    greet_all(devices, me)

    def push(source, target_ref, target, send, recv):
        pltpu.make_async_remote_copy(
            src_ref=source,
            dst_ref=target_ref,
            send_sem=send,
            recv_sem=recv,
            device_id=mesh_place(target),
            device_id_type=pl.DeviceIdType.MESH,
        ).start()

    def settle(some, semaphore):
        pltpu.make_async_copy(some, some, semaphore).wait()

    plans, slots, places, numbers = [], [], [], []
    for piece in pieces:
        plan = reduce_plan(piece[3], group)
        slots.append({m: i for i, m in enumerate(sum(plan[0], []))})
        place, number, at, count = {}, {}, 0, 0
        for step, groups in enumerate(plan):
            for masks in groups:
                for mask in masks:
                    place[step, mask], number[step, mask] = at, count
                    at += 1
                count += 1
        plans.append(plan)
        places.append(place)
        numbers.append(number)

    def rows_of(piece):
        return pl.ds(pieces[piece][1], pieces[piece][2])

    def send(piece, step, mask, bit, source):
        which = pieces[piece][0]
        kept = mask & ~(1 << bit)
        push(
            source,
            landed[which].at[places[piece][step, kept], rows_of(piece)],
            flipped(me, 1 << bit),
            leave.at[piece],
            arrive.at[piece, numbers[piece][step, kept]],
        )

    order = sorted(range(1, devices), key=lambda m: -bin(m).count("1"))

    def send_rows(amount):
        for _ in range(min(amount, len(order))):
            target = flipped(me, order.pop(0))
            push(rows_in.at[target], rows_out.at[me], target, rows_sem.at[0], rows_sem.at[1])

    own_rows = pltpu.make_async_copy(rows_in.at[me], rows_out.at[me], own_sem)
    own_rows.start()
    send_rows(spread[0])
    for masks in plans[0][0]:
        for piece in range(len(pieces)):
            which = pieces[piece][0]
            for mask in plans[piece][0][plans[0][0].index(masks)]:
                source = sources[which].at[flipped(me, mask | 1), rows_of(piece)]
                send(piece, 0, mask | 1, 0, source)
    for piece in range(len(pieces)):
        which = pieces[piece][0]
        for mask in slots[piece]:
            pltpu.make_async_copy(
                sources[which].at[flipped(me, mask), rows_of(piece)],
                held[which].at[slots[piece][mask], rows_of(piece)],
                load.at[piece],
            ).start()
    turn = 1
    for step in range(len(pieces[0][3]) + 1):
        for at in range(len(plans[0][step])):
            for piece in range(len(pieces)):
                which, _, _, bits = pieces[piece]
                rows = rows_of(piece)
                if step == 0 and at == 0:
                    settle(held[which].at[pl.ds(0, devices // 2), rows], load.at[piece])
                masks = plans[piece][step][at]
                some = landed[which].at[pl.ds(0, len(masks)), rows]
                settle(some, arrive.at[piece, numbers[piece][step, masks[0]]])
                for mask in masks:
                    slot = slots[piece][mask]
                    total = held[which][slot, rows].astype(F32)
                    total = total + landed[which][places[piece][step, mask], rows].astype(F32)
                    if step == len(bits):
                        outs[which][rows] = total
                        continue
                    held[which][slot, rows] = total.astype(held[which].dtype)
                    if (mask >> bits[step]) & 1:
                        send(piece, step + 1, mask, bits[step], held[which].at[slot, rows])
            send_rows(spread[turn] if turn < len(spread) else 0)
            turn += 1
    send_rows(devices)
    for piece in range(len(pieces)):
        which = pieces[piece][0]
        settle(landed[which].at[pl.ds(0, devices - 1), rows_of(piece)], leave.at[piece])
    own_rows.wait()
    for i in range(2):
        settle(rows_out.at[pl.ds(0, devices - 1)], rows_sem.at[i])


def reduce_all(sources, rows_in):
    devices = rows_in.shape[0]
    bits = devices.bit_length() - 1
    high = list(range(3, bits))
    one, other = (1, 2, *high), (2, 1, *high)
    pieces = []
    for i in (0, 2, 1, 3, 4):
        rows = sources[i].shape[1]
        cut = rows // 32 * 16 if i == 1 else 0
        pieces.append((i, cut, rows - cut, one if i in (0, 1, 3) else other))
        if cut:
            pieces.append((i, 0, cut, other))
    spread = [6] + [2] * devices
    count = max(sum(map(len, reduce_plan(p[3], max(devices // 16, 1)))) for p in pieces)
    anywhere = pl.BlockSpec(memory_space=pl.ANY)
    inside = pl.BlockSpec(memory_space=pltpu.VMEM)
    dma = pltpu.SemaphoreType.DMA
    *reduced, arrived = pl.pallas_call(
        lambda *refs: reduce_kernel(devices, pieces, spread, *refs),
        in_specs=[anywhere] * (len(sources) + 1),
        out_specs=[inside] * len(sources) + [anywhere],
        out_shape=[jax.ShapeDtypeStruct(s.shape[1:], F32) for s in sources]
        + [jax.ShapeDtypeStruct(rows_in.shape, rows_in.dtype)],
        scratch_shapes=[pltpu.VMEM((devices // 2, *s.shape[1:]), s.dtype) for s in sources]
        + [pltpu.VMEM((devices - 1, *s.shape[1:]), s.dtype) for s in sources]
        + [dma((len(pieces), count)), dma((len(pieces),)), dma((len(pieces),)), dma((2,)), dma],
        compiler_params=pltpu.CompilerParams(
            collective_id=1, has_side_effects=True, vmem_limit_bytes=48 * 2**20
        ),
    )(*sources, rows_in)
    return reduced, arrived


def product_kernel(devices, pieces, spread, *refs):
    count, computed = len({p[0] for p in pieces}), 3
    lefts, rights, others, rows_in = refs[:3], refs[3:7], refs[7 : count + 4], refs[count + 4]
    refs = refs[count + 5 :]
    outs, rows_out = refs[:count], refs[count]
    held, landed = refs[count + 1 : 2 * count + 1], refs[2 * count + 1 : 3 * count + 1]
    refs = refs[3 * count + 1 :]
    ready, refs = refs[:computed], refs[computed:]
    slab, slab_sem, arrive, leave, load, rows_sem, own_sem = refs
    me = place_of()
    groups = devices // 4
    half = groups // 2
    depth = groups.bit_length() - 1
    chunk = outs[0].shape[0]
    greet_all(devices, me)

    def push(source, target_ref, target, send, recv):
        pltpu.make_async_remote_copy(
            src_ref=source,
            dst_ref=target_ref,
            send_sem=send,
            recv_sem=recv,
            device_id=mesh_place(target),
            device_id_type=pl.DeviceIdType.MESH,
        ).start()

    def settle(some, semaphore):
        pltpu.make_async_copy(some, some, semaphore).wait()

    plans, slots, places = [], [], []
    for piece in pieces:
        plan = [sum(step, []) for step in reduce_plan(piece[3], 1)]
        slots.append({m: i for i, m in enumerate(plan[0])})
        place, at = {}, 0
        for step, masks in enumerate(plan):
            for mask in masks:
                place[step, mask] = at
                at += 1
        plans.append(plan)
        places.append(place)

    def rows_of(piece):
        return pl.ds(pieces[piece][1], pieces[piece][2])

    def send(piece, step, mask, bit, source):
        where = places[piece][step, mask & ~(1 << bit)]
        push(
            source,
            landed[pieces[piece][0]].at[where, rows_of(piece)],
            flipped(me, 1 << bit),
            leave.at[piece],
            arrive.at[piece, where],
        )

    order = sorted(range(1, devices), key=lambda m: -bin(m).count("1"))

    def send_rows(amount):
        for _ in range(min(amount, len(order))):
            target = flipped(me, order.pop(0))
            push(rows_in.at[target], rows_out.at[me], target, rows_sem.at[0], rows_sem.at[1])

    def group_of(turn):
        own, place = me // 4, 0
        for bit in range(depth):
            differs = 1 - (turn // (1 << (depth - 1 - bit))) % 2
            place = place + ((own // (1 << bit) + differs) % 2) * (1 << bit)
        return place

    def slab_copy(which, turn):
        width = 4 * chunk
        columns = pl.ds(pl.multiple_of(group_of(turn) * width, width), width)
        return pltpu.make_async_copy(
            lefts[which].at[:, columns],
            slab.at[turn % 2, which],
            slab_sem.at[turn % 2, which],
        )

    def slot_of(piece, turn, side):
        slot = 0
        for bit in pieces[piece][3]:
            digit = 1 - side if bit == 1 else (turn // (1 << (depth + 1 - bit))) % 2
            slot = slot * 2 + digit
        return slot

    big = [p for p in range(len(pieces)) if pieces[p][0] < computed]
    small = [p for p in range(len(pieces)) if pieces[p][0] >= computed]
    own_rows = pltpu.make_async_copy(rows_in.at[me], rows_out.at[me], own_sem)
    own_rows.start()
    for which in range(computed):
        slab_copy(which, 0).start()
    send_rows(spread[0])
    for piece in small:
        source = others[pieces[piece][0] - computed]
        for mask in plans[piece][0]:
            send(piece, 0, mask | 1, 0, source.at[flipped(me, mask | 1)])
            pltpu.make_async_copy(
                source.at[flipped(me, mask)],
                held[pieces[piece][0]].at[slots[piece][mask]],
                load.at[piece],
            ).start()

    near = (me // 2) % 2
    core = me % 2

    def add(piece, slot, where):
        which, rows = pieces[piece][0], rows_of(piece)
        some = landed[which].at[pl.ds(where, 1), rows]
        settle(some, arrive.at[piece, where])
        total = held[which][slot, rows].astype(F32)
        return total + landed[which][where, rows].astype(F32)

    def first_add(turn):
        for side in (1, 0):
            for piece in big:
                which, rows, bits = pieces[piece][0], rows_of(piece), pieces[piece][3]
                slot = slot_of(piece, turn, side)
                line = (near + side) % 2
                settle(landed[which].at[pl.ds(slot, 1), rows], arrive.at[piece, slot])
                total = ready[which][turn * 4 + line * 2 + core, rows].astype(F32)
                total = total + landed[which][slot, rows].astype(F32)
                held[which][slot, rows] = total.astype(BF)

                def on():
                    sent = len(plans[piece][0])
                    push(
                        held[which].at[slot, rows],
                        landed[which].at[sent + slot, rows],
                        flipped(me, 1 << bits[0]),
                        leave.at[piece],
                        arrive.at[piece, sent + slot],
                    )

                if bits[0] == 1 and side:
                    on()
                elif bits[0] == 2:
                    pl.when(turn < half)(on)

    @pl.loop(0, groups)
    def _(turn):
        @pl.when(turn + 1 < groups)
        def _():
            for which in range(computed):
                slab_copy(which, turn + 1).start()

        for which in (0, 2, 1):
            slab_copy(which, turn).wait()

            def product(right):
                block = contract_rows(slab[turn % 2, which], right[...])
                block = block.astype(BF).reshape(4, chunk, D)
                for i in range(4):
                    ready[which][turn * 4 + i] = block[i]

            if which == 0:
                first = group_of(turn) * 4 * chunk < 3 * D
                pl.when(first)(lambda: product(rights[0]))
                pl.when(jnp.logical_not(first))(lambda: product(rights[1]))
            else:
                product(rights[which + 1])
            for piece in big:
                if pieces[piece][0] != which:
                    continue
                rows = rows_of(piece)
                for side in range(2):
                    line = (near + side) % 2
                    slot = slot_of(piece, turn, side)
                    push(
                        ready[which].at[turn * 4 + line * 2 + 1 - core, rows],
                        landed[which].at[slot, rows],
                        flipped(me, 1),
                        leave.at[piece],
                        arrive.at[piece, slot],
                    )

        @pl.when(turn > 0)
        def _():
            first_add(turn - 1)

    first_add(groups - 1)
    turn = 1
    for step in range(len(pieces[0][3]) + 1):
        for at in range(len(plans[0][step])):
            for piece in small if step == 0 else (*big, *small):
                which, _, _, bits = pieces[piece]
                rows = rows_of(piece)
                if step == 0 and at == 0:
                    settle(held[which].at[pl.ds(0, devices // 2), rows], load.at[piece])
                mask = plans[piece][step][at]
                slot = slots[piece][mask]
                total = add(piece, slot, places[piece][step, mask])
                if step == len(bits):
                    outs[which][rows] = total
                    continue
                held[which][slot, rows] = total.astype(held[which].dtype)
                if (mask >> bits[step]) & 1:
                    send(piece, step + 1, mask, bits[step], held[which].at[slot, rows])
            if step or at == 0:
                send_rows(spread[turn] if turn < len(spread) else 0)
                turn += 1
    send_rows(devices)
    for piece in range(len(pieces)):
        which = pieces[piece][0]
        settle(landed[which].at[pl.ds(0, devices - 1), rows_of(piece)], leave.at[piece])
    own_rows.wait()
    for i in range(2):
        settle(rows_out.at[pl.ds(0, devices - 1)], rows_sem.at[i])


def reduce_products(lefts, rights, others, rows_in):
    devices = rows_in.shape[0]
    count, wide = lefts[0].shape
    chunk = wide // devices
    bits = devices.bit_length() - 1
    high = list(range(3, bits))
    one, other = (1, 2, *high), (2, 1, *high)
    one_early, other_early = (1, *high, 2), (2, *high, 1)
    cut = chunk // 32 * 16
    pieces = [(0, 0, chunk, one), (2, 0, chunk, other_early), (1, cut, chunk - cut, one_early)]
    pieces += [(1, 0, cut, other), (3, 0, others[0].shape[1], one), (4, 0, others[1].shape[1], other)]
    spread = [devices]
    anywhere = pl.BlockSpec(memory_space=pl.ANY)
    inside = pl.BlockSpec(memory_space=pltpu.VMEM)
    dma = pltpu.SemaphoreType.DMA
    kinds = [((chunk, D), BF)] * 3 + [(o.shape[1:], o.dtype) for o in others]
    *reduced, arrived = pl.pallas_call(
        lambda *refs: product_kernel(devices, pieces, spread, *refs),
        in_specs=[anywhere] * 3 + [inside] * 4 + [anywhere] * (len(others) + 1),
        out_specs=[inside] * len(kinds) + [anywhere],
        out_shape=[jax.ShapeDtypeStruct(shape, F32) for shape, _ in kinds]
        + [jax.ShapeDtypeStruct(rows_in.shape, rows_in.dtype)],
        scratch_shapes=[pltpu.VMEM((devices // 2, *shape), kind) for shape, kind in kinds]
        + [pltpu.VMEM((devices - 1, *shape), kind) for shape, kind in kinds]
        + [pltpu.VMEM((devices, chunk, D), BF)] * 3
        + [pltpu.VMEM((2, 3, count, 4 * chunk), BF), dma((2, 3))]
        + [dma((len(pieces), devices - 1)), dma((len(pieces),)), dma((len(pieces),)), dma((2,)), dma],
        compiler_params=pltpu.CompilerParams(
            collective_id=2, has_side_effects=True, vmem_limit_bytes=60 * 2**20
        ),
    )(*lefts, *rights, *others, rows_in)
    return reduced, arrived


TOK = 256


def normalize(values):
    average = jnp.mean(values, axis=-1, keepdims=True)
    centered = values - average
    inverse = lax.rsqrt(jnp.mean(centered * centered, axis=-1, keepdims=True) + NORM_EPS)
    return centered * inverse, inverse


def normalize_back(upstream, normed, inverse, gain):
    scaled = upstream * (1.0 + gain)
    return inverse * (
        scaled
        - jnp.mean(scaled, axis=-1, keepdims=True)
        - normed * jnp.mean(scaled * normed, axis=-1, keepdims=True)
    )


def vector(vec_ref, i):
    return vec_ref[i : i + 1, :]


def hot_rows(index, depth):
    hot = index == lax.broadcasted_iota(jnp.int32, (TOK, depth), 1)
    return hot.astype(F32).astype(BF)


def first_kernel(
    row_ref, place_ref, packed_ref, table_ref, vec_ref, qkv_ref, normed_ref, inv_ref, low_ref, z_ref
):
    values = matmul(hot_rows(row_ref[...], packed_ref.shape[0]), packed_ref[...])
    values = values + matmul(hot_rows(place_ref[...], PMAX), table_ref[...])
    normed, inverse = normalize(values)
    normed_ref[...] = normed
    inv_ref[...] = inverse
    low = (normed * (1.0 + vector(vec_ref, 0)) + vector(vec_ref, 1)).astype(BF)
    low_ref[...] = low
    for part, bias in ((0, 2), (1, None), (2, 3)):
        at = slice(part * D, (part + 1) * D)
        mixed = contract_cols(low, qkv_ref[at, :])
        if bias is not None:
            mixed = mixed + vector(vec_ref, bias)
        z_ref[:, at] = mixed.astype(BF)


def middle_kernel(
    context_ref, zero_ref, vec_ref, bias_ref, out_ref, up_ref, down_ref, head_ref, *results
):
    one_ref, one_inv_ref, one_low_ref, act_ref, slope_ref = results[:5]
    two_ref, two_inv_ref, two_low_ref, unit_ref, scale_ref, unit_low_ref = results[5:]
    hidden = zero_ref[...] * (1.0 + vector(vec_ref, 0)) + vector(vec_ref, 1)
    hidden = hidden + contract_cols(context_ref[...], out_ref[...]) + vector(vec_ref, 4)
    normed, inverse = normalize(hidden)
    one_ref[...] = normed
    one_inv_ref[...] = inverse
    hidden = normed * (1.0 + vector(vec_ref, 5)) + vector(vec_ref, 6)
    low = hidden.astype(BF)
    one_low_ref[...] = low
    total = hidden + vector(vec_ref, 7)
    for part in range(up_ref.shape[0] // D):
        at = slice(part * D, (part + 1) * D)
        inner = contract_cols(low, up_ref[at, :]) + bias_ref[:, at]
        cdf = 0.5 + 0.5 * lax.erf(inner * math.sqrt(0.5))
        activated = (inner * cdf).astype(BF)
        act_ref[:, at] = activated
        pdf = jnp.exp(-0.5 * inner * inner) * (1.0 / math.sqrt(2.0 * math.pi))
        slope_ref[:, at] = (cdf + inner * pdf).astype(BF)
        total = total + matmul(activated, down_ref[at, :])
    normed, inverse = normalize(total)
    two_ref[...] = normed
    two_inv_ref[...] = inverse
    low = (normed * (1.0 + vector(vec_ref, 8)) + vector(vec_ref, 9)).astype(BF)
    two_low_ref[...] = low
    projected = matmul(low, head_ref[...])
    scale = lax.rsqrt(jnp.sum(projected * projected, axis=-1, keepdims=True) + NORM_EPS)
    unit_ref[...] = projected * scale
    scale_ref[...] = scale
    unit_low_ref[...] = (projected * scale).astype(BF)


def column_sum(values):
    return jnp.sum(values, axis=0, keepdims=True)


def middle_back_kernel(
    grad_ref,
    unit_ref,
    scale_ref,
    two_ref,
    two_inv_ref,
    slope_ref,
    one_ref,
    one_inv_ref,
    vec_ref,
    out_ref,
    up_ref,
    down_ref,
    head_ref,
    *results,
):
    proj_ref, dtwo_ref, inner_ref, done_ref, done_low_ref, context_ref, sums_ref, bias_ref = results

    @pl.when(pl.program_id(0) == 0)
    def _():
        sums_ref[...] = jnp.zeros_like(sums_ref)
        bias_ref[...] = jnp.zeros_like(bias_ref)

    grad, unit = grad_ref[...], unit_ref[...]
    proj = (grad - unit * jnp.sum(grad * unit, axis=-1, keepdims=True)) * scale_ref[...]
    proj = proj.astype(BF)
    proj_ref[...] = proj
    upstream, normed = contract_cols(proj, head_ref[...]), two_ref[...]
    dtwo = normalize_back(upstream, normed, two_inv_ref[...], vector(vec_ref, 8))
    sums_ref[0:1, :] += column_sum(upstream * normed)
    sums_ref[1:2, :] += column_sum(upstream)
    sums_ref[2:3, :] += column_sum(dtwo)
    low = dtwo.astype(BF)
    dtwo_ref[...] = low
    upstream = dtwo
    for part in range(up_ref.shape[0] // D):
        at = slice(part * D, (part + 1) * D)
        inner = contract_cols(low, down_ref[at, :]) * slope_ref[:, at].astype(F32)
        bias_ref[:, at] += column_sum(inner)
        inner = inner.astype(BF)
        inner_ref[:, at] = inner
        upstream = upstream + matmul(inner, up_ref[at, :])
    normed = one_ref[...]
    done = normalize_back(upstream, normed, one_inv_ref[...], vector(vec_ref, 5))
    sums_ref[3:4, :] += column_sum(upstream * normed)
    sums_ref[4:5, :] += column_sum(upstream)
    sums_ref[5:6, :] += column_sum(done)
    done_ref[...] = done
    low = done.astype(BF)
    done_low_ref[...] = low
    context_ref[...] = matmul(low, out_ref[...]).astype(BF)


def first_back_kernel(
    z_ref, done_ref, zero_ref, inv_ref, place_ref, vec_ref, qkv_ref, low_ref, places_ref, sums_ref
):
    @pl.when(pl.program_id(0) == 0)
    def _():
        sums_ref[...] = jnp.zeros_like(sums_ref)
        places_ref[...] = jnp.zeros_like(places_ref)

    upstream, normed = done_ref[...], zero_ref[...]
    for part in range(3):
        at = slice(part * D, (part + 1) * D)
        upstream = upstream + matmul(z_ref[:, at], qkv_ref[at, :])
    grad = normalize_back(upstream, normed, inv_ref[...], vector(vec_ref, 0))
    sums_ref[0:1, :] += column_sum(upstream * normed)
    sums_ref[1:2, :] += column_sum(upstream)
    sums_ref[2:3, :] += column_sum(z_ref[:, :D].astype(F32))
    sums_ref[3:4, :] += column_sum(z_ref[:, 2 * D : 3 * D].astype(F32))
    low = grad.astype(BF)
    low_ref[...] = low
    places_ref[...] += contract_rows(hot_rows(place_ref[...], PMAX), low)


def by_tokens(width):
    return pl.BlockSpec((TOK, width), lambda i: (i, 0))


def resident(rows, width, at=0):
    return pl.BlockSpec((rows, width), lambda i: (at, 0), pipeline_mode=pl.Buffered(1))


def token_call(kernel, count, in_specs, outs, flops):
    return pl.pallas_call(
        kernel,
        grid=(count // TOK,),
        in_specs=in_specs,
        out_specs=[
            by_tokens(width) if rows is None else pl.BlockSpec((rows, width), lambda i: (0, 0))
            for rows, width, _ in outs
        ],
        out_shape=[
            jax.ShapeDtypeStruct((count if rows is None else rows, width), kind)
            for rows, width, kind in outs
        ],
        compiler_params=pltpu.CompilerParams(vmem_limit_bytes=56 * 2**20),
        cost_estimate=pl.CostEstimate(flops=flops, bytes_accessed=30000000, transcendentals=0),
    )


def adam_update(weight, moment, second, gradient, rate, count_steps):
    moment_new = BETA_ONE * moment + (1.0 - BETA_ONE) * gradient
    second_new = BETA_TWO * second + (1.0 - BETA_TWO) * gradient * gradient
    corrected = moment_new / (1.0 - BETA_ONE**count_steps)
    scaled = second_new / (1.0 - BETA_TWO**count_steps)
    weight_new = weight - rate * (corrected / (jnp.sqrt(scaled) + ADAM_EPS) + WEIGHT_DECAY * weight)
    return (weight_new, second_new)


def on_device(
    query_ids,
    passage_ids,
    passage_lengths,
    positives,
    negatives,
    pair_mask,
    assignments,
    step_count,
    embed_table,
    embed_table_moment,
    embed_table_second,
    attention_weight,
    attention_weight_moment,
    attention_weight_second,
    up_weight,
    up_weight_moment,
    up_weight_second,
    down_weight,
    down_weight_moment,
    down_weight_second,
    head_weight,
    head_weight_moment,
    head_weight_second,
    small_params,
    small_params_moment,
    small_params_second,
):
    devices = lax.axis_size("grp") * lax.axis_size("psg")
    members = lax.axis_size("psg")
    member = lax.axis_index("psg")
    group = lax.axis_index("grp")
    shard_rows = embed_table.shape[0]
    queries = query_ids.shape[0]
    negative_count = negatives.shape[1]
    query_rows = queries * SEG
    count = ROW + query_rows
    capacity = 16 * ((count // devices + 8 + 15) // 16)
    small_size = small_params.shape[0]
    head_rows = head_weight.shape[0]
    mask_float = pair_mask.astype(F32)

    tokens = jnp.concatenate([passage_ids.reshape(-1), query_ids.reshape(-1)])
    passage_segment, passage_position = layout_of(passage_lengths[0])
    query_place = jnp.arange(query_rows, dtype=jnp.int32)
    segment = jnp.concatenate([passage_segment, PPD + query_place // SEG])
    position = jnp.concatenate([passage_position, query_place % SEG])
    segment_column = segment[:, None]
    segment_windows = jnp.stack(
        [
            segment[window_start(i, count) : window_start(i, count) + WIN][None]
            for i in range(count // BLK)
        ]
    )

    def shard_of(rows):
        return jnp.pad(rows.astype(BF), ((0, -rows.shape[0] % 16), (0, 0)))

    matrix_rows = down_weight.shape[0]
    shards = [shard_of(attention_weight.T), shard_of(up_weight.T), shard_of(down_weight)]

    owner = tokens // shard_rows
    local_row = tokens - owner * shard_rows
    owner_hot = one_hot(owner, devices)
    row_hot = one_hot(local_row, shard_rows)
    needed = jnp.minimum(contract_rows(owner_hot, row_hot), 1.0)
    width = -(-shard_rows // 1024) * 1024
    table = jnp.pad(embed_table.astype(BF), ((0, width - shard_rows), (0, 0)))
    notes = jnp.concatenate(
        [
            v.reshape(-1).astype(BF)
            for v in (small_params, head_weight, passage_lengths, jnp.sum(mask_float))
        ]
    )
    notes = jnp.pad(notes, (0, -notes.size % 2048)).reshape(-1, 128)
    (*gathered, noted), packed, asked_rank = gather_all(
        [*shards, notes],
        jnp.pad(needed, ((0, 0), (0, width - shard_rows))).reshape(devices, width // 128, 128),
        table,
        capacity,
    )
    asked_rank = asked_rank[:, :shard_rows]
    attn_rows, up_rows, down_rows = (g[:, :matrix_rows].reshape(-1, D) for g in gathered)
    noted = noted.reshape(devices, -1)
    cut = [0, small_size, head_rows * DC, PPD, 1]
    for i in range(1, len(cut)):
        cut[i] += cut[i - 1]
    small_all, head_all, lengths_all, pairs_all = (noted[:, cut[i] : cut[i + 1]] for i in range(4))
    small_all = small_all.reshape(-1)
    head_full = head_all.reshape(D, DC)
    pair_floor = jnp.maximum(jnp.sum(pairs_all.astype(F32)), 1.0)
    place_row = jnp.arange(shard_rows, dtype=jnp.int32)
    earlier = (place_row[:, None] < place_row[None, :]).astype(BF)
    overflow = jnp.max(packed[:, capacity - 1, :1].astype(F32)) > 0.5 * MARK
    packed = packed.reshape(devices * capacity, D)
    needed_rank = jnp.minimum(matmul(needed.astype(BF), earlier), 255.0)
    token_rank = jnp.sum(matmul(owner_hot, needed_rank.astype(BF)) * row_hot.astype(F32), axis=1)
    slot = owner * capacity + jnp.minimum(token_rank.astype(jnp.int32), capacity - 1)
    slot_hot = one_hot(slot, devices * capacity)

    def whole_lookup():
        rows = lax.all_gather(embed_table.astype(BF), ALL, axis=0, tiled=True)[tokens]
        rows = jnp.pad(rows, ((0, devices * capacity - count), (0, 0)))
        return rows, jnp.arange(count, dtype=jnp.int32)

    packed, row_of = lax.cond(overflow, whole_lookup, lambda: (packed, slot))

    positions = small_all[: PMAX * D].reshape(PMAX, D)
    remainder = small_all[PMAX * D :].astype(F32)
    vectors = jnp.pad(remainder[: 10 * D].reshape(10, D), ((0, 6), (0, 0)))
    bias_up = remainder[None, 10 * D :]
    inner_width = up_rows.shape[0]
    place_column = position[:, None]
    norm_zero, inverse_zero, input_zero, mixed = token_call(
        first_kernel,
        count,
        [by_tokens(1), by_tokens(1), resident(devices * capacity, D)]
        + [resident(PMAX, D), resident(16, D), resident(3 * D, D)],
        [(None, D, F32), (None, 1, F32), (None, D, BF), (None, 3 * D, BF)],
        2 * count * D * (3 * D + PMAX),
    )(row_of[:, None], place_column, packed, positions, vectors, attn_rows)
    context, kept = attention_forward(segment_column, segment_windows, mixed)
    weight_specs = [
        resident(D, D, 3),
        resident(inner_width, D),
        resident(inner_width, D),
        resident(D, DC),
    ]
    weights = (attn_rows, up_rows, down_rows, head_full)
    middle_flops = 2 * count * D * (D + 2 * inner_width + DC)
    (
        norm_one,
        inverse_one,
        input_one,
        activated,
        slope,
        norm_two,
        inverse_two,
        input_two,
        unit,
        scale_inverse,
        unit_low,
    ) = token_call(
        middle_kernel,
        count,
        [by_tokens(D), by_tokens(D), resident(16, D), resident(1, inner_width), *weight_specs],
        [(None, D, F32), (None, 1, F32), (None, D, BF)]
        + [(None, inner_width, BF)] * 2
        + [(None, D, F32), (None, 1, F32), (None, D, BF)]
        + [(None, DC, F32), (None, 1, F32), (None, DC, BF)],
        middle_flops,
    )(context, norm_zero, vectors, bias_up, *weights)

    units = lax.all_gather(unit_low, "psg", axis=0)
    group_passage = units[:, :ROW]
    group_query = units[:, ROW:].reshape(members * query_rows, DC)
    own_query = unit_low[ROW:]
    own_passage = unit_low[:ROW]
    group_lengths = lax.dynamic_slice_in_dim(lengths_all, group * members, members, 0)
    group_segment, _ = layout_of(group_lengths.astype(jnp.int32))
    group_hot = one_hot(group_segment, PPD)
    passage_hot = one_hot(passage_segment, PPD)

    weighted_own = jnp.exp(
        jnp.einsum("qd,mtd->mqt", own_query, group_passage, preferred_element_type=F32) / TEMPER
    )
    sum_own = lambda part: jnp.einsum(
        "mqt,mtp->mqp", part, group_hot, preferred_element_type=F32
    )
    high, low = split_two(weighted_own)
    totals_own = sum_own(high) + sum_own(low)
    weighted = jnp.exp(contract_cols(group_query, own_passage) / TEMPER)
    high, low = split_two(weighted)
    totals = matmul(high, passage_hot) + matmul(low, passage_hot)
    own_scores = jnp.sum(
        (TEMPER * jnp.log(totals_own)).reshape(members, queries, SEG, PPD), axis=2
    )
    own_scores = own_scores.transpose(1, 0, 2).reshape(queries, members * PPD)
    columns = jnp.arange(members * PPD, dtype=jnp.int32)
    pick_positive = (positives[:, None] == columns[None, :]).astype(F32)
    pick_negative = (negatives[:, :, None] == columns[None, None, :]).astype(F32)
    pos_score = jnp.sum(own_scores * pick_positive, axis=1)
    neg_score = jnp.sum(pick_negative * own_scores[:, None, :], axis=2)
    margins = MARGIN - pos_score[:, None] + neg_score
    numerator = jnp.sum(mask_float * jax.nn.softplus(margins))
    factor = mask_float * jax.nn.sigmoid(margins) / pair_floor
    grad_own = (
        jnp.sum(factor[:, :, None] * pick_negative, axis=1)
        - jnp.sum(factor, axis=1)[:, None] * pick_positive
    )
    grad_group = lax.all_gather(grad_own, "psg", axis=0, tiled=True)
    grad_local = lax.dynamic_slice_in_dim(grad_group, member * PPD, PPD, 1)

    grad_own_split = grad_own.reshape(queries, 1, members, PPD).transpose(2, 0, 1, 3)
    ratio_own = (
        (TEMPER * grad_own_split) / totals_own.reshape(members, queries, SEG, PPD)
    ).reshape(members, query_rows, PPD)
    spread_own = jnp.einsum(
        "mqp,mtp->mqt", ratio_own.astype(BF), group_hot, preferred_element_type=F32
    )
    sims_own = (spread_own * weighted_own / TEMPER).astype(BF)
    grad_unit_query = jnp.einsum(
        "mqt,mtd->qd", sims_own, group_passage, preferred_element_type=F32
    )
    ratio = (
        (TEMPER * grad_local[:, None, :]) / totals.reshape(members * queries, SEG, PPD)
    ).reshape(members * query_rows, PPD)
    sims = (contract_cols(ratio.astype(BF), passage_hot) * weighted / TEMPER).astype(BF)
    grad_unit_passage = contract_rows(sims, group_query)
    grad_unit = jnp.concatenate([grad_unit_passage, grad_unit_query])

    picks = one_hot(assignments[0], NCENT)
    centroid_part = contract_rows(picks, own_passage)
    count_part = jnp.sum(picks.astype(F32), axis=0)
    (
        grad_proj,
        grad_two_low,
        grad_inner,
        grad_sum_one,
        grad_one_low,
        grad_context,
        sums,
        grad_bias_up,
    ) = token_call(
        middle_back_kernel,
        count,
        [by_tokens(DC), by_tokens(DC), by_tokens(1), by_tokens(D), by_tokens(1)]
        + [by_tokens(inner_width), by_tokens(D), by_tokens(1), resident(16, D), *weight_specs],
        [(None, DC, BF), (None, D, BF), (None, inner_width, BF), (None, D, F32)]
        + [(None, D, BF), (None, D, BF), (8, D, F32), (1, inner_width, F32)],
        middle_flops,
    )(
        grad_unit,
        unit,
        scale_inverse,
        norm_two,
        inverse_two,
        slope,
        norm_one,
        inverse_one,
        vectors,
        *weights,
    )
    grad_head = contract_rows(input_two, grad_proj)
    grad_attn = attention_backward(
        segment.reshape(-1, 1, BLK),
        segment_windows.transpose(0, 2, 1),
        mixed,
        grad_context,
        kept,
        grad_one_low,
    )
    grad_low, grad_positions, sums_zero = token_call(
        first_back_kernel,
        count,
        [by_tokens(3 * D), by_tokens(D), by_tokens(D), by_tokens(1), by_tokens(1)]
        + [resident(16, D), resident(3 * D, D)],
        [(None, D, BF), (PMAX, D, F32), (8, D, F32)],
        2 * count * D * (3 * D + PMAX),
    )(grad_attn, grad_sum_one, norm_zero, inverse_zero, place_column, vectors, attn_rows)
    grad_slots = contract_rows(slot_hot, grad_low).astype(BF).reshape(devices, capacity, D)
    grad_small = jnp.concatenate(
        [
            grad_positions.reshape(-1),
            sums_zero[:4].reshape(-1),
            sums[5],
            sums[3],
            sums[4],
            sums[2],
            sums[0],
            sums[1],
            grad_bias_up[0],
        ]
    )

    def side_by_side(parts, sublanes):
        joined = jnp.concatenate([p.reshape(devices, -1) for p in parts], axis=1)
        joined = jnp.pad(joined, ((0, 0), (0, -joined.shape[1] % (sublanes * 128))))
        return joined.reshape(devices, -1, 128)

    lefts = [grad_attn, grad_inner, activated]
    rights = [input_zero, context, input_one, grad_two_low]
    others = [
        side_by_side([centroid_part.astype(BF), grad_head.astype(BF)], 16),
        side_by_side([grad_small, count_part, jnp.broadcast_to(numerator, (devices, 1))], 8),
    ]
    if members * matrix_rows % 128 == 0 and members == 4:
        reduced, grad_slots = reduce_products(lefts, rights, others, grad_slots)
    else:
        right_of = [rights[:2], rights[2:3], rights[3:]]
        sums = []
        for left, right in zip(lefts, right_of):
            if len(right) == 2:
                rows = jnp.concatenate(
                    [
                        contract_rows(left[:, : 3 * D], right[0]),
                        contract_rows(left[:, 3 * D :], right[1]),
                    ]
                )
            else:
                rows = contract_rows(left, right[0])
            rows = rows.astype(BF).reshape(devices, matrix_rows, D)
            sums.append(jnp.pad(rows, ((0, 0), (0, -matrix_rows % 16), (0, 0))))
        reduced, grad_slots = reduce_all(sums + others, grad_slots)
    attn_reduced, up_reduced, down_reduced = (r[:matrix_rows] for r in reduced[:3])
    wide, fine = reduced[3].reshape(-1), reduced[4].reshape(-1)
    centroid_rows = NCENT // devices
    centroid_sums = wide[: centroid_rows * DC].reshape(centroid_rows, DC)
    head_reduced = wide[centroid_rows * DC :][: head_rows * DC].reshape(head_rows, DC)
    small_reduced = fine[:small_size]
    centroid_counts = fine[small_size:][:centroid_rows]
    loss = fine[small_size + centroid_rows] / pair_floor

    def whole_table():
        table = jnp.zeros((shard_rows * devices, D), F32).at[tokens].add(grad_low.astype(F32))
        return lax.psum_scatter(table, ALL, scatter_dimension=0, tiled=True)

    def own_rows():
        slots = jnp.arange(capacity, dtype=jnp.int32).astype(F32)
        picked = (asked_rank[:, None, :] == slots[None, :, None]).astype(BF)
        return contract_rows(
            picked.reshape(devices * capacity, shard_rows),
            grad_slots.reshape(devices * capacity, D),
        )

    table_reduced = lax.cond(
        overflow,
        whole_table,
        own_rows,
    )

    count_steps = step_count[0].astype(F32)
    attn_reduced = attn_reduced.T
    up_reduced = up_reduced.T
    table_new, table_second_new = adam_update(
        embed_table, embed_table_moment, embed_table_second, table_reduced, RATE_TABLE, count_steps
    )
    attn_new, attn_second_new = adam_update(
        attention_weight,
        attention_weight_moment,
        attention_weight_second,
        attn_reduced,
        RATE_MATRIX,
        count_steps,
    )
    up_new, up_second_new = adam_update(
        up_weight, up_weight_moment, up_weight_second, up_reduced, RATE_MATRIX, count_steps
    )
    down_new, down_second_new = adam_update(
        down_weight, down_weight_moment, down_weight_second, down_reduced, RATE_MATRIX, count_steps
    )
    head_new, head_second_new = adam_update(
        head_weight, head_weight_moment, head_weight_second, head_reduced, RATE_MATRIX, count_steps
    )
    small_new, small_second_new = adam_update(
        small_params, small_params_moment, small_params_second, small_reduced, RATE_TABLE, count_steps
    )
    return (
        loss,
        centroid_sums,
        centroid_counts,
        table_new,
        table_reduced,
        table_second_new,
        attn_new,
        attn_reduced,
        attn_second_new,
        up_new,
        up_reduced,
        up_second_new,
        down_new,
        down_reduced,
        down_second_new,
        head_new,
        head_reduced,
        head_second_new,
        small_new,
        small_reduced,
        small_second_new,
    )


def solution(mesh):
    in_specs = (
        P(("grp", "psg"), None),
        P(("grp", "psg"), None),
        P(("grp", "psg"), None),
        P(("grp", "psg")),
        P(("grp", "psg"), None),
        P(("grp", "psg"), None),
        P(("grp", "psg"), None),
        P(),
        P(("grp", "psg"), None),
        P(("grp", "psg"), None),
        P(("grp", "psg"), None),
        P(None, ("grp", "psg")),
        P(None, ("grp", "psg")),
        P(None, ("grp", "psg")),
        P(None, ("grp", "psg")),
        P(None, ("grp", "psg")),
        P(None, ("grp", "psg")),
        P(("grp", "psg"), None),
        P(("grp", "psg"), None),
        P(("grp", "psg"), None),
        P(("grp", "psg"), None),
        P(("grp", "psg"), None),
        P(("grp", "psg"), None),
        P(("grp", "psg")),
        P(("grp", "psg")),
        P(("grp", "psg")),
    )
    out_specs = (
        P(),
        P(("grp", "psg"), None),
        P(("grp", "psg")),
        P(("grp", "psg"), None),
        P(("grp", "psg"), None),
        P(("grp", "psg"), None),
        P(None, ("grp", "psg")),
        P(None, ("grp", "psg")),
        P(None, ("grp", "psg")),
        P(None, ("grp", "psg")),
        P(None, ("grp", "psg")),
        P(None, ("grp", "psg")),
        P(("grp", "psg"), None),
        P(("grp", "psg"), None),
        P(("grp", "psg"), None),
        P(("grp", "psg"), None),
        P(("grp", "psg"), None),
        P(("grp", "psg"), None),
        P(("grp", "psg")),
        P(("grp", "psg")),
        P(("grp", "psg")),
    )
    return jax.shard_map(
        on_device, mesh=mesh, in_specs=in_specs, out_specs=out_specs, check_vma=False
    )
```

```python
import math

import jax
import jax.numpy as jnp
from jax import lax
from jax.experimental import pallas as pl
from jax.experimental.pallas import tpu as pltpu
from jax.sharding import PartitionSpec as P

D = 768
HEADS = 12
HD = 64
SEG = 32
PMAX = 64
ROW = 1024
PPD = 32
QDEV = 8
NCENT = 1024
DC = 128
BLK = 128
WIN = 256
ALL = ("grp", "psg")
BF = jnp.bfloat16
F32 = jnp.float32
MARK = 1e30


TEMPER = 0.2
MARGIN = 1.0
NORM_EPS = 1e-06
BETA_ONE = 0.9
BETA_TWO = 0.999
ADAM_EPS = 1e-08
WEIGHT_DECAY = 0.01
RATE_MATRIX = 0.01
RATE_TABLE = 0.1


def matmul(lhs_mat, rhs_mat):
    return jnp.dot(lhs_mat, rhs_mat, preferred_element_type=jnp.float32)


def contract_rows(lhs_mat, rhs_mat):
    return lax.dot_general(
        lhs_mat, rhs_mat, (((0,), (0,)), ((), ())), preferred_element_type=jnp.float32
    )


def contract_cols(lhs_mat, rhs_mat):
    return lax.dot_general(
        lhs_mat, rhs_mat, (((1,), (1,)), ((), ())), preferred_element_type=jnp.float32
    )


def layer_norm(values, scale_gain, shift_bias):
    average = jnp.mean(values, axis=-1, keepdims=True)
    centered = values - average
    inverse = lax.rsqrt(jnp.mean(centered * centered, axis=-1, keepdims=True) + NORM_EPS)
    normed = centered * inverse
    return (normed * (1.0 + scale_gain) + shift_bias, (normed, inverse))


def norm_back(upstream, stored, scale_gain):
    normed, inverse = stored
    scaled = upstream * (1.0 + scale_gain)
    back = inverse * (
        scaled
        - jnp.mean(scaled, axis=-1, keepdims=True)
        - normed * jnp.mean(scaled * normed, axis=-1, keepdims=True)
    )
    return (back, jnp.sum(upstream * normed, axis=0), jnp.sum(upstream, axis=0))


def starts_of(lengths):
    order = jnp.arange(PPD, dtype=jnp.int32)
    before = (order[:, None] > order[None, :]).astype(jnp.int32)
    return jnp.sum(before * lengths[..., None, :], axis=-1)


def layout_of(lengths):
    starts = starts_of(lengths)
    place = jnp.arange(ROW, dtype=jnp.int32)
    above = (place[:, None] >= starts[..., None, :]).astype(jnp.int32)
    segment = jnp.sum(above, axis=-1) - 1
    begin = jnp.max(above * starts[..., None, :], axis=-1)
    return segment, place - begin


def one_hot(index, depth):
    return (index[..., None] == jnp.arange(depth, dtype=jnp.int32)).astype(BF)


def split_two(values):
    high = lax.reduce_precision(values, 8, 7)
    return high.astype(BF), (values - high).astype(BF)


def split_three(values):
    high = lax.reduce_precision(values, 8, 7)
    middle = lax.reduce_precision(values - high, 8, 7)
    return high.astype(BF), middle.astype(BF), (values - high - middle).astype(BF)


def window_start(block, count):
    return min(max(block * BLK - (WIN - BLK) // 2, 0), count - WIN)


def attn_forward_kernel(count, segc_ref, segw_ref, z_ref, o_ref, lse_ref):
    block = pl.program_id(0)
    row = pl.multiple_of(block * BLK, BLK)
    first = pl.multiple_of(jnp.clip(row - (WIN - BLK) // 2, 0, count - WIN), 64)
    allowed = segc_ref[...] == segw_ref[0]
    lane = lax.broadcasted_iota(jnp.int32, (BLK, 2 * HD), 1)
    lane_head = lax.broadcasted_iota(jnp.int32, (BLK, 128), 1)
    kept = jnp.zeros((BLK, 128), F32)
    for pair in range(HEADS // 2):
        at = pair * 2 * HD
        query = z_ref[pl.ds(row, BLK), at : at + 2 * HD] * BF(HD ** (-0.5))
        key = z_ref[pl.ds(first, WIN), D + at : D + at + 2 * HD]
        value = z_ref[pl.ds(first, WIN), 2 * D + at : 2 * D + at + 2 * HD]
        parts = []
        for half in range(2):
            mine = (lane >= half * HD) & (lane < (half + 1) * HD)
            scores = contract_cols(jnp.where(mine, query, BF(0)), key)
            scores = jnp.where(allowed, scores, -1000000000.0)
            top = jnp.max(scores, axis=-1, keepdims=True)
            weight = jnp.exp(scores - top)
            total = jnp.sum(weight, axis=-1, keepdims=True)
            probs = (weight * (1.0 / total)).astype(BF)
            parts.append(matmul(probs, value))
            kept = jnp.where(lane_head == 2 * pair + half, top + jnp.log(total), kept)
        o_ref[:, at : at + 2 * HD] = jnp.where(lane < HD, parts[0], parts[1]).astype(BF)
    lse_ref[...] = kept.T[:16]


def attn_backward_kernel(
    count, blocks, segr_ref, segw_ref, z_ref, do_ref, lse_ref, one_ref, dz_ref, dk_ref, dv_ref
):
    block = pl.program_id(0)
    row = pl.multiple_of(block * BLK, BLK)
    first = pl.multiple_of(jnp.clip(row - (WIN - BLK) // 2, 0, count - WIN), 64)

    @pl.when(block == 0)
    def _():
        dk_ref[...] = jnp.zeros_like(dk_ref)
        dv_ref[...] = jnp.zeros_like(dv_ref)

    allowed = segw_ref[0] == segr_ref[0]
    lane = lax.broadcasted_iota(jnp.int32, (BLK, 2 * HD), 1)
    for pair in range(HEADS // 2):
        at = pair * 2 * HD
        query = z_ref[pl.ds(row, BLK), at : at + 2 * HD] * BF(HD ** (-0.5))
        key = z_ref[pl.ds(first, WIN), D + at : D + at + 2 * HD]
        value = z_ref[pl.ds(first, WIN), 2 * D + at : 2 * D + at + 2 * HD]
        upstream = do_ref[:, at : at + 2 * HD]
        grad_query = []
        grad_key = jnp.zeros((WIN, 2 * HD), F32)
        grad_value = jnp.zeros((WIN, 2 * HD), F32)
        for half in range(2):
            mine = (lane >= half * HD) & (lane < (half + 1) * HD)
            query_own = jnp.where(mine, query, BF(0))
            up_own = jnp.where(mine, upstream, BF(0))
            head = 2 * pair + half
            scores = jnp.where(allowed, contract_cols(key, query_own), -1000000000.0)
            probs = jnp.exp(scores - lse_ref[head : head + 1, :])
            grad_probs = contract_cols(value, up_own)
            grad_value = grad_value + matmul(probs.astype(BF), up_own)
            inner = jnp.sum(grad_probs * probs, axis=0, keepdims=True)
            grad_scores = (probs * (grad_probs - inner)).astype(BF)
            grad_query.append(contract_rows(grad_scores, key))
            grad_key = grad_key + matmul(grad_scores, query_own)
        own = jnp.where(lane < HD, grad_query[0], grad_query[1]) * HD ** (-0.5)
        dz_ref[pl.ds(row, BLK), at : at + 2 * HD] = own.astype(BF)
        dk_ref[pl.ds(first, WIN), at : at + 2 * HD] += grad_key
        dv_ref[pl.ds(first, WIN), at : at + 2 * HD] += grad_value

    dz_ref[pl.ds(row, BLK), 3 * D :] = one_ref[...]

    @pl.when(block == blocks - 1)
    def _():
        dz_ref[:, D : 2 * D] = dk_ref[...].astype(BF)
        dz_ref[:, 2 * D : 3 * D] = dv_ref[...].astype(BF)


def attention_specs(count):
    return [
        pl.BlockSpec((BLK, 1), lambda i: (i, 0)),
        pl.BlockSpec((1, 1, WIN), lambda i: (i, 0, 0)),
        pl.BlockSpec((count, 3 * D), lambda i: (0, 0)),
    ]


def attention_forward(segment_column, segment_windows, mixed):
    count = mixed.shape[0]
    blocks = count // BLK
    return pl.pallas_call(
        lambda *refs: attn_forward_kernel(count, *refs),
        grid=(blocks,),
        in_specs=attention_specs(count),
        out_specs=[
            pl.BlockSpec((BLK, D), lambda i: (i, 0)),
            pl.BlockSpec((16, BLK), lambda i: (0, i)),
        ],
        out_shape=[
            jax.ShapeDtypeStruct((count, D), BF),
            jax.ShapeDtypeStruct((16, count), F32),
        ],
        compiler_params=pltpu.CompilerParams(vmem_limit_bytes=40 * 2**20),
        cost_estimate=pl.CostEstimate(
            flops=4 * count * WIN * 128 * HEADS, bytes_accessed=12000000, transcendentals=0
        ),
    )(segment_column, segment_windows, mixed)


def attention_backward(segment_rows, segment_windows, mixed, upstream, kept, beside):
    count = mixed.shape[0]
    blocks = count // BLK
    return pl.pallas_call(
        lambda *refs: attn_backward_kernel(count, blocks, *refs),
        grid=(blocks,),
        in_specs=[
            pl.BlockSpec((1, 1, BLK), lambda i: (i, 0, 0)),
            pl.BlockSpec((1, WIN, 1), lambda i: (i, 0, 0)),
            pl.BlockSpec((count, 3 * D), lambda i: (0, 0), pipeline_mode=pl.Buffered(1)),
            pl.BlockSpec((BLK, D), lambda i: (i, 0)),
            pl.BlockSpec((16, BLK), lambda i: (0, i)),
            pl.BlockSpec((BLK, D), lambda i: (i, 0)),
        ],
        out_specs=pl.BlockSpec((count, 4 * D), lambda i: (0, 0)),
        out_shape=jax.ShapeDtypeStruct((count, 4 * D), BF),
        scratch_shapes=[pltpu.VMEM((count, D), F32), pltpu.VMEM((count, D), F32)],
        compiler_params=pltpu.CompilerParams(vmem_limit_bytes=56 * 2**20),
        cost_estimate=pl.CostEstimate(
            flops=10 * count * WIN * 128 * HEADS, bytes_accessed=18000000, transcendentals=0
        ),
    )(segment_rows, segment_windows, mixed, upstream, kept, beside)


def place_of():
    return lax.axis_index("grp") * lax.axis_size("psg") + lax.axis_index("psg")


def mesh_place(place):
    members = lax.axis_size("psg")
    return (place // members, place % members)


def flipped(place, mask):
    result, bit = place, 0
    while mask >> bit:
        if (mask >> bit) & 1:
            result = result + (1 - 2 * ((place // (1 << bit)) % 2)) * (1 << bit)
        bit += 1
    return result


def greet_all(devices, me):
    barrier = pltpu.get_barrier_semaphore()

    @pl.loop(1, devices)
    def _(i):
        pl.semaphore_signal(
            barrier,
            inc=1,
            device_id=mesh_place((me + i) % devices),
            device_id_type=pl.DeviceIdType.MESH,
        )

    pl.semaphore_wait(barrier, devices - 1)


def gather_plan(order, group):
    held, steps = [0], []
    for bit in order:
        fresh = [(1 << bit) | m for m in held]
        steps.append([fresh[i : i + group] for i in range(0, len(fresh), group)])
        held = held + fresh
    return steps


def earlier_rows(width):
    above = lax.broadcasted_iota(jnp.int32, (width, width), 0)
    return (above < lax.broadcasted_iota(jnp.int32, (width, width), 1)).astype(F32).astype(BF)


def rank_rows(asked, earlier, rank_ref):
    width = earlier.shape[0]
    asked = jnp.concatenate([asked[:, j, :] for j in range(width // 128)], axis=1)
    rank_ref[...] = jnp.where(asked > 0.5, matmul(asked.astype(BF), earlier), -1.0)
    return jnp.max(jnp.sum(asked, axis=1, keepdims=True), axis=0, keepdims=True)


def pack_rows(places, slot, most, table, rank_ref, packed_ref):
    capacity, width = packed_ref.shape[1], table.shape[0]
    at = lax.broadcasted_iota(jnp.int32, (capacity, width), 0).astype(F32)
    picked = [
        jnp.where(rank_ref[pl.ds(place, 1), :] == at, 1.0, 0.0).astype(BF) for place in places
    ]
    rows = matmul(jnp.concatenate(picked), table[...]).reshape(len(places), capacity, D)
    last = lax.broadcasted_iota(jnp.int32, (len(places), capacity, D), 1) == capacity - 1
    rows = jnp.where(last & (most > capacity)[:, :, None], MARK, rows)
    packed_ref[slot : slot + len(places)] = rows.astype(BF)


def gather_kernel(devices, pieces, *refs):
    matrices = 4
    sources, (needed, table) = refs[:matrices], refs[matrices : matrices + 2]
    outs, (rows_out, rank) = refs[6:10], refs[10:12]
    asked, earlier, packed, arrive, beside, leave, local, ask_sem, rows_sem = refs[12:]
    me = place_of()
    group = max(devices // 8, 1)
    greet_all(devices, me)

    def push(source, target_ref, target, send, recv):
        pltpu.make_async_remote_copy(
            src_ref=source,
            dst_ref=target_ref,
            send_sem=send,
            recv_sem=recv,
            device_id=mesh_place(target),
            device_id_type=pl.DeviceIdType.MESH,
        ).start()

    def settle(some, semaphore):
        pltpu.make_async_copy(some, some, semaphore).wait()

    @pl.loop(1, devices)
    def _(i):
        target = (me + i) % devices
        push(needed.at[target], asked.at[me], target, ask_sem.at[0], ask_sem.at[1])

    def start(piece, mask, target, semaphore):
        which, first, rows, _ = pieces[piece]
        there = outs[which].at[flipped(me, mask), pl.ds(first, rows)]
        here = sources[which].at[pl.ds(first, rows)] if mask == 0 else there
        push(here, there, flipped(me, target), leave.at[piece], semaphore)

    def wait(piece, blocks, semaphore):
        which, first, rows, _ = pieces[piece]
        settle(outs[which].at[pl.ds(0, blocks), pl.ds(first, rows)], semaphore)

    plans, numbers = [], []
    for piece in range(len(pieces)):
        plan = gather_plan(pieces[piece][3], group)
        number, count = {}, 0
        for groups in plan:
            for masks in groups:
                for mask in masks:
                    number[mask] = count
                count += 1
        plans.append(plan)
        numbers.append(number)

    def send_on(piece, mask, after):
        order = pieces[piece][3]
        for step in range(after + 1, len(order)):
            target = 1 << order[step]
            start(piece, mask, target, arrive.at[piece, numbers[piece][mask | target]])
        start(piece, mask, 1, beside.at[piece])

    def pass_on(piece, step):
        for masks in plans[piece][step]:
            wait(piece, len(masks), arrive.at[piece, numbers[piece][masks[0]]])
            for mask in masks:
                send_on(piece, mask, step)

    for piece in range(len(pieces)):
        send_on(piece, 0, -1)

    own = [
        pltpu.make_async_copy(source, out.at[me], local.at[i])
        for i, (source, out) in enumerate(zip(sources, outs))
    ]
    own_asked = pltpu.make_async_copy(needed.at[me], asked.at[me], local.at[matrices])
    for copy in own:
        copy.start()
    own_asked.start()
    earlier[...] = earlier_rows(table.shape[0])
    for piece in range(len(pieces)):
        pass_on(piece, 0)
    own_asked.wait()
    for i in range(2):
        settle(asked.at[pl.ds(0, devices - 1)], ask_sem.at[i])
    most = rank_rows(asked[...], earlier[...], rank)

    masks = sorted(range(devices), key=lambda m: -bin(m).count("1"))
    steps = len(pieces[0][3])
    each = -(-(devices - 1) // (len(pieces) * (steps - 1)))
    kept_rows = pltpu.make_async_copy(
        packed.at[devices - 1], rows_out.at[me], local.at[matrices + 1]
    )
    sent, made, together = 0, 0, 8
    for step in range(1, steps):
        for piece in range(len(pieces)):
            now = min(sent + each, devices)
            while made < now:
                group_now = masks[made : made + together]
                places = [flipped(me, m) for m in group_now]
                pack_rows(places, made, most, table, rank, packed)
                made += together
            pass_on(piece, step)
            for i in range(sent, now):
                target = flipped(me, masks[i])
                if masks[i]:
                    push(packed.at[i], rows_out.at[me], target, rows_sem.at[0], rows_sem.at[1])
                else:
                    kept_rows.start()
            sent = now
    for piece in range(len(pieces)):
        wait(piece, devices // 2, beside.at[piece])
        wait(piece, devices - 1, leave.at[piece])
    for copy in own:
        copy.wait()
    kept_rows.wait()
    for i in range(2):
        settle(rows_out.at[pl.ds(0, devices - 1)], rows_sem.at[i])


def gather_all(sources, needed, table, capacity):
    devices = needed.shape[0]
    rows = sources[0].shape[0]
    bits = devices.bit_length() - 1
    high = list(range(3, bits))[::-1]
    one, other = (*high, 2, 1), (*high, 1, 2)
    cut = rows // 32 * 16
    pieces = [(0, 0, rows, one), (2, 0, rows, other), (1, cut, rows - cut, one)]
    if cut:
        pieces.append((1, 0, cut, other))
    pieces.append((3, 0, sources[3].shape[0], one))
    count = max(sum(map(len, gather_plan(p[3], max(devices // 8, 1)))) for p in pieces)
    anywhere = pl.BlockSpec(memory_space=pl.ANY)
    inside = pl.BlockSpec(memory_space=pltpu.VMEM)
    dma = pltpu.SemaphoreType.DMA
    *gathered, arrived, rank = pl.pallas_call(
        lambda *refs: gather_kernel(devices, pieces, *refs),
        in_specs=[anywhere] * 4 + [inside] * 2,
        out_specs=[anywhere] * 5 + [inside],
        out_shape=[jax.ShapeDtypeStruct((devices, *s.shape), s.dtype) for s in sources]
        + [
            jax.ShapeDtypeStruct((devices, capacity, D), BF),
            jax.ShapeDtypeStruct((devices, table.shape[0]), F32),
        ],
        scratch_shapes=[
            pltpu.VMEM(needed.shape, F32),
            pltpu.VMEM((table.shape[0], table.shape[0]), BF),
            pltpu.VMEM((devices, capacity, D), BF),
            dma((len(pieces), count)),
            dma((len(pieces),)),
            dma((len(pieces),)),
            dma((6,)),
            dma((2,)),
            dma((2,)),
        ],
        compiler_params=pltpu.CompilerParams(
            collective_id=0, has_side_effects=True, vmem_limit_bytes=48 * 2**20
        ),
    )(*sources, needed, table)
    return gathered, arrived, rank


def reduce_plan(order, group):
    held = [0]
    for bit in reversed(order):
        held = [m | (1 << bit) for m in held] + held
    steps = []
    for step in range(len(order) + 1):
        if step:
            held = [m for m in held if not (m >> order[step - 1]) & 1]
        steps.append([held[i : i + group] for i in range(0, len(held), group)])
    return steps


def reduce_kernel(devices, pieces, spread, *refs):
    count = len({p[0] for p in pieces})
    sources, rows_in = refs[:count], refs[count]
    outs, rows_out = refs[count + 1 : 2 * count + 1], refs[2 * count + 1]
    held, landed = refs[2 * count + 2 : 3 * count + 2], refs[3 * count + 2 : 4 * count + 2]
    arrive, leave, load, rows_sem, own_sem = refs[4 * count + 2 :]
    me = place_of()
    group = max(devices // 16, 1)
    greet_all(devices, me)

    def push(source, target_ref, target, send, recv):
        pltpu.make_async_remote_copy(
            src_ref=source,
            dst_ref=target_ref,
            send_sem=send,
            recv_sem=recv,
            device_id=mesh_place(target),
            device_id_type=pl.DeviceIdType.MESH,
        ).start()

    def settle(some, semaphore):
        pltpu.make_async_copy(some, some, semaphore).wait()

    plans, slots, places, numbers = [], [], [], []
    for piece in pieces:
        plan = reduce_plan(piece[3], group)
        slots.append({m: i for i, m in enumerate(sum(plan[0], []))})
        place, number, at, count = {}, {}, 0, 0
        for step, groups in enumerate(plan):
            for masks in groups:
                for mask in masks:
                    place[step, mask], number[step, mask] = at, count
                    at += 1
                count += 1
        plans.append(plan)
        places.append(place)
        numbers.append(number)

    def rows_of(piece):
        return pl.ds(pieces[piece][1], pieces[piece][2])

    def send(piece, step, mask, bit, source):
        which = pieces[piece][0]
        kept = mask & ~(1 << bit)
        push(
            source,
            landed[which].at[places[piece][step, kept], rows_of(piece)],
            flipped(me, 1 << bit),
            leave.at[piece],
            arrive.at[piece, numbers[piece][step, kept]],
        )

    order = sorted(range(1, devices), key=lambda m: -bin(m).count("1"))

    def send_rows(amount):
        for _ in range(min(amount, len(order))):
            target = flipped(me, order.pop(0))
            push(rows_in.at[target], rows_out.at[me], target, rows_sem.at[0], rows_sem.at[1])

    own_rows = pltpu.make_async_copy(rows_in.at[me], rows_out.at[me], own_sem)
    own_rows.start()
    send_rows(spread[0])
    for masks in plans[0][0]:
        for piece in range(len(pieces)):
            which = pieces[piece][0]
            for mask in plans[piece][0][plans[0][0].index(masks)]:
                source = sources[which].at[flipped(me, mask | 1), rows_of(piece)]
                send(piece, 0, mask | 1, 0, source)
    for piece in range(len(pieces)):
        which = pieces[piece][0]
        for mask in slots[piece]:
            pltpu.make_async_copy(
                sources[which].at[flipped(me, mask), rows_of(piece)],
                held[which].at[slots[piece][mask], rows_of(piece)],
                load.at[piece],
            ).start()
    turn = 1
    for step in range(len(pieces[0][3]) + 1):
        for at in range(len(plans[0][step])):
            for piece in range(len(pieces)):
                which, _, _, bits = pieces[piece]
                rows = rows_of(piece)
                if step == 0 and at == 0:
                    settle(held[which].at[pl.ds(0, devices // 2), rows], load.at[piece])
                masks = plans[piece][step][at]
                some = landed[which].at[pl.ds(0, len(masks)), rows]
                settle(some, arrive.at[piece, numbers[piece][step, masks[0]]])
                for mask in masks:
                    slot = slots[piece][mask]
                    total = held[which][slot, rows].astype(F32)
                    total = total + landed[which][places[piece][step, mask], rows].astype(F32)
                    if step == len(bits):
                        outs[which][rows] = total
                        continue
                    held[which][slot, rows] = total.astype(held[which].dtype)
                    if (mask >> bits[step]) & 1:
                        send(piece, step + 1, mask, bits[step], held[which].at[slot, rows])
            send_rows(spread[turn] if turn < len(spread) else 0)
            turn += 1
    send_rows(devices)
    for piece in range(len(pieces)):
        which = pieces[piece][0]
        settle(landed[which].at[pl.ds(0, devices - 1), rows_of(piece)], leave.at[piece])
    own_rows.wait()
    for i in range(2):
        settle(rows_out.at[pl.ds(0, devices - 1)], rows_sem.at[i])


def reduce_all(sources, rows_in):
    devices = rows_in.shape[0]
    bits = devices.bit_length() - 1
    high = list(range(3, bits))
    one, other = (1, 2, *high), (2, 1, *high)
    pieces = []
    for i in (0, 2, 1, 3, 4):
        rows = sources[i].shape[1]
        cut = rows // 32 * 16 if i == 1 else 0
        pieces.append((i, cut, rows - cut, one if i in (0, 1, 3) else other))
        if cut:
            pieces.append((i, 0, cut, other))
    spread = [6] + [2] * devices
    count = max(sum(map(len, reduce_plan(p[3], max(devices // 16, 1)))) for p in pieces)
    anywhere = pl.BlockSpec(memory_space=pl.ANY)
    inside = pl.BlockSpec(memory_space=pltpu.VMEM)
    dma = pltpu.SemaphoreType.DMA
    *reduced, arrived = pl.pallas_call(
        lambda *refs: reduce_kernel(devices, pieces, spread, *refs),
        in_specs=[anywhere] * (len(sources) + 1),
        out_specs=[inside] * len(sources) + [anywhere],
        out_shape=[jax.ShapeDtypeStruct(s.shape[1:], F32) for s in sources]
        + [jax.ShapeDtypeStruct(rows_in.shape, rows_in.dtype)],
        scratch_shapes=[pltpu.VMEM((devices // 2, *s.shape[1:]), s.dtype) for s in sources]
        + [pltpu.VMEM((devices - 1, *s.shape[1:]), s.dtype) for s in sources]
        + [dma((len(pieces), count)), dma((len(pieces),)), dma((len(pieces),)), dma((2,)), dma],
        compiler_params=pltpu.CompilerParams(
            collective_id=1, has_side_effects=True, vmem_limit_bytes=48 * 2**20
        ),
    )(*sources, rows_in)
    return reduced, arrived


def product_kernel(devices, pieces, spread, *refs):
    count, computed = len({p[0] for p in pieces}), 3
    lefts, rights, others, rows_in = refs[:3], refs[3:7], refs[7 : count + 4], refs[count + 4]
    refs = refs[count + 5 :]
    outs, rows_out = refs[:count], refs[count]
    held, landed = refs[count + 1 : 2 * count + 1], refs[2 * count + 1 : 3 * count + 1]
    refs = refs[3 * count + 1 :]
    ready, refs = refs[:computed], refs[computed:]
    slab, slab_sem, arrive, leave, load, rows_sem, own_sem = refs
    me = place_of()
    groups = devices // 4
    half = groups // 2
    depth = groups.bit_length() - 1
    chunk = outs[0].shape[0]
    greet_all(devices, me)

    def push(source, target_ref, target, send, recv):
        pltpu.make_async_remote_copy(
            src_ref=source,
            dst_ref=target_ref,
            send_sem=send,
            recv_sem=recv,
            device_id=mesh_place(target),
            device_id_type=pl.DeviceIdType.MESH,
        ).start()

    def settle(some, semaphore):
        pltpu.make_async_copy(some, some, semaphore).wait()

    plans, slots, places = [], [], []
    for piece in pieces:
        plan = [sum(step, []) for step in reduce_plan(piece[3], 1)]
        slots.append({m: i for i, m in enumerate(plan[0])})
        place, at = {}, 0
        for step, masks in enumerate(plan):
            for mask in masks:
                place[step, mask] = at
                at += 1
        plans.append(plan)
        places.append(place)

    def rows_of(piece):
        return pl.ds(pieces[piece][1], pieces[piece][2])

    def send(piece, step, mask, bit, source):
        where = places[piece][step, mask & ~(1 << bit)]
        push(
            source,
            landed[pieces[piece][0]].at[where, rows_of(piece)],
            flipped(me, 1 << bit),
            leave.at[piece],
            arrive.at[piece, where],
        )

    order = sorted(range(1, devices), key=lambda m: -bin(m).count("1"))

    def send_rows(amount):
        for _ in range(min(amount, len(order))):
            target = flipped(me, order.pop(0))
            push(rows_in.at[target], rows_out.at[me], target, rows_sem.at[0], rows_sem.at[1])

    def group_of(turn):
        own, place = me // 4, 0
        for bit in range(depth):
            differs = 1 - (turn // (1 << (depth - 1 - bit))) % 2
            place = place + ((own // (1 << bit) + differs) % 2) * (1 << bit)
        return place

    def slab_copy(which, turn):
        width = 4 * chunk
        columns = pl.ds(pl.multiple_of(group_of(turn) * width, width), width)
        return pltpu.make_async_copy(
            lefts[which].at[:, columns],
            slab.at[turn % 2, which],
            slab_sem.at[turn % 2, which],
        )

    def slot_of(piece, turn, side):
        slot = 0
        for bit in pieces[piece][3]:
            digit = 1 - side if bit == 1 else (turn // (1 << (depth + 1 - bit))) % 2
            slot = slot * 2 + digit
        return slot

    big = [p for p in range(len(pieces)) if pieces[p][0] < computed]
    small = [p for p in range(len(pieces)) if pieces[p][0] >= computed]
    own_rows = pltpu.make_async_copy(rows_in.at[me], rows_out.at[me], own_sem)
    own_rows.start()
    for which in range(computed):
        slab_copy(which, 0).start()
    send_rows(spread[0])
    for piece in small:
        source = others[pieces[piece][0] - computed]
        for mask in plans[piece][0]:
            send(piece, 0, mask | 1, 0, source.at[flipped(me, mask | 1)])
            pltpu.make_async_copy(
                source.at[flipped(me, mask)],
                held[pieces[piece][0]].at[slots[piece][mask]],
                load.at[piece],
            ).start()

    near = (me // 2) % 2
    core = me % 2

    def add(piece, slot, where):
        which, rows = pieces[piece][0], rows_of(piece)
        some = landed[which].at[pl.ds(where, 1), rows]
        settle(some, arrive.at[piece, where])
        total = held[which][slot, rows].astype(F32)
        return total + landed[which][where, rows].astype(F32)

    def first_add(turn):
        for side in (1, 0):
            for piece in big:
                which, rows, bits = pieces[piece][0], rows_of(piece), pieces[piece][3]
                slot = slot_of(piece, turn, side)
                line = (near + side) % 2
                settle(landed[which].at[pl.ds(slot, 1), rows], arrive.at[piece, slot])
                total = ready[which][turn * 4 + line * 2 + core, rows].astype(F32)
                total = total + landed[which][slot, rows].astype(F32)
                held[which][slot, rows] = total.astype(BF)

                def on():
                    sent = len(plans[piece][0])
                    push(
                        held[which].at[slot, rows],
                        landed[which].at[sent + slot, rows],
                        flipped(me, 1 << bits[0]),
                        leave.at[piece],
                        arrive.at[piece, sent + slot],
                    )

                if bits[0] == 1 and side:
                    on()
                elif bits[0] == 2:
                    pl.when(turn < half)(on)

    @pl.loop(0, groups)
    def _(turn):
        @pl.when(turn + 1 < groups)
        def _():
            for which in range(computed):
                slab_copy(which, turn + 1).start()

        for which in (0, 2, 1):
            slab_copy(which, turn).wait()

            def product(right):
                block = contract_rows(slab[turn % 2, which], right[...])
                block = block.astype(BF).reshape(4, chunk, D)
                for i in range(4):
                    ready[which][turn * 4 + i] = block[i]

            if which == 0:
                first = group_of(turn) * 4 * chunk < 3 * D
                pl.when(first)(lambda: product(rights[0]))
                pl.when(jnp.logical_not(first))(lambda: product(rights[1]))
            else:
                product(rights[which + 1])
            for piece in big:
                if pieces[piece][0] != which:
                    continue
                rows = rows_of(piece)
                for side in range(2):
                    line = (near + side) % 2
                    slot = slot_of(piece, turn, side)
                    push(
                        ready[which].at[turn * 4 + line * 2 + 1 - core, rows],
                        landed[which].at[slot, rows],
                        flipped(me, 1),
                        leave.at[piece],
                        arrive.at[piece, slot],
                    )

        @pl.when(turn > 0)
        def _():
            first_add(turn - 1)

    first_add(groups - 1)
    turn = 1
    for step in range(len(pieces[0][3]) + 1):
        for at in range(len(plans[0][step])):
            for piece in small if step == 0 else (*big, *small):
                which, _, _, bits = pieces[piece]
                rows = rows_of(piece)
                if step == 0 and at == 0:
                    settle(held[which].at[pl.ds(0, devices // 2), rows], load.at[piece])
                mask = plans[piece][step][at]
                slot = slots[piece][mask]
                total = add(piece, slot, places[piece][step, mask])
                if step == len(bits):
                    outs[which][rows] = total
                    continue
                held[which][slot, rows] = total.astype(held[which].dtype)
                if (mask >> bits[step]) & 1:
                    send(piece, step + 1, mask, bits[step], held[which].at[slot, rows])
            if step or at == 0:
                send_rows(spread[turn] if turn < len(spread) else 0)
                turn += 1
    send_rows(devices)
    for piece in range(len(pieces)):
        which = pieces[piece][0]
        settle(landed[which].at[pl.ds(0, devices - 1), rows_of(piece)], leave.at[piece])
    own_rows.wait()
    for i in range(2):
        settle(rows_out.at[pl.ds(0, devices - 1)], rows_sem.at[i])


def reduce_products(lefts, rights, others, rows_in):
    devices = rows_in.shape[0]
    count, wide = lefts[0].shape
    chunk = wide // devices
    bits = devices.bit_length() - 1
    high = list(range(3, bits))
    one, other = (1, 2, *high), (2, 1, *high)
    one_early, other_early = (1, *high, 2), (2, *high, 1)
    cut = chunk // 32 * 16
    pieces = [(0, 0, chunk, one), (2, 0, chunk, other_early), (1, cut, chunk - cut, one_early)]
    pieces += [(1, 0, cut, other), (3, 0, others[0].shape[1], one), (4, 0, others[1].shape[1], other)]
    spread = [devices]
    anywhere = pl.BlockSpec(memory_space=pl.ANY)
    inside = pl.BlockSpec(memory_space=pltpu.VMEM)
    dma = pltpu.SemaphoreType.DMA
    kinds = [((chunk, D), BF)] * 3 + [(o.shape[1:], o.dtype) for o in others]
    *reduced, arrived = pl.pallas_call(
        lambda *refs: product_kernel(devices, pieces, spread, *refs),
        in_specs=[anywhere] * 3 + [inside] * 4 + [anywhere] * (len(others) + 1),
        out_specs=[inside] * len(kinds) + [anywhere],
        out_shape=[jax.ShapeDtypeStruct(shape, F32) for shape, _ in kinds]
        + [jax.ShapeDtypeStruct(rows_in.shape, rows_in.dtype)],
        scratch_shapes=[pltpu.VMEM((devices // 2, *shape), kind) for shape, kind in kinds]
        + [pltpu.VMEM((devices - 1, *shape), kind) for shape, kind in kinds]
        + [pltpu.VMEM((devices, chunk, D), BF)] * 3
        + [pltpu.VMEM((2, 3, count, 4 * chunk), BF), dma((2, 3))]
        + [dma((len(pieces), devices - 1)), dma((len(pieces),)), dma((len(pieces),)), dma((2,)), dma],
        compiler_params=pltpu.CompilerParams(
            collective_id=2, has_side_effects=True, vmem_limit_bytes=60 * 2**20
        ),
    )(*lefts, *rights, *others, rows_in)
    return reduced, arrived


TOK = 256


def normalize(values):
    average = jnp.mean(values, axis=-1, keepdims=True)
    centered = values - average
    inverse = lax.rsqrt(jnp.mean(centered * centered, axis=-1, keepdims=True) + NORM_EPS)
    return centered * inverse, inverse


def normalize_back(upstream, normed, inverse, gain):
    scaled = upstream * (1.0 + gain)
    return inverse * (
        scaled
        - jnp.mean(scaled, axis=-1, keepdims=True)
        - normed * jnp.mean(scaled * normed, axis=-1, keepdims=True)
    )


def vector(vec_ref, i):
    return vec_ref[i : i + 1, :]


def hot_rows(index, depth):
    hot = index == lax.broadcasted_iota(jnp.int32, (TOK, depth), 1)
    return hot.astype(F32).astype(BF)


def first_kernel(
    row_ref, place_ref, packed_ref, table_ref, vec_ref, qkv_ref, normed_ref, inv_ref, low_ref, z_ref
):
    values = matmul(hot_rows(row_ref[...], packed_ref.shape[0]), packed_ref[...])
    values = values + matmul(hot_rows(place_ref[...], PMAX), table_ref[...])
    normed, inverse = normalize(values)
    normed_ref[...] = normed
    inv_ref[...] = inverse
    low = (normed * (1.0 + vector(vec_ref, 0)) + vector(vec_ref, 1)).astype(BF)
    low_ref[...] = low
    for part, bias in ((0, 2), (1, None), (2, 3)):
        at = slice(part * D, (part + 1) * D)
        mixed = contract_cols(low, qkv_ref[at, :])
        if bias is not None:
            mixed = mixed + vector(vec_ref, bias)
        z_ref[:, at] = mixed.astype(BF)


def middle_kernel(
    context_ref, zero_ref, vec_ref, bias_ref, out_ref, up_ref, down_ref, head_ref, *results
):
    one_ref, one_inv_ref, one_low_ref, act_ref, slope_ref = results[:5]
    two_ref, two_inv_ref, two_low_ref, unit_ref, scale_ref = results[5:10]
    unit_low_ref, units_ref, mine_ref, sems = results[10:]
    step = pl.program_id(0)
    members = lax.axis_size("psg")
    member = lax.axis_index("psg")
    peers = [(lax.axis_index("grp"), (member + i) % members) for i in range(1, members)]

    @pl.when(step == 0)
    def _():
        barrier = pltpu.get_barrier_semaphore()
        for peer in peers:
            pl.semaphore_signal(
                barrier, inc=1, device_id=peer, device_id_type=pl.DeviceIdType.MESH
            )
        pl.semaphore_wait(barrier, members - 1)

    hidden = zero_ref[...] * (1.0 + vector(vec_ref, 0)) + vector(vec_ref, 1)
    hidden = hidden + contract_cols(context_ref[...], out_ref[...]) + vector(vec_ref, 4)
    normed, inverse = normalize(hidden)
    one_ref[...] = normed
    one_inv_ref[...] = inverse
    hidden = normed * (1.0 + vector(vec_ref, 5)) + vector(vec_ref, 6)
    low = hidden.astype(BF)
    one_low_ref[...] = low
    total = hidden + vector(vec_ref, 7)
    for part in range(up_ref.shape[0] // D):
        at = slice(part * D, (part + 1) * D)
        inner = contract_cols(low, up_ref[at, :]) + bias_ref[:, at]
        cdf = 0.5 + 0.5 * lax.erf(inner * math.sqrt(0.5))
        activated = (inner * cdf).astype(BF)
        act_ref[:, at] = activated
        pdf = jnp.exp(-0.5 * inner * inner) * (1.0 / math.sqrt(2.0 * math.pi))
        slope_ref[:, at] = (cdf + inner * pdf).astype(BF)
        total = total + matmul(activated, down_ref[at, :])
    normed, inverse = normalize(total)
    two_ref[...] = normed
    two_inv_ref[...] = inverse
    low = (normed * (1.0 + vector(vec_ref, 8)) + vector(vec_ref, 9)).astype(BF)
    two_low_ref[...] = low
    projected = matmul(low, head_ref[...])
    scale = lax.rsqrt(jnp.sum(projected * projected, axis=-1, keepdims=True) + NORM_EPS)
    unit_ref[...] = projected * scale
    scale_ref[...] = scale
    unit_low = (projected * scale).astype(BF)
    unit_low_ref[...] = unit_low
    mine_ref[step] = unit_low
    there = units_ref.at[member, pl.ds(pl.multiple_of(step * TOK, TOK), TOK)]
    for peer in peers:
        pltpu.make_async_remote_copy(
            src_ref=mine_ref.at[step],
            dst_ref=there,
            send_sem=sems.at[0],
            recv_sem=sems.at[1],
            device_id=peer,
            device_id_type=pl.DeviceIdType.MESH,
        ).start()
    pltpu.make_async_copy(mine_ref.at[step], there, sems.at[2]).start()

    @pl.when(step == mine_ref.shape[0] - 1)
    def _():
        for i in range(2):
            some = units_ref.at[pl.ds(0, members - 1)]
            pltpu.make_async_copy(some, some, sems.at[i]).wait()
        pltpu.make_async_copy(units_ref.at[0], units_ref.at[0], sems.at[2]).wait()


def column_sum(values):
    return jnp.sum(values, axis=0, keepdims=True)


def middle_back_kernel(
    grad_ref,
    unit_ref,
    scale_ref,
    two_ref,
    two_inv_ref,
    slope_ref,
    one_ref,
    one_inv_ref,
    vec_ref,
    out_ref,
    up_ref,
    down_ref,
    head_ref,
    *results,
):
    proj_ref, dtwo_ref, inner_ref, done_ref, done_low_ref, context_ref, sums_ref, bias_ref = results

    @pl.when(pl.program_id(0) == 0)
    def _():
        sums_ref[...] = jnp.zeros_like(sums_ref)
        bias_ref[...] = jnp.zeros_like(bias_ref)

    grad, unit = grad_ref[...], unit_ref[...]
    proj = (grad - unit * jnp.sum(grad * unit, axis=-1, keepdims=True)) * scale_ref[...]
    proj = proj.astype(BF)
    proj_ref[...] = proj
    upstream, normed = contract_cols(proj, head_ref[...]), two_ref[...]
    dtwo = normalize_back(upstream, normed, two_inv_ref[...], vector(vec_ref, 8))
    sums_ref[0:1, :] += column_sum(upstream * normed)
    sums_ref[1:2, :] += column_sum(upstream)
    sums_ref[2:3, :] += column_sum(dtwo)
    low = dtwo.astype(BF)
    dtwo_ref[...] = low
    upstream = dtwo
    for part in range(up_ref.shape[0] // D):
        at = slice(part * D, (part + 1) * D)
        inner = contract_cols(low, down_ref[at, :]) * slope_ref[:, at].astype(F32)
        bias_ref[:, at] += column_sum(inner)
        inner = inner.astype(BF)
        inner_ref[:, at] = inner
        upstream = upstream + matmul(inner, up_ref[at, :])
    normed = one_ref[...]
    done = normalize_back(upstream, normed, one_inv_ref[...], vector(vec_ref, 5))
    sums_ref[3:4, :] += column_sum(upstream * normed)
    sums_ref[4:5, :] += column_sum(upstream)
    sums_ref[5:6, :] += column_sum(done)
    done_ref[...] = done
    low = done.astype(BF)
    done_low_ref[...] = low
    context_ref[...] = matmul(low, out_ref[...]).astype(BF)


def first_back_kernel(
    z_ref, done_ref, zero_ref, inv_ref, place_ref, vec_ref, qkv_ref, low_ref, places_ref, sums_ref
):
    @pl.when(pl.program_id(0) == 0)
    def _():
        sums_ref[...] = jnp.zeros_like(sums_ref)
        places_ref[...] = jnp.zeros_like(places_ref)

    upstream, normed = done_ref[...], zero_ref[...]
    for part in range(3):
        at = slice(part * D, (part + 1) * D)
        upstream = upstream + matmul(z_ref[:, at], qkv_ref[at, :])
    grad = normalize_back(upstream, normed, inv_ref[...], vector(vec_ref, 0))
    sums_ref[0:1, :] += column_sum(upstream * normed)
    sums_ref[1:2, :] += column_sum(upstream)
    sums_ref[2:3, :] += column_sum(z_ref[:, :D].astype(F32))
    sums_ref[3:4, :] += column_sum(z_ref[:, 2 * D : 3 * D].astype(F32))
    low = grad.astype(BF)
    low_ref[...] = low
    places_ref[...] += contract_rows(hot_rows(place_ref[...], PMAX), low)


def by_tokens(width):
    return pl.BlockSpec((TOK, width), lambda i: (i, 0))


def resident(rows, width, at=0):
    return pl.BlockSpec((rows, width), lambda i: (at, 0), pipeline_mode=pl.Buffered(1))


def token_call(kernel, count, in_specs, outs, flops, whole=(), scratch=(), **params):
    return pl.pallas_call(
        kernel,
        grid=(count // TOK,),
        in_specs=in_specs,
        out_specs=[
            by_tokens(width) if rows is None else pl.BlockSpec((rows, width), lambda i: (0, 0))
            for rows, width, _ in outs
        ]
        + [pl.BlockSpec(memory_space=pl.ANY) for _ in whole],
        out_shape=[
            jax.ShapeDtypeStruct((count if rows is None else rows, width), kind)
            for rows, width, kind in outs
        ]
        + list(whole),
        scratch_shapes=list(scratch),
        compiler_params=pltpu.CompilerParams(vmem_limit_bytes=56 * 2**20, **params),
        cost_estimate=pl.CostEstimate(flops=flops, bytes_accessed=30000000, transcendentals=0),
    )


def adam_step(weight, moment, second, gradient, rate, share_one, share_two):
    moment_new = BETA_ONE * moment + (1.0 - BETA_ONE) * gradient
    second_new = BETA_TWO * second + (1.0 - BETA_TWO) * gradient * gradient
    corrected = moment_new / share_one
    scaled = second_new / share_two
    weight_new = weight - rate * (corrected / (jnp.sqrt(scaled) + ADAM_EPS) + WEIGHT_DECAY * weight)
    return (weight_new, second_new)


def adam_update(weight, moment, second, gradient, rate, count_steps):
    share_one, share_two = 1.0 - BETA_ONE**count_steps, 1.0 - BETA_TWO**count_steps
    return adam_step(weight, moment, second, gradient, rate, share_one, share_two)


def on_device(
    query_ids,
    passage_ids,
    passage_lengths,
    positives,
    negatives,
    pair_mask,
    assignments,
    step_count,
    embed_table,
    embed_table_moment,
    embed_table_second,
    attention_weight,
    attention_weight_moment,
    attention_weight_second,
    up_weight,
    up_weight_moment,
    up_weight_second,
    down_weight,
    down_weight_moment,
    down_weight_second,
    head_weight,
    head_weight_moment,
    head_weight_second,
    small_params,
    small_params_moment,
    small_params_second,
):
    devices = lax.axis_size("grp") * lax.axis_size("psg")
    members = lax.axis_size("psg")
    member = lax.axis_index("psg")
    group = lax.axis_index("grp")
    shard_rows = embed_table.shape[0]
    queries = query_ids.shape[0]
    negative_count = negatives.shape[1]
    query_rows = queries * SEG
    count = ROW + query_rows
    capacity = 16 * ((count // devices + 8 + 15) // 16)
    small_size = small_params.shape[0]
    head_rows = head_weight.shape[0]
    mask_float = pair_mask.astype(F32)

    tokens = jnp.concatenate([passage_ids.reshape(-1), query_ids.reshape(-1)])
    passage_segment, passage_position = layout_of(passage_lengths[0])
    query_place = jnp.arange(query_rows, dtype=jnp.int32)
    segment = jnp.concatenate([passage_segment, PPD + query_place // SEG])
    position = jnp.concatenate([passage_position, query_place % SEG])
    segment_column = segment[:, None]
    segment_windows = jnp.stack(
        [
            segment[window_start(i, count) : window_start(i, count) + WIN][None]
            for i in range(count // BLK)
        ]
    )

    def shard_of(rows):
        return jnp.pad(rows.astype(BF), ((0, -rows.shape[0] % 16), (0, 0)))

    matrix_rows = down_weight.shape[0]
    shards = [shard_of(attention_weight.T), shard_of(up_weight.T), shard_of(down_weight)]

    owner = tokens // shard_rows
    local_row = tokens - owner * shard_rows
    owner_hot = one_hot(owner, devices)
    row_hot = one_hot(local_row, shard_rows)
    needed = jnp.minimum(contract_rows(owner_hot, row_hot), 1.0)
    width = -(-shard_rows // 1024) * 1024
    table = jnp.pad(embed_table.astype(BF), ((0, width - shard_rows), (0, 0)))
    notes = jnp.concatenate(
        [
            v.reshape(-1).astype(BF)
            for v in (small_params, head_weight, passage_lengths, jnp.sum(mask_float))
        ]
    )
    notes = jnp.pad(notes, (0, -notes.size % 2048)).reshape(-1, 128)
    (*gathered, noted), packed, asked_rank = gather_all(
        [*shards, notes],
        jnp.pad(needed, ((0, 0), (0, width - shard_rows))).reshape(devices, width // 128, 128),
        table,
        capacity,
    )
    asked_rank = asked_rank[:, :shard_rows]
    attn_rows, up_rows, down_rows = (g[:, :matrix_rows].reshape(-1, D) for g in gathered)
    noted = noted.reshape(devices, -1)
    cut = [0, small_size, head_rows * DC, PPD, 1]
    for i in range(1, len(cut)):
        cut[i] += cut[i - 1]
    small_all, head_all, lengths_all, pairs_all = (noted[:, cut[i] : cut[i + 1]] for i in range(4))
    small_all = small_all.reshape(-1)
    head_full = head_all.reshape(D, DC)
    pair_floor = jnp.maximum(jnp.sum(pairs_all.astype(F32)), 1.0)
    place_row = jnp.arange(shard_rows, dtype=jnp.int32)
    earlier = (place_row[:, None] < place_row[None, :]).astype(BF)
    overflow = jnp.max(packed[:, capacity - 1, :1].astype(F32)) > 0.5 * MARK
    packed = packed.reshape(devices * capacity, D)
    needed_rank = jnp.minimum(matmul(needed.astype(BF), earlier), 255.0)
    token_rank = jnp.sum(matmul(owner_hot, needed_rank.astype(BF)) * row_hot.astype(F32), axis=1)
    slot = owner * capacity + jnp.minimum(token_rank.astype(jnp.int32), capacity - 1)
    slot_hot = one_hot(slot, devices * capacity)

    def whole_lookup():
        rows = lax.all_gather(embed_table.astype(BF), ALL, axis=0, tiled=True)[tokens]
        rows = jnp.pad(rows, ((0, devices * capacity - count), (0, 0)))
        return rows, jnp.arange(count, dtype=jnp.int32)

    packed, row_of = lax.cond(overflow, whole_lookup, lambda: (packed, slot))

    positions = small_all[: PMAX * D].reshape(PMAX, D)
    remainder = small_all[PMAX * D :].astype(F32)
    vectors = jnp.pad(remainder[: 10 * D].reshape(10, D), ((0, 6), (0, 0)))
    bias_up = remainder[None, 10 * D :]
    inner_width = up_rows.shape[0]
    place_column = position[:, None]
    norm_zero, inverse_zero, input_zero, mixed = token_call(
        first_kernel,
        count,
        [by_tokens(1), by_tokens(1), resident(devices * capacity, D)]
        + [resident(PMAX, D), resident(16, D), resident(3 * D, D)],
        [(None, D, F32), (None, 1, F32), (None, D, BF), (None, 3 * D, BF)],
        2 * count * D * (3 * D + PMAX),
    )(row_of[:, None], place_column, packed, positions, vectors, attn_rows)
    context, kept = attention_forward(segment_column, segment_windows, mixed)
    weight_specs = [
        resident(D, D, 3),
        resident(inner_width, D),
        resident(inner_width, D),
        resident(D, DC),
    ]
    weights = (attn_rows, up_rows, down_rows, head_full)
    middle_flops = 2 * count * D * (D + 2 * inner_width + DC)
    (
        norm_one,
        inverse_one,
        input_one,
        activated,
        slope,
        norm_two,
        inverse_two,
        input_two,
        unit,
        scale_inverse,
        unit_low,
        units,
    ) = token_call(
        middle_kernel,
        count,
        [by_tokens(D), by_tokens(D), resident(16, D), resident(1, inner_width), *weight_specs],
        [(None, D, F32), (None, 1, F32), (None, D, BF)]
        + [(None, inner_width, BF)] * 2
        + [(None, D, F32), (None, 1, F32), (None, D, BF)]
        + [(None, DC, F32), (None, 1, F32), (None, DC, BF)],
        middle_flops,
        [jax.ShapeDtypeStruct((members, count, DC), BF)],
        [pltpu.VMEM((count // TOK, TOK, DC), BF), pltpu.SemaphoreType.DMA((3,))],
        collective_id=3,
        has_side_effects=True,
    )(context, norm_zero, vectors, bias_up, *weights)

    group_passage = units[:, :ROW]
    group_query = units[:, ROW:].reshape(members * query_rows, DC)
    own_query = unit_low[ROW:]
    own_passage = unit_low[:ROW]
    group_lengths = lax.dynamic_slice_in_dim(lengths_all, group * members, members, 0)
    group_segment, _ = layout_of(group_lengths.astype(jnp.int32))
    group_hot = one_hot(group_segment, PPD)
    passage_hot = one_hot(passage_segment, PPD)

    weighted_own = jnp.exp(
        jnp.einsum("qd,mtd->mqt", own_query, group_passage, preferred_element_type=F32) / TEMPER
    )
    sum_own = lambda part: jnp.einsum(
        "mqt,mtp->mqp", part, group_hot, preferred_element_type=F32
    )
    high, low = split_two(weighted_own)
    totals_own = sum_own(high) + sum_own(low)
    weighted = jnp.exp(contract_cols(group_query, own_passage) / TEMPER)
    high, low = split_two(weighted)
    totals = matmul(high, passage_hot) + matmul(low, passage_hot)
    own_scores = jnp.sum(
        (TEMPER * jnp.log(totals_own)).reshape(members, queries, SEG, PPD), axis=2
    )
    own_scores = own_scores.transpose(1, 0, 2).reshape(queries, members * PPD)
    columns = jnp.arange(members * PPD, dtype=jnp.int32)
    pick_positive = (positives[:, None] == columns[None, :]).astype(F32)
    pick_negative = (negatives[:, :, None] == columns[None, None, :]).astype(F32)
    pos_score = jnp.sum(own_scores * pick_positive, axis=1)
    neg_score = jnp.sum(pick_negative * own_scores[:, None, :], axis=2)
    margins = MARGIN - pos_score[:, None] + neg_score
    numerator = jnp.sum(mask_float * jax.nn.softplus(margins))
    factor = mask_float * jax.nn.sigmoid(margins) / pair_floor
    grad_own = (
        jnp.sum(factor[:, :, None] * pick_negative, axis=1)
        - jnp.sum(factor, axis=1)[:, None] * pick_positive
    )
    grad_group = lax.all_gather(grad_own, "psg", axis=0, tiled=True)
    grad_local = lax.dynamic_slice_in_dim(grad_group, member * PPD, PPD, 1)

    grad_own_split = grad_own.reshape(queries, 1, members, PPD).transpose(2, 0, 1, 3)
    ratio_own = (
        (TEMPER * grad_own_split) / totals_own.reshape(members, queries, SEG, PPD)
    ).reshape(members, query_rows, PPD)
    spread_own = jnp.einsum(
        "mqp,mtp->mqt", ratio_own.astype(BF), group_hot, preferred_element_type=F32
    )
    sims_own = (spread_own * weighted_own / TEMPER).astype(BF)
    grad_unit_query = jnp.einsum(
        "mqt,mtd->qd", sims_own, group_passage, preferred_element_type=F32
    )
    ratio = (
        (TEMPER * grad_local[:, None, :]) / totals.reshape(members * queries, SEG, PPD)
    ).reshape(members * query_rows, PPD)
    sims = (contract_cols(ratio.astype(BF), passage_hot) * weighted / TEMPER).astype(BF)
    grad_unit_passage = contract_rows(sims, group_query)
    grad_unit = jnp.concatenate([grad_unit_passage, grad_unit_query])

    picks = one_hot(assignments[0], NCENT)
    centroid_part = contract_rows(picks, own_passage)
    count_part = jnp.sum(picks.astype(F32), axis=0)
    (
        grad_proj,
        grad_two_low,
        grad_inner,
        grad_sum_one,
        grad_one_low,
        grad_context,
        sums,
        grad_bias_up,
    ) = token_call(
        middle_back_kernel,
        count,
        [by_tokens(DC), by_tokens(DC), by_tokens(1), by_tokens(D), by_tokens(1)]
        + [by_tokens(inner_width), by_tokens(D), by_tokens(1), resident(16, D), *weight_specs],
        [(None, DC, BF), (None, D, BF), (None, inner_width, BF), (None, D, F32)]
        + [(None, D, BF), (None, D, BF), (8, D, F32), (1, inner_width, F32)],
        middle_flops,
    )(
        grad_unit,
        unit,
        scale_inverse,
        norm_two,
        inverse_two,
        slope,
        norm_one,
        inverse_one,
        vectors,
        *weights,
    )
    grad_head = contract_rows(input_two, grad_proj)
    grad_attn = attention_backward(
        segment.reshape(-1, 1, BLK),
        segment_windows.transpose(0, 2, 1),
        mixed,
        grad_context,
        kept,
        grad_one_low,
    )
    grad_low, grad_positions, sums_zero = token_call(
        first_back_kernel,
        count,
        [by_tokens(3 * D), by_tokens(D), by_tokens(D), by_tokens(1), by_tokens(1)]
        + [resident(16, D), resident(3 * D, D)],
        [(None, D, BF), (PMAX, D, F32), (8, D, F32)],
        2 * count * D * (3 * D + PMAX),
    )(grad_attn, grad_sum_one, norm_zero, inverse_zero, place_column, vectors, attn_rows)
    grad_slots = contract_rows(slot_hot, grad_low).astype(BF).reshape(devices, capacity, D)
    grad_small = jnp.concatenate(
        [
            grad_positions.reshape(-1),
            sums_zero[:4].reshape(-1),
            sums[5],
            sums[3],
            sums[4],
            sums[2],
            sums[0],
            sums[1],
            grad_bias_up[0],
        ]
    )

    def side_by_side(parts, sublanes):
        joined = jnp.concatenate([p.reshape(devices, -1) for p in parts], axis=1)
        joined = jnp.pad(joined, ((0, 0), (0, -joined.shape[1] % (sublanes * 128))))
        return joined.reshape(devices, -1, 128)

    lefts = [grad_attn, grad_inner, activated]
    rights = [input_zero, context, input_one, grad_two_low]
    others = [
        side_by_side([centroid_part.astype(BF), grad_head.astype(BF)], 16),
        side_by_side([grad_small, count_part, jnp.broadcast_to(numerator, (devices, 1))], 8),
    ]
    if members * matrix_rows % 128 == 0 and members == 4:
        reduced, grad_slots = reduce_products(lefts, rights, others, grad_slots)
    else:
        right_of = [rights[:2], rights[2:3], rights[3:]]
        sums = []
        for left, right in zip(lefts, right_of):
            if len(right) == 2:
                rows = jnp.concatenate(
                    [
                        contract_rows(left[:, : 3 * D], right[0]),
                        contract_rows(left[:, 3 * D :], right[1]),
                    ]
                )
            else:
                rows = contract_rows(left, right[0])
            rows = rows.astype(BF).reshape(devices, matrix_rows, D)
            sums.append(jnp.pad(rows, ((0, 0), (0, -matrix_rows % 16), (0, 0))))
        reduced, grad_slots = reduce_all(sums + others, grad_slots)
    attn_reduced, up_reduced, down_reduced = (r[:matrix_rows] for r in reduced[:3])
    wide, fine = reduced[3].reshape(-1), reduced[4].reshape(-1)
    centroid_rows = NCENT // devices
    centroid_sums = wide[: centroid_rows * DC].reshape(centroid_rows, DC)
    head_reduced = wide[centroid_rows * DC :][: head_rows * DC].reshape(head_rows, DC)
    small_reduced = fine[:small_size]
    centroid_counts = fine[small_size:][:centroid_rows]
    loss = fine[small_size + centroid_rows] / pair_floor

    def whole_table():
        table = jnp.zeros((shard_rows * devices, D), F32).at[tokens].add(grad_low.astype(F32))
        return lax.psum_scatter(table, ALL, scatter_dimension=0, tiled=True)

    def own_rows():
        slots = jnp.arange(capacity, dtype=jnp.int32).astype(F32)
        picked = (asked_rank[:, None, :] == slots[None, :, None]).astype(BF)
        return contract_rows(
            picked.reshape(devices * capacity, shard_rows),
            grad_slots.reshape(devices * capacity, D),
        )

    table_reduced = lax.cond(
        overflow,
        whole_table,
        own_rows,
    )

    count_steps = step_count[0].astype(F32)
    attn_reduced = attn_reduced.T
    up_reduced = up_reduced.T
    table_new, table_second_new = adam_update(
        embed_table, embed_table_moment, embed_table_second, table_reduced, RATE_TABLE, count_steps
    )
    attn_new, attn_second_new = adam_update(
        attention_weight,
        attention_weight_moment,
        attention_weight_second,
        attn_reduced,
        RATE_MATRIX,
        count_steps,
    )
    up_new, up_second_new = adam_update(
        up_weight, up_weight_moment, up_weight_second, up_reduced, RATE_MATRIX, count_steps
    )
    down_new, down_second_new = adam_update(
        down_weight, down_weight_moment, down_weight_second, down_reduced, RATE_MATRIX, count_steps
    )
    head_new, head_second_new = adam_update(
        head_weight, head_weight_moment, head_weight_second, head_reduced, RATE_MATRIX, count_steps
    )
    small_new, small_second_new = adam_update(
        small_params, small_params_moment, small_params_second, small_reduced, RATE_TABLE, count_steps
    )
    return (
        loss,
        centroid_sums,
        centroid_counts,
        table_new,
        table_reduced,
        table_second_new,
        attn_new,
        attn_reduced,
        attn_second_new,
        up_new,
        up_reduced,
        up_second_new,
        down_new,
        down_reduced,
        down_second_new,
        head_new,
        head_reduced,
        head_second_new,
        small_new,
        small_reduced,
        small_second_new,
    )


def solution(mesh):
    in_specs = (
        P(("grp", "psg"), None),
        P(("grp", "psg"), None),
        P(("grp", "psg"), None),
        P(("grp", "psg")),
        P(("grp", "psg"), None),
        P(("grp", "psg"), None),
        P(("grp", "psg"), None),
        P(),
        P(("grp", "psg"), None),
        P(("grp", "psg"), None),
        P(("grp", "psg"), None),
        P(None, ("grp", "psg")),
        P(None, ("grp", "psg")),
        P(None, ("grp", "psg")),
        P(None, ("grp", "psg")),
        P(None, ("grp", "psg")),
        P(None, ("grp", "psg")),
        P(("grp", "psg"), None),
        P(("grp", "psg"), None),
        P(("grp", "psg"), None),
        P(("grp", "psg"), None),
        P(("grp", "psg"), None),
        P(("grp", "psg"), None),
        P(("grp", "psg")),
        P(("grp", "psg")),
        P(("grp", "psg")),
    )
    out_specs = (
        P(),
        P(("grp", "psg"), None),
        P(("grp", "psg")),
        P(("grp", "psg"), None),
        P(("grp", "psg"), None),
        P(("grp", "psg"), None),
        P(None, ("grp", "psg")),
        P(None, ("grp", "psg")),
        P(None, ("grp", "psg")),
        P(None, ("grp", "psg")),
        P(None, ("grp", "psg")),
        P(None, ("grp", "psg")),
        P(("grp", "psg"), None),
        P(("grp", "psg"), None),
        P(("grp", "psg"), None),
        P(("grp", "psg"), None),
        P(("grp", "psg"), None),
        P(("grp", "psg"), None),
        P(("grp", "psg")),
        P(("grp", "psg")),
        P(("grp", "psg")),
    )
    return jax.shard_map(
        on_device, mesh=mesh, in_specs=in_specs, out_specs=out_specs, check_vma=False
    )
```
